256 devices in a mesh: inst: 64 (over x, y_lo, z), head: 4 (over y_hi, core).
Axes of the slice: x: 4, y: 4 (y_hi: 2, y_lo: 2; y = y_hi * 2 + y_lo), z: 8, core: 2. Of those that a mesh axis runs over, the one named last changes fastest.
Arguments:
- queries: bfloat16 [16384, 8192], P('inst', 'head'), may hold values from -256 to 256
- keys: bfloat16 [16384, 1024], P('inst', 'head'), may hold values from -6 to 6
- values: bfloat16 [16384, 1024], P('inst', 'head'), may hold values from -6 to 6
- segments: int32 [16384], P('inst'), may hold values from 0 to 5, never falling along the last dimension, each value on 1 to 5120 neighbouring positions
- owners: int32 [16384, 1], P('inst'), may hold values from 0 to 63; in each aligned block of 256 rows (0 to 255, 256 to 511, ...) at most 8 rows name the same one
Outputs:
- attended: bfloat16 [16384, 8192], P('inst', 'head')
- cache: bfloat16 [32768, 2048], P('inst')
The draws below stay inside these ranges and needn't reach their ends.
Inputs may be any that keep to these rules, and one draw needn't show every extreme that they name: `segments`: requests lie in order; each has 1 to 5120 consecutive tokens, one exactly 5120. `owners`: of the 256 tokens of one index of inst, at most 8 name one owner; some owner is named exactly 8 times.
All inputs are finite; a program needn't handle non-finite values.
Results may differ from the reference program's by a relative error of at most 0.006.
Values may be sent and summed in bfloat16 or wider, within the bound.
A program may use at most 128 MiB of HBM per device.

```python
import math
import jax
import jax.numpy as jnp
import numpy as np
from jax import lax

Q_HEADS = 64
KV_HEADS = 8
HEAD_FEATURES = 128
TOK_DEV = 256
REQS = 6
TOKENS = 16384
MOST_LEN = 5120
SLOT = 8
N_INST = 64
N_HEAD = 4


def base_keys(key):
    return jnp.clip(jax.random.normal(key, (TOKENS, KV_HEADS * HEAD_FEATURES), jnp.float32), -6.0, 6.0)


def draw_keys(key, part):
    base = base_keys(key)
    return base.astype(jnp.bfloat16)


def draw_queries(key, part):
    key = jax.random.fold_in(key, 7)
    fresh = jnp.clip(jax.random.normal(key, (TOKENS, Q_HEADS * HEAD_FEATURES), jnp.float32), -6.0, 6.0)
    return fresh.astype(jnp.bfloat16)


def block_levels(key, extent, split, least, largest):
    gain = 1.0
    for axis_at, parts in split:
        heights = jax.random.uniform(jax.random.fold_in(jax.random.fold_in(key, 6), axis_at), (parts,), jnp.float32, least / len(split), largest / len(split))
        gain = gain * jnp.repeat(jnp.exp(heights), extent[axis_at] // parts).reshape((-1,) + (1,) * (len(extent) - 1 - axis_at))
    return gain


def split_up(amount, total, limit, lean):
    portions = [(1 << 20) // math.isqrt(rank ** lean) + 1 for rank in range(2, amount + 1)]
    rest, counts = total - limit - (amount - 1), [1] * (amount - 1)
    while rest > 0:
        movable = [i for i in range(amount - 1) if counts[i] < limit]
        whole, left = sum([portions[i] for i in movable]), rest
        for i in movable:
            addition = min(limit - counts[i], max(1, left * portions[i] // whole), rest)
            counts[i] = counts[i] + addition
            rest = rest - addition
    return np.array([limit] + counts)


def ragged(key, amount, total, bound, skew):
    if amount == 2:
        one = jax.random.randint(key, (), max(1, total - bound), min(bound, total - 1) + 1)
        return jnp.stack([one, total - one])
    lengths = jnp.asarray(split_up(amount, total, bound, skew), jnp.int32)
    couples = (amount - 1) // 2
    giver, taker = lengths[1:1 + 2 * couples:2], lengths[2:2 + 2 * couples:2]
    margin = jnp.minimum(giver - 1, bound - taker)
    shifted = jax.random.randint(jax.random.fold_in(key, 1), (couples,), 0, 1 << 20) % (margin + 1)
    lengths = lengths.at[1:1 + 2 * couples:2].set(giver - shifted).at[2:2 + 2 * couples:2].set(taker + shifted)
    return lengths[jax.random.permutation(jax.random.fold_in(key, 2), amount)]


def shared_out(own_key, own, number, rows, amount, top, limit, skew):
    order = jax.random.permutation(own_key, amount)
    crowded, ordinary = shares(amount, rows * top, limit, skew, True), shares(amount, rows * top, limit, skew, False)
    places = jnp.arange(amount)

    def named(lengths, offset_by):
        used = int((lengths > 0).sum())
        fixed = max(1, used // 4)
        passed = fixed + (places - fixed + offset_by * (used - fixed)) % max(1, amount - fixed)
        return jnp.zeros((amount,), jnp.int32).at[order[jnp.where(places < fixed, places, passed)]].set(jnp.asarray(lengths, jnp.int32))

    lengths = jnp.where(number % 4 == 0, named(crowded, number // 4), named(ordinary, number - number // 4 - 1))
    mixed = jax.random.permutation(jax.random.fold_in(own, 3), amount)
    donor, taker = mixed[0:amount // 2 * 2:2], mixed[1:amount // 2 * 2:2]
    room = jnp.minimum(lengths[donor] - 1, limit - lengths[taker]) // 2
    room = jnp.where((donor == order[0]) | (taker == order[0]) | (lengths[taker] == 0), 0, jnp.maximum(room, 0))
    passed = jax.random.randint(jax.random.fold_in(own, 4), (amount // 2,), 0, 1 << 20) % (room + 1)
    lengths = lengths.at[donor].add(-passed).at[taker].add(passed)
    labels = jnp.searchsorted(jnp.cumsum(lengths), jnp.arange(rows * top), side="right").astype(jnp.int32)
    table = labels.reshape(top, rows).T
    table = table[jax.random.permutation(jax.random.fold_in(own, 1), rows)]
    offset_by = jax.random.randint(jax.random.fold_in(own, 2), (rows, 1), 0, top)
    return jnp.take_along_axis(table, (jnp.arange(top)[None, :] + offset_by) % top, axis=1)


def shares(amount, total, bound, skew, full):
    loads = [(1 << 20) // math.isqrt(grade ** skew) + 1 for grade in range(1, amount + 1)]
    largest = bound if full else min(bound, max(-(-total // amount), total * loads[0] // sum(loads)))
    least = 1 if total - largest >= amount - 1 else 0
    holding, rest = [largest] + [least] * (amount - 1), total - largest - least * (amount - 1)
    while rest > 0:
        movable = [i for i in range(1, amount) if holding[i] < largest] or [i for i in range(1, amount) if holding[i] < bound]
        whole, remaining = sum([loads[i] for i in movable]), rest
        for i in movable:
            extra = min(bound - holding[i], max(1, remaining * loads[i] // whole), rest)
            holding[i] = holding[i] + extra
            rest = rest - extra
    return np.array(holding)


def centred(rng, extent, scale, most, pieces=(), kind=jnp.bfloat16):
    values = jax.random.normal(rng, extent, jnp.float32) * scale
    if len(pieces) > 0:
        values = block_levels(rng, extent, pieces, -0.22, 0.18) * values
    return jnp.clip(values, min=-most, max=most).astype(kind)


def setup_inputs(seed: int = 0) -> dict:
    splits = jax.random.split(jax.random.key(seed), 6)
    queries = draw_queries(jax.random.fold_in(splits[5], 71), 0)
    keys = draw_keys(jax.random.fold_in(splits[5], 71), 0)
    values = centred(splits[2], (TOKENS, KV_HEADS * HEAD_FEATURES), 1.0, 6.0, ((0, 64), (1, 4)))
    segments = jnp.searchsorted(jnp.cumsum(ragged(splits[3], REQS, TOKENS, MOST_LEN, 2)), jnp.arange(TOKENS), side="right").astype(jnp.int32)
    owners_keys = jax.random.split(jax.random.fold_in(splits[4], 1), TOKENS // TOK_DEV)
    owners_turns = jax.random.permutation(jax.random.fold_in(splits[4], 3), TOKENS // TOK_DEV)
    owners = jax.vmap(lambda own, number: shared_out(jax.random.fold_in(splits[4], 2), own, number, TOK_DEV, N_INST, 1, SLOT, 2))(owners_keys, owners_turns).reshape((TOKENS, 1))
    return dict(queries=queries, keys=keys, values=values, segments=segments, owners=owners)


def attend_block(queries, keys, values, segments, index):
    ratio = Q_HEADS // KV_HEADS
    width = min(TOKENS, 512 * ((MOST_LEN + 511) // 512 + 1))
    qstart = index * 512
    kstart = jnp.clip(qstart + 512 - width, 0, TOKENS - width).astype(jnp.int32)
    qgrid = lax.dynamic_slice_in_dim(queries, qstart, 512, 0).reshape(512, KV_HEADS, ratio, HEAD_FEATURES).astype(jnp.float32)
    kgrid = lax.dynamic_slice_in_dim(keys, kstart, width, 0).reshape(width, KV_HEADS, HEAD_FEATURES).astype(jnp.float32)
    vgrid = lax.dynamic_slice_in_dim(values, kstart, width, 0).reshape(width, KV_HEADS, HEAD_FEATURES).astype(jnp.float32)
    qseg = lax.dynamic_slice_in_dim(segments, qstart, 512, 0)
    kseg = lax.dynamic_slice_in_dim(segments, kstart, width, 0)
    qpos = qstart + jnp.arange(512, dtype=jnp.int32)
    kpos = kstart + jnp.arange(width, dtype=jnp.int32)
    visible = (qseg[:, None] == kseg[None, :]) & (kpos[None, :] <= qpos[:, None])
    visible = visible[:, None, None, :]
    scores = jnp.einsum("tgra,sga->tgrs", qgrid, kgrid) * (HEAD_FEATURES ** -0.5)
    scores = jnp.where(visible, scores, jnp.float32(-1e30))
    peak = jnp.max(scores, axis=-1)
    weight_probs = jnp.where(visible, jnp.exp(scores - peak[..., None]), jnp.float32(0.0))
    total = jnp.sum(weight_probs, axis=-1)
    rounded = lax.optimization_barrier(weight_probs.astype(jnp.bfloat16))
    summed = jnp.einsum("oyce,eyk->oyck", rounded.astype(jnp.float32), vgrid)
    return (summed / total[..., None]).astype(jnp.bfloat16).reshape(512, Q_HEADS * HEAD_FEATURES)


def reference(queries, keys, values, segments, owners):
    blocks = jnp.arange(TOKENS // 512, dtype=jnp.int32)
    attended = lax.map(lambda index: attend_block(queries, keys, values, segments, index), blocks)
    attended = attended.reshape(TOKENS, Q_HEADS * HEAD_FEATURES)
    dest = owners[:, 0].reshape(N_INST, TOK_DEV)
    onehot = (dest[:, :, None] == jnp.arange(N_INST, dtype=jnp.int32)[None, None, :]).astype(jnp.int32)
    slot = jnp.sum(onehot * (jnp.cumsum(onehot, axis=1) - onehot), axis=-1)
    source = jnp.arange(N_INST, dtype=jnp.int32)[:, None]
    target = (dest * (N_INST * SLOT) + source * SLOT + slot).reshape(TOKENS).astype(jnp.int32)
    kgroups = keys.reshape(TOKENS, N_HEAD, KV_HEADS * HEAD_FEATURES // N_HEAD)
    vgroups = values.reshape(TOKENS, N_HEAD, KV_HEADS * HEAD_FEATURES // N_HEAD)
    rows = jnp.stack([kgroups, vgroups], axis=2).reshape(TOKENS, 2 * KV_HEADS * HEAD_FEATURES)
    cache = jnp.zeros((N_INST * N_INST * SLOT, 2 * KV_HEADS * HEAD_FEATURES), jnp.bfloat16).at[target].set(rows)
    return attended, cache
```

```python
import functools

import jax
import jax.numpy as jnp
from jax import lax
from jax.experimental import pallas as pl
from jax.experimental.pallas import tpu as pltpu
from jax.sharding import PartitionSpec as P

MESH = pl.DeviceIdType.MESH
F32, BF16 = jnp.float32, jnp.bfloat16

HEADS, SIZE, RATIO = 16, 128, 8
TOK = 256
REACH = 20
SLOT = 8
STEP = 4
SEG_ROW = 2 * TOK
BLOCK_ROWS = 2 * TOK + 16
TO_LOG2 = SIZE ** -0.5 * 1.4426950408889634

ARRIVALS = (
    ((16, 215, 109, 308, 301, 214, 307, 17, 102, 213, 306, 18, 212, 310, 211, 104, 305, 103, 20, 19),
     (16, 308, 215, 109, 214, 110, 101, 213, 307, 17, 102, 212, 103, 18, 111, 19, 306, 205, 204, 20)),
    ((16, 101, 308, 215, 117, 307, 110, 214, 302, 309, 213, 18, 212, 103, 19, 306, 211, 204, 305, 20),
     (101, 16, 215, 17, 308, 214, 309, 110, 213, 111, 102, 307, 18, 306, 205, 103, 104, 19, 212, 120)),
    ((101, 16, 308, 17, 215, 309, 102, 214, 18, 213, 111, 310, 212, 307, 303, 205, 306, 19, 304, 20),
     (16, 101, 215, 102, 308, 17, 214, 18, 307, 109, 310, 206, 111, 112, 213, 103, 119, 205, 104, 120)),
    ((101, 16, 17, 215, 308, 102, 214, 307, 18, 213, 103, 206, 309, 19, 310, 305, 212, 304, 111, 20),
     (16, 101, 215, 308, 17, 102, 214, 307, 103, 18, 309, 19, 110, 206, 111, 213, 112, 205, 104, 120)),
    ((101, 16, 215, 308, 17, 214, 207, 102, 213, 310, 18, 103, 206, 309, 19, 311, 204, 205, 20, 212),
     (16, 101, 215, 117, 308, 307, 102, 309, 18, 103, 214, 310, 19, 104, 206, 111, 20, 112, 113, 205)),
    ((16, 101, 215, 308, 102, 17, 307, 214, 18, 109, 205, 310, 103, 311, 19, 306, 104, 213, 112, 20),
     (101, 16, 308, 17, 215, 102, 309, 207, 18, 310, 103, 205, 19, 214, 104, 213, 20, 311, 206, 112)),
    ((16, 101, 308, 215, 206, 17, 102, 307, 103, 18, 310, 19, 214, 309, 213, 104, 311, 112, 20, 305),
     (101, 16, 17, 308, 102, 309, 206, 18, 215, 214, 103, 307, 110, 19, 104, 311, 205, 20, 213, 112)),
    ((16, 207, 101, 308, 17, 309, 102, 215, 18, 103, 214, 310, 104, 19, 111, 20, 213, 306, 105, 312),
     (101, 16, 207, 17, 308, 102, 215, 18, 309, 103, 310, 19, 220, 306, 214, 311, 104, 105, 312, 213)),
    ((308, 16, 215, 109, 317, 207, 101, 214, 102, 103, 18, 310, 19, 206, 213, 111, 205, 104, 320, 312),
     (16, 308, 215, 101, 207, 102, 17, 18, 309, 206, 214, 103, 310, 104, 19, 320, 311, 205, 213, 112)),
    ((16, 308, 101, 215, 109, 17, 110, 207, 318, 214, 102, 206, 103, 104, 19, 320, 213, 311, 205, 212),
     (101, 16, 308, 17, 309, 207, 215, 102, 214, 103, 18, 19, 310, 206, 212, 104, 313, 111, 20, 105)),
    ((16, 101, 308, 17, 309, 215, 102, 207, 110, 18, 214, 111, 319, 206, 103, 320, 212, 104, 213, 105),
     (308, 16, 101, 215, 102, 207, 17, 309, 18, 310, 206, 103, 213, 104, 314, 19, 20, 311, 205, 112)),
    ((101, 16, 308, 215, 17, 309, 102, 310, 18, 207, 206, 103, 311, 213, 112, 19, 314, 120, 205, 104),
     (16, 308, 101, 109, 215, 17, 207, 214, 102, 310, 103, 18, 311, 19, 206, 104, 205, 20, 213, 112)),
    ((16, 308, 101, 309, 207, 102, 17, 18, 214, 215, 103, 310, 19, 206, 311, 104, 113, 20, 312, 205),
     (101, 16, 308, 215, 17, 309, 207, 102, 110, 18, 206, 103, 311, 112, 19, 214, 204, 205, 120, 213)),
    ((308, 101, 16, 215, 17, 309, 207, 102, 310, 103, 18, 19, 214, 313, 104, 205, 311, 20, 112, 206),
     (16, 308, 101, 309, 207, 102, 17, 18, 215, 310, 205, 103, 111, 19, 206, 313, 104, 214, 312, 20)),
    ((16, 308, 101, 215, 102, 17, 309, 18, 314, 310, 206, 103, 207, 104, 19, 20, 213, 111, 105, 312),
     (308, 101, 16, 17, 309, 206, 207, 102, 215, 103, 18, 19, 314, 310, 213, 104, 311, 20, 312, 105)),
    ((16, 101, 207, 308, 17, 215, 309, 102, 103, 18, 310, 214, 19, 311, 104, 312, 105, 20, 213, 106),
     (207, 308, 16, 101, 309, 102, 17, 215, 18, 310, 214, 103, 311, 104, 19, 213, 20, 105, 312, 106)),
)


def offset_of(kind, link):
    y, z = divmod(kind, 8)
    return (16, 1 if z > 0 else -7, -1 if z < 7 else 7, 8 if y == 1 else -8)[link]


def target_of(kind, link):
    y, z = divmod(kind, 8)
    return (kind, y * 8 + (z + 1) % 8, y * 8 + (z + 7) % 8, (1 - y) * 8 + z)[link]


def forward_table():
    table = []
    for kind in range(16):
        halves = []
        for half in range(2):
            held = [0] + [a % 100 for a in ARRIVALS[kind][half]]
            rows = []
            for distance in held:
                row = []
                for link in range(4):
                    there = target_of(kind, link)
                    far = distance + offset_of(there, link)
                    order = ARRIVALS[there][half]
                    wanted = link * 100 + far
                    row.append(order.index(wanted) + 1 if 1 <= far <= REACH and wanted in order else 0)
                rows.append(row)
            halves.append(rows)
        table.append(halves)
    return table


TABLE = forward_table()


def kernel(q_hbm, k_hbm, v_hbm, seg_hbm, own_hbm, out_ref, cache_ref,
           q_ref, seg_ref, own_ref, kv, bias, top, total, acc, outgoing, mid, recv, block,
           in_sem, kv_send, kv_recv, z_send, z_recv, x_send, x_recv, y_send, y_recv, c_send, c_recv, own_sem):
    me, g = lax.axis_index("inst"), lax.axis_index("head")
    kind = me % 16
    x, y, z = me // 16, (me // 8) % 2, me % 8
    other_y = x * 16 + (1 - y) * 8 + z
    other_chip, other_core = (g + 2) % 4, g + 1 - 2 * (g % 2)
    near = (
        ((x + 1) % 4) * 16 + kind,
        me - z + (z + 1) % 8,
        me - z + (z + 7) % 8,
        other_y,
    )

    inputs = [
        pltpu.make_async_copy(k_hbm.at[:, half * SIZE:(half + 1) * SIZE], kv.at[half, 0, 0:TOK], in_sem.at[half])
        for half in range(2)
    ] + [
        pltpu.make_async_copy(v_hbm.at[:, half * SIZE:(half + 1) * SIZE], kv.at[half, 0, TOK:2 * TOK], in_sem.at[2 + half])
        for half in range(2)
    ] + [
        pltpu.make_async_copy(seg_hbm, seg_ref, in_sem.at[4]),
        pltpu.make_async_copy(own_hbm, own_ref, in_sem.at[5]),
        pltpu.make_async_copy(q_hbm, q_ref, in_sem.at[6]),
    ]
    for copy in inputs:
        copy.start()

    def along_z(by):
        return (me - z + (z + by) % 8, g)

    def along_x(by):
        return (((x + by) % 4) * 16 + kind, g)

    beside = ((me, other_chip), (other_y, g), (other_y, other_chip))
    sibling = (me, other_core)
    barrier = pltpu.get_barrier_semaphore()
    partners = [along_z(by) for by in range(1, 8)] + [along_x(by) for by in range(1, 4)] + list(beside) + [sibling]
    for partner in partners:
        pl.semaphore_signal(barrier, inc=1, device_id=partner, device_id_type=MESH)

    def pick(values):
        chosen = jnp.int32(values[0])
        if len(set(values)) == 1:
            return chosen
        for t in range(1, 16):
            chosen = jnp.where(kind == t, jnp.int32(values[t]), chosen)
        return chosen

    first = [[pick([TABLE[t][half][0][link] for t in range(16)]) for link in range(4)] for half in range(2)]
    codes = [
        [
            [pick([sum(TABLE[t][half][STEP * k + jj + 1][link] * 64 ** k for k in range(5)) for t in range(16)]) for link in range(4)]
            for jj in range(STEP)
        ]
        for half in range(2)
    ]

    def digits(half, jj, k):
        return [(codes[half][jj][link] >> (6 * k)) & 63 for link in range(4)]

    def forward(half, slot, theres, wait=False):
        for link in range(4):
            there = theres[link]

            @pl.when(there > 0)
            def _():
                copy = pltpu.make_async_remote_copy(
                    src_ref=kv.at[half, slot],
                    dst_ref=kv.at[half, there],
                    send_sem=kv_send.at[half * 4 + link, slot],
                    recv_sem=kv_recv.at[half, there],
                    device_id=(near[link], g),
                    device_id_type=MESH,
                )
                if wait:
                    copy.wait_send()
                else:
                    copy.start()

    def arrive(k, h, j):
        half, jj = j % 2, 2 * h + j // 2
        slot = STEP * k + jj + 1
        pltpu.make_async_copy(kv.at[half, slot], kv.at[half, slot], kv_recv.at[half, slot]).wait()
        forward(half, slot, digits(half, jj, k))

    for copy in inputs[:5]:
        copy.wait()
    seg_row = seg_ref[...].astype(F32)
    seg_wide = jnp.broadcast_to(seg_row, (TOK, TOK))
    for half in range(2):
        kv[half, 0, SEG_ROW:BLOCK_ROWS, :] = jnp.concatenate(
            [jnp.broadcast_to(seg_row[:, 0:SIZE], (8, SIZE)), jnp.broadcast_to(seg_row[:, SIZE:], (8, SIZE))], axis=0
        ).astype(BF16)
    pl.semaphore_wait(barrier, len(partners))
    forward(0, 0, first[0])
    forward(1, 0, first[1])

    inputs[5].wait()
    dest = own_ref[...]
    owner = lax.broadcasted_iota(jnp.int32, (64, TOK), 0)
    hot = (owner == dest).astype(F32)
    before = (lax.broadcasted_iota(jnp.int32, (TOK, TOK), 0) < lax.broadcasted_iota(jnp.int32, (TOK, TOK), 1)).astype(BF16)
    count = jnp.dot(hot.astype(BF16), before, preferred_element_type=F32)
    place = jnp.sum(hot * count, axis=0, keepdims=True).astype(jnp.int32)
    target = dest * (2 * SLOT) + place
    row = lax.broadcasted_iota(jnp.int32, (1024, TOK), 0)
    of_keys = (row == target).astype(BF16)
    of_values = (row == target + SLOT).astype(BF16)
    for half in range(2):
        rows = jnp.dot(of_keys, kv[half, 0, 0:TOK, :], preferred_element_type=F32)
        rows += jnp.dot(of_values, kv[half, 0, TOK:2 * TOK, :], preferred_element_type=F32)
        outgoing[:, :, :, :, half * SIZE:(half + 1) * SIZE] = rows.astype(BF16).reshape(4, 2, 8, 2 * SLOT, SIZE)

    def z_copy(by):
        return pltpu.make_async_remote_copy(
            src_ref=outgoing.at[:, :, (z + by) % 8], dst_ref=mid.at[z], send_sem=z_send.at[by], recv_sem=z_recv.at[z],
            device_id=along_z(by), device_id_type=MESH)

    def x_copy(by):
        return pltpu.make_async_remote_copy(
            src_ref=mid.at[:, (x + by) % 4], dst_ref=recv.at[x], send_sem=x_send.at[by], recv_sem=x_recv.at[x],
            device_id=along_x(by), device_id_type=MESH)

    def rows_of(source_y, group):
        return cache_ref.at[:, source_y, :, pl.ds(pl.multiple_of(group * 512, 512), 512)]

    def y_copy(n):
        return pltpu.make_async_remote_copy(
            src_ref=block.at[y if n == 0 else 1 - y], dst_ref=rows_of(y, g), send_sem=y_send.at[n], recv_sem=y_recv.at[n],
            device_id=beside[n], device_id_type=MESH)

    from_y = ((y, other_chip), (1 - y, g), (1 - y, other_chip))

    def c_copy(n):
        if n == 3:
            src, place = block.at[y], rows_of(y, g)
        else:
            src = place = rows_of(*from_y[n])
        return pltpu.make_async_remote_copy(
            src_ref=src, dst_ref=place, send_sem=c_send.at[n], recv_sem=c_recv.at[n],
            device_id=sibling, device_id_type=MESH)

    def own_copy():
        return pltpu.make_async_copy(block.at[y], rows_of(y, g), own_sem)

    def first_leg():
        for by in (1, 7, 2, 6, 3, 5, 4):
            z_copy(by).start()
        for i in range(4):
            for j in range(2):
                mid[z, i, j] = outgoing[i, j, z]

    def second_leg():
        for by in range(1, 8):
            src = (z + 8 - by) % 8
            pltpu.make_async_copy(mid.at[src], mid.at[src], z_recv.at[src]).wait()
        for by in (1, 3, 2):
            x_copy(by).start()
        for i in range(8):
            recv[x, i] = mid[i, x]

    def third_leg():
        for by in range(1, 4):
            src = (x + 4 - by) % 4
            pltpu.make_async_copy(recv.at[src], recv.at[src], x_recv.at[src]).wait()
        a = lax.broadcasted_iota(jnp.int32, (64, 128), 0)
        b = lax.broadcasted_iota(jnp.int32, (64, 128), 1)
        key_rows = (b == 2 * a - (a & 7)).astype(BF16)
        value_rows = (b == 2 * a - (a & 7) + 8).astype(BF16)
        for src in range(4):
            for j in range(2):
                arrived = recv[src, :, j].reshape(128, 2 * SIZE)
                block[j, src, :, 0:256] = jnp.dot(key_rows, arrived, preferred_element_type=F32).astype(BF16)
                block[j, src, :, 256:512] = jnp.dot(value_rows, arrived, preferred_element_type=F32).astype(BF16)
        for n in range(3):
            y_copy(n).start()
        c_copy(3).start()
        own_copy().start()

    def fourth_leg():
        for n in range(3):
            here = rows_of(*from_y[n])
            pltpu.make_async_copy(here, here, y_recv.at[n]).wait()
            c_copy(n).start()

    at0 = lax.broadcasted_iota(jnp.int32, (TOK, TOK), 0)
    at1 = lax.broadcasted_iota(jnp.int32, (TOK, TOK), 1)
    seg_col = jnp.sum(jnp.where(at0 == at1, seg_wide, 0.0), axis=1, keepdims=True)
    seg_col = jnp.broadcast_to(seg_col, (TOK, SIZE))
    seg_both = jnp.concatenate([seg_col, seg_col], axis=1)
    bias[:, 0:TOK] = jnp.where((seg_both == seg_wide) & (at0 >= at1), 0.0, -1e30)

    def head_scores(h, slot, c):
        q_h = q_ref[:, h * SIZE:(h + 1) * SIZE]
        scores = lax.dot_general(q_h, kv[h // RATIO, slot, 0:TOK, :], (((1,), (1,)), ((), ())), preferred_element_type=F32)
        return scores + bias[:, c * TOK:(c + 1) * TOK]

    def weighted(h, slot, scores, peak):
        weights = jnp.exp2((scores - jnp.concatenate([peak, peak], axis=1)) * TO_LOG2)
        product = jnp.dot(weights.astype(BF16), kv[h // RATIO, slot, TOK:2 * TOK, :], preferred_element_type=F32)
        return weights[:, 0:SIZE] + weights[:, SIZE:], product

    inputs[6].wait()
    for half in range(2):
        for j in range(4):
            for h in range(half * RATIO + 2 * j, half * RATIO + 2 * j + 2):
                scores = head_scores(h, 0, 0)
                peak = jnp.broadcast_to(jnp.max(scores, axis=1, keepdims=True), (TOK, SIZE))
                part, product = weighted(h, 0, scores, peak)
                top[h], total[h], acc[h] = peak, part, product
            arrive(0, half, j)
        if half == 0:
            first_leg()
    second_leg()

    def step(k, carry):
        for half in range(2):
            slots = [STEP * k + 1 + c for c in range(STEP)]
            for c in range(STEP):
                seg_rows = kv[half, slots[c], SEG_ROW:BLOCK_ROWS, :].astype(F32)
                for part in range(2):
                    key_seg = jnp.broadcast_to(seg_rows[8 * part:8 * part + 1, :], (TOK, SIZE))
                    at = c * TOK + part * SIZE
                    bias[:, at:at + SIZE] = jnp.where(seg_col == key_seg, 0.0, -1e30)
            for j in range(4):
                for h in range(half * RATIO + 2 * j, half * RATIO + 2 * j + 2):
                    scores = [head_scores(h, slots[c], c) for c in range(STEP)]
                    largest = functools.reduce(jnp.maximum, scores)
                    old = top[h]
                    peak = jnp.maximum(old, jnp.max(largest, axis=1, keepdims=True))
                    shrink = jnp.exp2((old - peak) * TO_LOG2)
                    parts, products = zip(*[weighted(h, slots[c], scores[c], peak) for c in range(STEP)])
                    top[h] = peak
                    total[h] = total[h] * shrink + sum(parts[1:], parts[0])
                    acc[h] = acc[h] * shrink + sum(products[1:], products[0])

                @pl.when(k < 4)
                def _():
                    arrive(k + 1, half, j)

        @pl.when(k == 1)
        def _():
            third_leg()

        @pl.when(k == 3)
        def _():
            fourth_leg()

        return carry

    lax.fori_loop(0, 5, step, 0)

    for h in range(HEADS):
        denominator = jnp.sum(total[h], axis=1, keepdims=True)
        out_ref[:, h * SIZE:(h + 1) * SIZE] = (acc[h] / denominator).astype(BF16)

    for half in range(2):
        forward(half, 0, first[half], wait=True)

    def drain(k, carry):
        for half in range(2):
            for jj in range(STEP):
                forward(half, STEP * k + jj + 1, digits(half, jj, k), wait=True)
        return carry

    lax.fori_loop(0, 5, drain, 0)
    for by in range(1, 8):
        z_copy(by).wait_send()
    for by in range(1, 4):
        x_copy(by).wait_send()
    for n in range(3):
        y_copy(n).wait_send()
    own_copy().wait()
    across = (other_core + 2) % 4
    from_core = ((y, across), (1 - y, other_core), (1 - y, across), (y, other_core))
    for n in range(4):
        c_copy(n).wait_send()
        here = rows_of(*from_core[n])
        pltpu.make_async_copy(here, here, c_recv.at[n]).wait()


def on_device(queries, keys, values, segments, owners):
    whole = pl.BlockSpec(memory_space=pl.ANY)
    attended, cache = pl.pallas_call(
        kernel,
        out_shape=(
            jax.ShapeDtypeStruct((TOK, HEADS * SIZE), BF16),
            jax.ShapeDtypeStruct((4, 2, 64, 2048), BF16),
        ),
        in_specs=[whole] * 5,
        out_specs=(pl.BlockSpec(memory_space=pltpu.VMEM), whole),
        scratch_shapes=[
            pltpu.VMEM((TOK, HEADS * SIZE), BF16),
            pltpu.VMEM((1, TOK), jnp.int32),
            pltpu.VMEM((1, TOK), jnp.int32),
            pltpu.VMEM((2, REACH + 1, BLOCK_ROWS, SIZE), BF16),
            pltpu.VMEM((TOK, STEP * TOK), F32),
            pltpu.VMEM((HEADS, TOK, SIZE), F32),
            pltpu.VMEM((HEADS, TOK, SIZE), F32),
            pltpu.VMEM((HEADS, TOK, SIZE), F32),
            pltpu.VMEM((4, 2, 8, 2 * SLOT, 2 * SIZE), BF16),
            pltpu.VMEM((8, 4, 2, 2 * SLOT, 2 * SIZE), BF16),
            pltpu.VMEM((4, 8, 2, 2 * SLOT, 2 * SIZE), BF16),
            pltpu.VMEM((2, 4, 64, 4 * SIZE), BF16),
            pltpu.SemaphoreType.DMA((7,)),
            pltpu.SemaphoreType.DMA((8, REACH + 1)),
            pltpu.SemaphoreType.DMA((2, REACH + 1)),
            pltpu.SemaphoreType.DMA((8,)),
            pltpu.SemaphoreType.DMA((8,)),
            pltpu.SemaphoreType.DMA((4,)),
            pltpu.SemaphoreType.DMA((4,)),
            pltpu.SemaphoreType.DMA((3,)),
            pltpu.SemaphoreType.DMA((3,)),
            pltpu.SemaphoreType.DMA((4,)),
            pltpu.SemaphoreType.DMA((4,)),
            pltpu.SemaphoreType.DMA(()),
        ],
        compiler_params=pltpu.CompilerParams(
            collective_id=0, has_side_effects=True, vmem_limit_bytes=56 * 1024 * 1024
        ),
        cost_estimate=pl.CostEstimate(flops=12_000_000_000, bytes_accessed=6_000_000, transcendentals=22_000_000),
        name="attend_and_send",
    )(queries, keys, values, segments.reshape(1, TOK), owners.reshape(1, TOK))
    return attended, cache.reshape(64 * SLOT, 2048)


def solution(mesh):
    return jax.shard_map(
        on_device,
        mesh=mesh,
        in_specs=(
            P("inst", "head"),
            P("inst", "head"),
            P("inst", "head"),
            P("inst"),
            P("inst", None),
        ),
        out_specs=(P("inst", "head"), P("inst", None)),
        check_vma=False,
    )
```

```python
import functools

import jax
import jax.numpy as jnp
from jax import lax
from jax.experimental import pallas as pl
from jax.experimental.pallas import tpu as pltpu
from jax.sharding import PartitionSpec as P

MESH = pl.DeviceIdType.MESH
F32, BF16 = jnp.float32, jnp.bfloat16

HEADS, SIZE, RATIO = 16, 128, 8
TOK = 256
REACH = 20
SLOT = 8
STEP = 4
KEY_ROW, MASK_ROW, SENT_ROWS, ALL_ROWS = 128, 256, 272, 384
FAR = 1024.0
ROWS = 16
TO_LOG2 = SIZE ** -0.5 * 1.4426950408889634

ARRIVALS = (
    ((16, 215, 109, 308, 301, 214, 307, 17, 102, 213, 306, 18, 212, 310, 211, 104, 305, 103, 20, 19),
     (16, 308, 215, 109, 214, 110, 101, 213, 307, 17, 102, 212, 103, 18, 111, 19, 306, 205, 204, 20)),
    ((16, 101, 308, 215, 117, 307, 110, 214, 302, 309, 213, 18, 212, 103, 19, 306, 211, 204, 305, 20),
     (101, 16, 215, 17, 308, 214, 309, 110, 213, 111, 102, 307, 18, 306, 205, 103, 104, 19, 212, 120)),
    ((101, 16, 308, 17, 215, 309, 102, 214, 18, 213, 111, 310, 212, 307, 303, 205, 306, 19, 304, 20),
     (16, 101, 215, 102, 308, 17, 214, 18, 307, 109, 310, 206, 111, 112, 213, 103, 119, 205, 104, 120)),
    ((101, 16, 17, 215, 308, 102, 214, 307, 18, 213, 103, 206, 309, 19, 310, 305, 212, 304, 111, 20),
     (16, 101, 215, 308, 17, 102, 214, 307, 103, 18, 309, 19, 110, 206, 111, 213, 112, 205, 104, 120)),
    ((101, 16, 215, 308, 17, 214, 207, 102, 213, 310, 18, 103, 206, 309, 19, 311, 204, 205, 20, 212),
     (16, 101, 215, 117, 308, 307, 102, 309, 18, 103, 214, 310, 19, 104, 206, 111, 20, 112, 113, 205)),
    ((16, 101, 215, 308, 102, 17, 307, 214, 18, 109, 205, 310, 103, 311, 19, 306, 104, 213, 112, 20),
     (101, 16, 308, 17, 215, 102, 309, 207, 18, 310, 103, 205, 19, 214, 104, 213, 20, 311, 206, 112)),
    ((16, 101, 308, 215, 206, 17, 102, 307, 103, 18, 310, 19, 214, 309, 213, 104, 311, 112, 20, 305),
     (101, 16, 17, 308, 102, 309, 206, 18, 215, 214, 103, 307, 110, 19, 104, 311, 205, 20, 213, 112)),
    ((16, 207, 101, 308, 17, 309, 102, 215, 18, 103, 214, 310, 104, 19, 111, 20, 213, 306, 105, 312),
     (101, 16, 207, 17, 308, 102, 215, 18, 309, 103, 310, 19, 220, 306, 214, 311, 104, 105, 312, 213)),
    ((308, 16, 215, 109, 317, 207, 101, 214, 102, 103, 18, 310, 19, 206, 213, 111, 205, 104, 320, 312),
     (16, 308, 215, 101, 207, 102, 17, 18, 309, 206, 214, 103, 310, 104, 19, 320, 311, 205, 213, 112)),
    ((16, 308, 101, 215, 109, 17, 110, 207, 318, 214, 102, 206, 103, 104, 19, 320, 213, 311, 205, 212),
     (101, 16, 308, 17, 309, 207, 215, 102, 214, 103, 18, 19, 310, 206, 212, 104, 313, 111, 20, 105)),
    ((16, 101, 308, 17, 309, 215, 102, 207, 110, 18, 214, 111, 319, 206, 103, 320, 212, 104, 213, 105),
     (308, 16, 101, 215, 102, 207, 17, 309, 18, 310, 206, 103, 213, 104, 314, 19, 20, 311, 205, 112)),
    ((101, 16, 308, 215, 17, 309, 102, 310, 18, 207, 206, 103, 311, 213, 112, 19, 314, 120, 205, 104),
     (16, 308, 101, 109, 215, 17, 207, 214, 102, 310, 103, 18, 311, 19, 206, 104, 205, 20, 213, 112)),
    ((16, 308, 101, 309, 207, 102, 17, 18, 214, 215, 103, 310, 19, 206, 311, 104, 113, 20, 312, 205),
     (101, 16, 308, 215, 17, 309, 207, 102, 110, 18, 206, 103, 311, 112, 19, 214, 204, 205, 120, 213)),
    ((308, 101, 16, 215, 17, 309, 207, 102, 310, 103, 18, 19, 214, 313, 104, 205, 311, 20, 112, 206),
     (16, 308, 101, 309, 207, 102, 17, 18, 215, 310, 205, 103, 111, 19, 206, 313, 104, 214, 312, 20)),
    ((16, 308, 101, 215, 102, 17, 309, 18, 314, 310, 206, 103, 207, 104, 19, 20, 213, 111, 105, 312),
     (308, 101, 16, 17, 309, 206, 207, 102, 215, 103, 18, 19, 314, 310, 213, 104, 311, 20, 312, 105)),
    ((16, 101, 207, 308, 17, 215, 309, 102, 103, 18, 310, 214, 19, 311, 104, 312, 105, 20, 213, 106),
     (207, 308, 16, 101, 309, 102, 17, 215, 18, 310, 214, 103, 311, 104, 19, 213, 20, 105, 312, 106)),
)


def offset_of(kind, link):
    y, z = divmod(kind, 8)
    return (16, 1 if z > 0 else -7, -1 if z < 7 else 7, 8 if y == 1 else -8)[link]


def target_of(kind, link):
    y, z = divmod(kind, 8)
    return (kind, y * 8 + (z + 1) % 8, y * 8 + (z + 7) % 8, (1 - y) * 8 + z)[link]


def forward_table():
    table = []
    for kind in range(16):
        halves = []
        for half in range(2):
            held = [0] + [a % 100 for a in ARRIVALS[kind][half]]
            rows = []
            for distance in held:
                row = []
                for link in range(4):
                    there = target_of(kind, link)
                    far = distance + offset_of(there, link)
                    order = ARRIVALS[there][half]
                    wanted = link * 100 + far
                    row.append(order.index(wanted) + 1 if 1 <= far <= REACH and wanted in order else 0)
                rows.append(row)
            halves.append(rows)
        table.append(halves)
    return table


TABLE = forward_table()


def kernel(q_hbm, k_hbm, v_hbm, seg_hbm, own_hbm, out_ref, cache_ref,
           q_aug, k_own, v_own, seg_ref, own_ref, kv, bias, top, total, acc, scores_a, scores_b, weights_a, weights_b, shrink_a, shrink_b,
           outgoing, mid, recv, block,
           in_sem, q_sem, kv_send, kv_recv, z_send, z_recv, x_send, x_recv, y_send, y_recv, c_send, c_recv, own_sem):
    me, g = lax.axis_index("inst"), lax.axis_index("head")
    kind = me % 16
    x, y, z = me // 16, (me // 8) % 2, me % 8
    other_y = x * 16 + (1 - y) * 8 + z
    other_chip, other_core = (g + 2) % 4, g + 1 - 2 * (g % 2)
    near = (
        ((x + 1) % 4) * 16 + kind,
        me - z + (z + 1) % 8,
        me - z + (z + 7) % 8,
        other_y,
    )

    inputs = [
        pltpu.make_async_copy(src, dst, in_sem.at[n])
        for n, (src, dst) in enumerate(((k_hbm, k_own), (v_hbm, v_own), (seg_hbm, seg_ref), (own_hbm, own_ref)))
    ]
    queries = [
        pltpu.make_async_copy(q_hbm.at[:, h * SIZE:(h + 1) * SIZE], q_aug.at[h, :, 0:SIZE], q_sem.at[h]) for h in range(HEADS)
    ]
    for copy in inputs + queries:
        copy.start()

    def along_z(by):
        return (me - z + (z + by) % 8, g)

    def along_x(by):
        return (((x + by) % 4) * 16 + kind, g)

    beside = ((me, other_chip), (other_y, g), (other_y, other_chip))
    sibling = (me, other_core)
    barrier = pltpu.get_barrier_semaphore()
    partners = [along_z(by) for by in range(1, 8)] + [along_x(by) for by in range(1, 4)] + list(beside) + [sibling]
    for partner in partners:
        pl.semaphore_signal(barrier, inc=1, device_id=partner, device_id_type=MESH)

    def pick(values):
        chosen = jnp.int32(values[0])
        if len(set(values)) == 1:
            return chosen
        for t in range(1, 16):
            chosen = jnp.where(kind == t, jnp.int32(values[t]), chosen)
        return chosen

    first = [[pick([TABLE[t][half][0][link] for t in range(16)]) for link in range(4)] for half in range(2)]
    codes = [
        [
            [pick([sum(TABLE[t][half][STEP * k + jj + 1][link] * 64 ** k for k in range(5)) for t in range(16)]) for link in range(4)]
            for jj in range(STEP)
        ]
        for half in range(2)
    ]

    def digits(half, jj, k):
        return [(codes[half][jj][link] >> (6 * k)) & 63 for link in range(4)]

    def forward(half, slot, theres, wait=False):
        for link in range(4):
            there = theres[link]

            @pl.when(there > 0)
            def _():
                copy = pltpu.make_async_remote_copy(
                    src_ref=kv.at[half, slot, 0:SENT_ROWS],
                    dst_ref=kv.at[half, there, 0:SENT_ROWS],
                    send_sem=kv_send.at[half * 4 + link, slot],
                    recv_sem=kv_recv.at[half, there],
                    device_id=(near[link], g),
                    device_id_type=MESH,
                )
                if wait:
                    copy.wait_send()
                else:
                    copy.start()

    def arrive(k, h, j):
        half, jj = j % 2, 2 * h + j // 2
        slot = STEP * k + jj + 1
        here = kv.at[half, slot, 0:SENT_ROWS]
        pltpu.make_async_copy(here, here, kv_recv.at[half, slot]).wait()
        forward(half, slot, digits(half, jj, k))

    for copy in inputs[:3]:
        copy.wait()
    seg_row = seg_ref[...].astype(F32)
    seg_wide = jnp.broadcast_to(seg_row, (TOK, TOK))
    request = lax.broadcasted_iota(jnp.int32, (16, TOK), 0).astype(F32)
    for half in range(2):
        feat = slice(half * SIZE, (half + 1) * SIZE)
        kv[half, 0, 0:KEY_ROW, 0:SIZE] = v_own[0:SIZE, feat]
        kv[half, 0, 0:KEY_ROW, SIZE:TOK] = v_own[SIZE:TOK, feat]
        kv[half, 0, KEY_ROW:MASK_ROW, :] = k_own[:, feat].astype(F32).T.astype(BF16)
        kv[half, 0, MASK_ROW:SENT_ROWS, :] = jnp.where(seg_wide[0:16] == request, 0.0, -FAR).astype(BF16)
    pl.semaphore_wait(barrier, len(partners))
    forward(0, 0, first[0])
    forward(1, 0, first[1])

    def clear(slot, carry):
        for half in range(2):
            kv[half, slot, SENT_ROWS:ALL_ROWS, :] = jnp.zeros((ALL_ROWS - SENT_ROWS, TOK), BF16)
        return carry

    lax.fori_loop(0, REACH + 1, clear, 0)

    inputs[3].wait()
    dest = own_ref[...]
    owner = lax.broadcasted_iota(jnp.int32, (64, TOK), 0)
    hot = (owner == dest).astype(F32)
    before = (lax.broadcasted_iota(jnp.int32, (TOK, TOK), 0) < lax.broadcasted_iota(jnp.int32, (TOK, TOK), 1)).astype(BF16)
    count = jnp.dot(hot.astype(BF16), before, preferred_element_type=F32)
    place = jnp.sum(hot * count, axis=0, keepdims=True).astype(jnp.int32)
    target = dest * (2 * SLOT) + place
    row = lax.broadcasted_iota(jnp.int32, (1024, TOK), 0)
    of_keys = (row == target).astype(BF16)
    of_values = (row == target + SLOT).astype(BF16)
    rows = jnp.dot(of_keys, k_own[...], preferred_element_type=F32)
    rows += jnp.dot(of_values, v_own[...], preferred_element_type=F32)
    outgoing[...] = rows.astype(BF16).reshape(4, 2, 8, 2 * SLOT, 2 * SIZE)

    def z_copy(by):
        return pltpu.make_async_remote_copy(
            src_ref=outgoing.at[:, :, (z + by) % 8], dst_ref=mid.at[z], send_sem=z_send.at[by], recv_sem=z_recv.at[z],
            device_id=along_z(by), device_id_type=MESH)

    def x_copy(by):
        return pltpu.make_async_remote_copy(
            src_ref=mid.at[:, (x + by) % 4], dst_ref=recv.at[x], send_sem=x_send.at[by], recv_sem=x_recv.at[x],
            device_id=along_x(by), device_id_type=MESH)

    def rows_of(source_y, group):
        return cache_ref.at[:, source_y, :, pl.ds(pl.multiple_of(group * 512, 512), 512)]

    def y_copy(n):
        return pltpu.make_async_remote_copy(
            src_ref=block.at[y if n == 0 else 1 - y], dst_ref=rows_of(y, g), send_sem=y_send.at[n], recv_sem=y_recv.at[n],
            device_id=beside[n], device_id_type=MESH)

    from_y = ((y, other_chip), (1 - y, g), (1 - y, other_chip))

    def c_copy(n):
        if n == 3:
            src, place = block.at[y], rows_of(y, g)
        else:
            src = place = rows_of(*from_y[n])
        return pltpu.make_async_remote_copy(
            src_ref=src, dst_ref=place, send_sem=c_send.at[n], recv_sem=c_recv.at[n],
            device_id=sibling, device_id_type=MESH)

    def own_copy():
        return pltpu.make_async_copy(block.at[y], rows_of(y, g), own_sem)

    def first_leg():
        for by in (1, 7, 2, 6, 3, 5, 4):
            z_copy(by).start()
        for i in range(4):
            for j in range(2):
                mid[z, i, j] = outgoing[i, j, z]

    def second_leg():
        for by in range(1, 8):
            src = (z + 8 - by) % 8
            pltpu.make_async_copy(mid.at[src], mid.at[src], z_recv.at[src]).wait()
        for by in (1, 3, 2):
            x_copy(by).start()
        for i in range(8):
            recv[x, i] = mid[i, x]

    def third_leg():
        for by in range(1, 4):
            src = (x + 4 - by) % 4
            pltpu.make_async_copy(recv.at[src], recv.at[src], x_recv.at[src]).wait()
        a = lax.broadcasted_iota(jnp.int32, (64, 128), 0)
        b = lax.broadcasted_iota(jnp.int32, (64, 128), 1)
        key_rows = (b == 2 * a - (a & 7)).astype(BF16)
        value_rows = (b == 2 * a - (a & 7) + 8).astype(BF16)
        for src in range(4):
            for j in range(2):
                arrived = recv[src, :, j].reshape(128, 2 * SIZE)
                block[j, src, :, 0:256] = jnp.dot(key_rows, arrived, preferred_element_type=F32).astype(BF16)
                block[j, src, :, 256:512] = jnp.dot(value_rows, arrived, preferred_element_type=F32).astype(BF16)
        for n in range(3):
            y_copy(n).start()
        c_copy(3).start()
        own_copy().start()

    def fourth_leg():
        for n in range(3):
            here = rows_of(*from_y[n])
            pltpu.make_async_copy(here, here, y_recv.at[n]).wait()
            c_copy(n).start()

    at0 = lax.broadcasted_iota(jnp.int32, (TOK, TOK), 0)
    at1 = lax.broadcasted_iota(jnp.int32, (TOK, TOK), 1)
    seg_col = jnp.sum(jnp.where(at0 == at1, seg_wide, 0.0), axis=1, keepdims=True)
    lane = lax.broadcasted_iota(jnp.int32, (TOK, SIZE), 1).astype(F32)
    query_mask = jnp.where(lane == seg_col, FAR, 0.0).astype(BF16)
    for h in range(HEADS):
        q_aug[h, :, SIZE:2 * SIZE] = query_mask
    bias[...] = jnp.where(at0 >= at1, 0.0, -1e30)
    scores_of, weights_of, shrink_of = (scores_a, scores_b), (weights_a, weights_b), (shrink_a, shrink_b)

    def unit(half, slots, diagonal):
        width = len(slots) * TOK

        def score(i, c):
            scores_of[i % 2][:, c * TOK:(c + 1) * TOK] = jnp.dot(
                q_aug[half * RATIO + i], kv[half, slots[c], KEY_ROW:ALL_ROWS, :], preferred_element_type=F32)

        def soften(i, at):
            h, rows = half * RATIO + i, slice(at, at + ROWS)
            parts = [scores_of[i % 2][rows, j:j + SIZE] for j in range(0, width, SIZE)]
            if diagonal:
                parts = [part + bias[rows, n * SIZE:(n + 1) * SIZE] for n, part in enumerate(parts)]
            largest = jnp.max(functools.reduce(jnp.maximum, parts), axis=1, keepdims=True)
            if diagonal:
                peak = jnp.broadcast_to(largest, (ROWS, SIZE))
            else:
                old = top[h, rows, :]
                peak = jnp.maximum(old, largest)
                shrink = jnp.exp2((old - peak) * TO_LOG2)
                shrink_of[i % 2][rows, :] = shrink
            weights = [jnp.exp2((part - peak) * TO_LOG2) for part in parts]
            for n, weight in enumerate(weights):
                weights_of[i % 2][rows, n * SIZE:(n + 1) * SIZE] = weight.astype(BF16)
            added = functools.reduce(jnp.add, weights)
            top[h, rows, :] = peak
            total[h, rows, :] = added if diagonal else total[h, rows, :] * shrink + added

        def combine(i):
            h = half * RATIO + i
            values = jnp.concatenate(
                [kv[half, slot, 0:KEY_ROW, lanes:lanes + SIZE] for slot in slots for lanes in (0, SIZE)], axis=0)
            product = jnp.dot(weights_of[i % 2][:, 0:width], values, preferred_element_type=F32)
            acc[h] = product if diagonal else acc[h] * shrink_of[i % 2][...] + product

        for c in range(len(slots)):
            score(0, c)
        for i in range(RATIO):
            for quarter in range(4):
                if i + 1 < RATIO and quarter < len(slots):
                    score(i + 1, quarter)
                for at in range(quarter * 64, quarter * 64 + 64, ROWS):
                    soften(i, at)
                if quarter == 1 and i > 0:
                    combine(i - 1)
        combine(RATIO - 1)

    for copy in queries:
        copy.wait()
    for half in range(2):
        unit(half, [0], True)
        for j in range(4):
            arrive(0, half, j)
        if half == 0:
            first_leg()
    second_leg()

    def step(k, carry):
        for half in range(2):
            unit(half, [STEP * k + 1 + c for c in range(STEP)], False)

            @pl.when(k < 4)
            def _():
                for j in range(4):
                    arrive(k + 1, half, j)

        @pl.when(k == 1)
        def _():
            third_leg()

        @pl.when(k == 3)
        def _():
            fourth_leg()

        return carry

    lax.fori_loop(0, 5, step, 0)

    for h in range(HEADS):
        denominator = jnp.sum(total[h], axis=1, keepdims=True)
        out_ref[:, h * SIZE:(h + 1) * SIZE] = (acc[h] / denominator).astype(BF16)

    for half in range(2):
        forward(half, 0, first[half], wait=True)

    def drain(k, carry):
        for half in range(2):
            for jj in range(STEP):
                forward(half, STEP * k + jj + 1, digits(half, jj, k), wait=True)
        return carry

    lax.fori_loop(0, 5, drain, 0)
    for by in range(1, 8):
        z_copy(by).wait_send()
    for by in range(1, 4):
        x_copy(by).wait_send()
    for n in range(3):
        y_copy(n).wait_send()
    own_copy().wait()
    across = (other_core + 2) % 4
    from_core = ((y, across), (1 - y, other_core), (1 - y, across), (y, other_core))
    for n in range(4):
        c_copy(n).wait_send()
        here = rows_of(*from_core[n])
        pltpu.make_async_copy(here, here, c_recv.at[n]).wait()


def on_device(queries, keys, values, segments, owners):
    whole = pl.BlockSpec(memory_space=pl.ANY)
    attended, cache = pl.pallas_call(
        kernel,
        out_shape=(
            jax.ShapeDtypeStruct((TOK, HEADS * SIZE), BF16),
            jax.ShapeDtypeStruct((4, 2, 64, 2048), BF16),
        ),
        in_specs=[whole] * 5,
        out_specs=(pl.BlockSpec(memory_space=pltpu.VMEM), whole),
        scratch_shapes=[
            pltpu.VMEM((HEADS, TOK, 2 * SIZE), BF16),
            pltpu.VMEM((TOK, 2 * SIZE), BF16),
            pltpu.VMEM((TOK, 2 * SIZE), BF16),
            pltpu.VMEM((1, TOK), jnp.int32),
            pltpu.VMEM((1, TOK), jnp.int32),
            pltpu.VMEM((2, REACH + 1, ALL_ROWS, TOK), BF16),
            pltpu.VMEM((TOK, TOK), F32),
            pltpu.VMEM((HEADS, TOK, SIZE), F32),
            pltpu.VMEM((HEADS, TOK, SIZE), F32),
            pltpu.VMEM((HEADS, TOK, SIZE), F32),
            pltpu.VMEM((TOK, STEP * TOK), F32),
            pltpu.VMEM((TOK, STEP * TOK), F32),
            pltpu.VMEM((TOK, STEP * TOK), BF16),
            pltpu.VMEM((TOK, STEP * TOK), BF16),
            pltpu.VMEM((TOK, SIZE), F32),
            pltpu.VMEM((TOK, SIZE), F32),
            pltpu.VMEM((4, 2, 8, 2 * SLOT, 2 * SIZE), BF16),
            pltpu.VMEM((8, 4, 2, 2 * SLOT, 2 * SIZE), BF16),
            pltpu.VMEM((4, 8, 2, 2 * SLOT, 2 * SIZE), BF16),
            pltpu.VMEM((2, 4, 64, 4 * SIZE), BF16),
            pltpu.SemaphoreType.DMA((4,)),
            pltpu.SemaphoreType.DMA((HEADS,)),
            pltpu.SemaphoreType.DMA((8, REACH + 1)),
            pltpu.SemaphoreType.DMA((2, REACH + 1)),
            pltpu.SemaphoreType.DMA((8,)),
            pltpu.SemaphoreType.DMA((8,)),
            pltpu.SemaphoreType.DMA((4,)),
            pltpu.SemaphoreType.DMA((4,)),
            pltpu.SemaphoreType.DMA((3,)),
            pltpu.SemaphoreType.DMA((3,)),
            pltpu.SemaphoreType.DMA((4,)),
            pltpu.SemaphoreType.DMA((4,)),
            pltpu.SemaphoreType.DMA(()),
        ],
        compiler_params=pltpu.CompilerParams(
            collective_id=0, has_side_effects=True, vmem_limit_bytes=56 * 1024 * 1024
        ),
        cost_estimate=pl.CostEstimate(flops=12_000_000_000, bytes_accessed=6_000_000, transcendentals=22_000_000),
        name="attend_and_send",
    )(queries, keys, values, segments.reshape(1, TOK), owners.reshape(1, TOK))
    return attended, cache.reshape(64 * SLOT, 2048)


def solution(mesh):
    return jax.shard_map(
        on_device,
        mesh=mesh,
        in_specs=(
            P("inst", "head"),
            P("inst", "head"),
            P("inst", "head"),
            P("inst"),
            P("inst", None),
        ),
        out_specs=(P("inst", "head"), P("inst", None)),
        check_vma=False,
    )
```

```python
import functools

import jax
import jax.numpy as jnp
from jax import lax
from jax.experimental import pallas as pl
from jax.experimental.pallas import tpu as pltpu
from jax.sharding import PartitionSpec as P

MESH = pl.DeviceIdType.MESH
F32, BF16 = jnp.float32, jnp.bfloat16

HEADS, SIZE, RATIO = 16, 128, 8
TOK = 256
REACH = 20
SLOT = 8
STEP = 4
KEY_ROW, MASK_ROW, SENT_ROWS, ALL_ROWS = 128, 256, 272, 384
FAR = 1024.0
ROWS = 16
TO_LOG2 = SIZE ** -0.5 * 1.4426950408889634

ARRIVALS = (
    ((16, 215, 308, 109, 214, 307, 101, 206, 102, 213, 17, 305, 18, 310, 212, 311, 204, 103, 20, 19),
     (16, 308, 109, 215, 301, 110, 214, 17, 307, 102, 213, 306, 205, 103, 18, 112, 19, 304, 211, 20)),
    ((16, 101, 308, 215, 117, 307, 214, 110, 213, 309, 102, 103, 305, 212, 18, 19, 306, 211, 204, 20),
     (101, 16, 17, 308, 215, 110, 309, 214, 302, 111, 206, 18, 307, 212, 305, 213, 103, 104, 19, 120)),
    ((16, 101, 308, 215, 17, 307, 214, 102, 109, 18, 306, 213, 111, 310, 212, 103, 305, 104, 19, 20),
     (101, 16, 17, 308, 215, 102, 18, 307, 214, 213, 111, 309, 306, 212, 103, 305, 19, 210, 104, 120)),
    ((16, 101, 308, 215, 17, 102, 307, 214, 18, 103, 309, 213, 110, 19, 205, 112, 311, 206, 104, 120),
     (101, 16, 17, 308, 215, 102, 309, 214, 18, 103, 306, 213, 19, 310, 212, 311, 104, 305, 207, 20)),
    ((16, 101, 308, 215, 17, 102, 307, 214, 18, 309, 103, 306, 204, 310, 19, 20, 311, 213, 205, 212),
     (101, 16, 215, 17, 308, 102, 309, 214, 18, 103, 213, 19, 104, 207, 110, 20, 306, 111, 312, 205)),
    ((101, 16, 17, 215, 308, 307, 102, 205, 309, 18, 103, 214, 306, 19, 104, 213, 110, 20, 212, 311),
     (16, 101, 215, 308, 102, 17, 214, 18, 103, 205, 309, 19, 104, 213, 307, 311, 20, 206, 310, 112)),
    ((101, 16, 308, 17, 206, 102, 18, 309, 215, 307, 103, 310, 214, 19, 104, 213, 311, 212, 20, 105),
     (16, 101, 215, 308, 17, 307, 206, 102, 103, 18, 214, 19, 104, 310, 209, 311, 20, 105, 312, 213)),
    ((207, 16, 101, 308, 102, 17, 309, 18, 215, 103, 214, 19, 213, 306, 104, 310, 212, 311, 20, 105),
     (16, 101, 207, 308, 17, 215, 102, 309, 18, 310, 103, 306, 104, 19, 214, 20, 105, 213, 311, 212)),
    ((308, 16, 215, 101, 207, 317, 102, 213, 103, 18, 309, 314, 19, 206, 310, 212, 104, 205, 111, 20),
     (16, 308, 109, 207, 317, 102, 215, 318, 214, 206, 103, 101, 19, 212, 310, 104, 311, 20, 313, 205)),
    ((16, 308, 101, 215, 109, 17, 214, 102, 207, 213, 318, 103, 104, 19, 206, 310, 20, 311, 212, 205),
     (308, 101, 16, 17, 309, 215, 110, 207, 318, 103, 213, 319, 206, 314, 104, 212, 102, 20, 311, 105)),
    ((16, 101, 308, 215, 17, 309, 214, 102, 207, 110, 18, 103, 213, 319, 206, 104, 212, 105, 320, 311),
     (308, 16, 101, 309, 215, 102, 17, 18, 310, 214, 111, 207, 213, 319, 104, 320, 212, 105, 206, 103)),
    ((16, 308, 101, 215, 102, 17, 309, 18, 207, 310, 214, 103, 111, 213, 19, 206, 104, 212, 320, 105),
     (101, 16, 308, 17, 309, 215, 214, 102, 310, 103, 18, 19, 311, 207, 112, 213, 320, 105, 206, 204)),
    ((16, 308, 101, 215, 17, 309, 214, 102, 207, 103, 18, 310, 19, 213, 311, 104, 206, 312, 20, 205),
     (101, 16, 308, 215, 17, 309, 102, 18, 310, 207, 103, 311, 214, 104, 19, 20, 206, 112, 205, 113)),
    ((101, 16, 308, 215, 17, 309, 207, 102, 214, 18, 310, 103, 313, 104, 19, 311, 206, 20, 205, 212),
     (16, 308, 101, 215, 102, 17, 309, 18, 310, 103, 214, 19, 207, 313, 206, 104, 311, 105, 20, 312)),
    ((16, 308, 101, 309, 215, 102, 17, 18, 314, 310, 207, 103, 206, 19, 213, 104, 311, 105, 20, 312),
     (308, 101, 16, 215, 17, 309, 206, 102, 207, 103, 18, 314, 19, 310, 104, 311, 213, 20, 312, 105)),
    ((308, 101, 16, 207, 17, 215, 309, 102, 310, 103, 214, 18, 19, 311, 220, 104, 312, 213, 105, 106),
     (16, 207, 308, 101, 309, 102, 17, 215, 18, 214, 310, 103, 104, 19, 311, 20, 312, 213, 105, 106)),
)


def offset_of(kind, link):
    y, z = divmod(kind, 8)
    return (16, 1 if z > 0 else -7, -1 if z < 7 else 7, 8 if y == 1 else -8)[link]


def target_of(kind, link):
    y, z = divmod(kind, 8)
    return (kind, y * 8 + (z + 1) % 8, y * 8 + (z + 7) % 8, (1 - y) * 8 + z)[link]


def forward_table():
    table = []
    for kind in range(16):
        halves = []
        for half in range(2):
            held = [0] + [a % 100 for a in ARRIVALS[kind][half]]
            rows = []
            for distance in held:
                row = []
                for link in range(4):
                    there = target_of(kind, link)
                    far = distance + offset_of(there, link)
                    order = ARRIVALS[there][half]
                    wanted = link * 100 + far
                    row.append(order.index(wanted) + 1 if 1 <= far <= REACH and wanted in order else 0)
                rows.append(row)
            halves.append(rows)
        table.append(halves)
    return table


TABLE = forward_table()


def kernel(q_hbm, k_hbm, v_hbm, seg_hbm, own_hbm, out_ref, cache_ref,
           q_aug, k_own, v_own, seg_ref, own_ref, kv, bias, top, total, acc, scores_a, scores_b, weights_a, weights_b, shrink_a, shrink_b,
           outgoing, mid, recv, block,
           in_sem, q_sem, kv_send, kv_recv, z_send, z_recv, x_send, x_recv, y_send, y_recv, c_send, c_recv, own_sem):
    me, g = lax.axis_index("inst"), lax.axis_index("head")
    kind = me % 16
    x, y, z = me // 16, (me // 8) % 2, me % 8
    other_y = x * 16 + (1 - y) * 8 + z
    other_chip, other_core = (g + 2) % 4, g + 1 - 2 * (g % 2)
    near = (
        ((x + 1) % 4) * 16 + kind,
        me - z + (z + 1) % 8,
        me - z + (z + 7) % 8,
        other_y,
    )

    inputs = [
        pltpu.make_async_copy(src, dst, in_sem.at[n])
        for n, (src, dst) in enumerate(((k_hbm, k_own), (v_hbm, v_own), (seg_hbm, seg_ref), (own_hbm, own_ref)))
    ]
    queries = [
        pltpu.make_async_copy(q_hbm.at[:, h * SIZE:(h + 1) * SIZE], q_aug.at[h, :, 0:SIZE], q_sem.at[h]) for h in range(HEADS)
    ]
    for copy in inputs + queries:
        copy.start()

    def along_z(by):
        return (me - z + (z + by) % 8, g)

    def along_x(by):
        return (((x + by) % 4) * 16 + kind, g)

    beside = ((me, other_chip), (other_y, g), (other_y, other_chip))
    sibling = (me, other_core)
    barrier = pltpu.get_barrier_semaphore()
    partners = [along_z(by) for by in range(1, 8)] + [along_x(by) for by in range(1, 4)] + list(beside) + [sibling]
    for partner in partners:
        pl.semaphore_signal(barrier, inc=1, device_id=partner, device_id_type=MESH)

    def pick(values):
        chosen = jnp.int32(values[0])
        if len(set(values)) == 1:
            return chosen
        for t in range(1, 16):
            chosen = jnp.where(kind == t, jnp.int32(values[t]), chosen)
        return chosen

    first = [[pick([TABLE[t][half][0][link] for t in range(16)]) for link in range(4)] for half in range(2)]
    codes = [
        [
            [pick([sum(TABLE[t][half][STEP * k + jj + 1][link] * 64 ** k for k in range(5)) for t in range(16)]) for link in range(4)]
            for jj in range(STEP)
        ]
        for half in range(2)
    ]

    def digits(half, jj, k):
        return [(codes[half][jj][link] >> (6 * k)) & 63 for link in range(4)]

    def forward(half, slot, theres, wait=False):
        for link in range(4):
            there = theres[link]

            @pl.when(there > 0)
            def _():
                copy = pltpu.make_async_remote_copy(
                    src_ref=kv.at[half, slot, 0:SENT_ROWS],
                    dst_ref=kv.at[half, there, 0:SENT_ROWS],
                    send_sem=kv_send.at[half * 4 + link, slot],
                    recv_sem=kv_recv.at[half, there],
                    device_id=(near[link], g),
                    device_id_type=MESH,
                )
                if wait:
                    copy.wait_send()
                else:
                    copy.start()

    def arrive(k, h, j):
        half, jj = j % 2, 2 * h + j // 2
        slot = STEP * k + jj + 1
        here = kv.at[half, slot, 0:SENT_ROWS]
        pltpu.make_async_copy(here, here, kv_recv.at[half, slot]).wait()
        forward(half, slot, digits(half, jj, k))

    for copy in inputs[:3]:
        copy.wait()
    seg_row = seg_ref[...].astype(F32)
    seg_wide = jnp.broadcast_to(seg_row, (TOK, TOK))
    request = lax.broadcasted_iota(jnp.int32, (16, TOK), 0).astype(F32)
    for half in range(2):
        feat = slice(half * SIZE, (half + 1) * SIZE)
        kv[half, 0, 0:KEY_ROW, 0:SIZE] = v_own[0:SIZE, feat]
        kv[half, 0, 0:KEY_ROW, SIZE:TOK] = v_own[SIZE:TOK, feat]
        kv[half, 0, KEY_ROW:MASK_ROW, :] = k_own[:, feat].astype(F32).T.astype(BF16)
        kv[half, 0, MASK_ROW:SENT_ROWS, :] = jnp.where(seg_wide[0:16] == request, 0.0, -FAR).astype(BF16)
    pl.semaphore_wait(barrier, len(partners))
    forward(0, 0, first[0])
    forward(1, 0, first[1])

    def clear(slot, carry):
        for half in range(2):
            kv[half, slot, SENT_ROWS:ALL_ROWS, :] = jnp.zeros((ALL_ROWS - SENT_ROWS, TOK), BF16)
        return carry

    lax.fori_loop(0, REACH + 1, clear, 0)

    inputs[3].wait()
    dest = own_ref[...]
    owner = lax.broadcasted_iota(jnp.int32, (64, TOK), 0)
    hot = (owner == dest).astype(F32)
    before = (lax.broadcasted_iota(jnp.int32, (TOK, TOK), 0) < lax.broadcasted_iota(jnp.int32, (TOK, TOK), 1)).astype(BF16)
    count = jnp.dot(hot.astype(BF16), before, preferred_element_type=F32)
    place = jnp.sum(hot * count, axis=0, keepdims=True).astype(jnp.int32)
    target = dest * (2 * SLOT) + place
    row = lax.broadcasted_iota(jnp.int32, (1024, TOK), 0)
    of_keys = (row == target).astype(BF16)
    of_values = (row == target + SLOT).astype(BF16)
    rows = jnp.dot(of_keys, k_own[...], preferred_element_type=F32)
    rows += jnp.dot(of_values, v_own[...], preferred_element_type=F32)
    outgoing[...] = rows.astype(BF16).reshape(4, 2, 8, 2 * SLOT, 2 * SIZE)

    def z_copy(by):
        return pltpu.make_async_remote_copy(
            src_ref=outgoing.at[:, :, (z + by) % 8], dst_ref=mid.at[z], send_sem=z_send.at[by], recv_sem=z_recv.at[z],
            device_id=along_z(by), device_id_type=MESH)

    def x_copy(by):
        return pltpu.make_async_remote_copy(
            src_ref=mid.at[:, (x + by) % 4], dst_ref=recv.at[x], send_sem=x_send.at[by], recv_sem=x_recv.at[x],
            device_id=along_x(by), device_id_type=MESH)

    def rows_of(source_y, group):
        return cache_ref.at[:, source_y, :, pl.ds(pl.multiple_of(group * 512, 512), 512)]

    def y_copy(n):
        return pltpu.make_async_remote_copy(
            src_ref=block.at[y if n == 0 else 1 - y], dst_ref=rows_of(y, g), send_sem=y_send.at[n], recv_sem=y_recv.at[n],
            device_id=beside[n], device_id_type=MESH)

    from_y = ((y, other_chip), (1 - y, g), (1 - y, other_chip))

    def c_copy(n):
        if n == 3:
            src, place = block.at[y], rows_of(y, g)
        else:
            src = place = rows_of(*from_y[n])
        return pltpu.make_async_remote_copy(
            src_ref=src, dst_ref=place, send_sem=c_send.at[n], recv_sem=c_recv.at[n],
            device_id=sibling, device_id_type=MESH)

    def own_copy():
        return pltpu.make_async_copy(block.at[y], rows_of(y, g), own_sem)

    def first_leg():
        for by in (1, 7, 2, 6, 3, 5, 4):
            z_copy(by).start()
        for i in range(4):
            for j in range(2):
                mid[z, i, j] = outgoing[i, j, z]

    def second_leg():
        for by in range(1, 8):
            src = (z + 8 - by) % 8
            pltpu.make_async_copy(mid.at[src], mid.at[src], z_recv.at[src]).wait()
        for by in (1, 3, 2):
            x_copy(by).start()
        for i in range(8):
            recv[x, i] = mid[i, x]

    def third_leg():
        for by in range(1, 4):
            src = (x + 4 - by) % 4
            pltpu.make_async_copy(recv.at[src], recv.at[src], x_recv.at[src]).wait()
        a = lax.broadcasted_iota(jnp.int32, (64, 128), 0)
        b = lax.broadcasted_iota(jnp.int32, (64, 128), 1)
        key_rows = (b == 2 * a - (a & 7)).astype(BF16)
        value_rows = (b == 2 * a - (a & 7) + 8).astype(BF16)
        for src in range(4):
            for j in range(2):
                arrived = recv[src, :, j].reshape(128, 2 * SIZE)
                block[j, src, :, 0:256] = jnp.dot(key_rows, arrived, preferred_element_type=F32).astype(BF16)
                block[j, src, :, 256:512] = jnp.dot(value_rows, arrived, preferred_element_type=F32).astype(BF16)
        for n in range(3):
            y_copy(n).start()
        c_copy(3).start()
        own_copy().start()

    def fourth_leg():
        for n in range(3):
            here = rows_of(*from_y[n])
            pltpu.make_async_copy(here, here, y_recv.at[n]).wait()
            c_copy(n).start()

    at0 = lax.broadcasted_iota(jnp.int32, (TOK, TOK), 0)
    at1 = lax.broadcasted_iota(jnp.int32, (TOK, TOK), 1)
    seg_col = jnp.sum(jnp.where(at0 == at1, seg_wide, 0.0), axis=1, keepdims=True)
    lane = lax.broadcasted_iota(jnp.int32, (TOK, SIZE), 1).astype(F32)
    query_mask = jnp.where(lane == seg_col, FAR, 0.0).astype(BF16)
    for h in range(HEADS):
        q_aug[h, :, SIZE:2 * SIZE] = query_mask
    bias[...] = jnp.where(at0 >= at1, 0.0, -1e30)
    scores_of, weights_of, shrink_of = (scores_a, scores_b), (weights_a, weights_b), (shrink_a, shrink_b)

    def unit(half, slots, diagonal):
        width = len(slots) * TOK

        def score(i, c):
            scores_of[i % 2][:, c * TOK:(c + 1) * TOK] = jnp.dot(
                q_aug[half * RATIO + i], kv[half, slots[c], KEY_ROW:ALL_ROWS, :], preferred_element_type=F32)

        def soften(i, at):
            h, rows = half * RATIO + i, slice(at, at + ROWS)
            parts = [scores_of[i % 2][rows, j:j + SIZE] for j in range(0, width, SIZE)]
            if diagonal:
                parts = [part + bias[rows, n * SIZE:(n + 1) * SIZE] for n, part in enumerate(parts)]
            largest = jnp.max(functools.reduce(jnp.maximum, parts), axis=1, keepdims=True)
            if diagonal:
                peak = jnp.broadcast_to(largest, (ROWS, SIZE))
            else:
                old = top[h, rows, :]
                peak = jnp.maximum(old, largest)
                shrink = jnp.exp2((old - peak) * TO_LOG2)
                shrink_of[i % 2][rows, :] = shrink
            weights = [jnp.exp2((part - peak) * TO_LOG2) for part in parts]
            for n, weight in enumerate(weights):
                weights_of[i % 2][rows, n * SIZE:(n + 1) * SIZE] = weight.astype(BF16)
            added = functools.reduce(jnp.add, weights)
            top[h, rows, :] = peak
            total[h, rows, :] = added if diagonal else total[h, rows, :] * shrink + added

        def combine(i):
            h = half * RATIO + i
            values = jnp.concatenate(
                [kv[half, slot, 0:KEY_ROW, lanes:lanes + SIZE] for slot in slots for lanes in (0, SIZE)], axis=0)
            product = jnp.dot(weights_of[i % 2][:, 0:width], values, preferred_element_type=F32)
            acc[h] = product if diagonal else acc[h] * shrink_of[i % 2][...] + product

        for c in range(len(slots)):
            score(0, c)
        for i in range(RATIO):
            for quarter in range(4):
                if i + 1 < RATIO and quarter < len(slots):
                    score(i + 1, quarter)
                for at in range(quarter * 64, quarter * 64 + 64, ROWS):
                    soften(i, at)
                if quarter == 1 and i > 0:
                    combine(i - 1)
        combine(RATIO - 1)

    for copy in queries:
        copy.wait()
    for half in range(2):
        unit(half, [0], True)
        for j in range(4):
            arrive(0, half, j)
        if half == 0:
            first_leg()

    def step(k, carry):
        for half in range(2):
            unit(half, [STEP * k + 1 + c for c in range(STEP)], False)

            @pl.when(k < 4)
            def _():
                for j in range(4):
                    arrive(k + 1, half, j)

            @pl.when(k == (3, 1)[half])
            def _():
                (third_leg, second_leg)[half]()

        return carry

    lax.fori_loop(0, 5, step, 0)
    fourth_leg()

    for h in range(HEADS):
        denominator = jnp.sum(total[h], axis=1, keepdims=True)
        out_ref[:, h * SIZE:(h + 1) * SIZE] = (acc[h] / denominator).astype(BF16)

    for half in range(2):
        forward(half, 0, first[half], wait=True)

    def drain(k, carry):
        for half in range(2):
            for jj in range(STEP):
                forward(half, STEP * k + jj + 1, digits(half, jj, k), wait=True)
        return carry

    lax.fori_loop(0, 5, drain, 0)
    for by in range(1, 8):
        z_copy(by).wait_send()
    for by in range(1, 4):
        x_copy(by).wait_send()
    for n in range(3):
        y_copy(n).wait_send()
    own_copy().wait()
    across = (other_core + 2) % 4
    from_core = ((y, across), (1 - y, other_core), (1 - y, across), (y, other_core))
    for n in range(4):
        c_copy(n).wait_send()
        here = rows_of(*from_core[n])
        pltpu.make_async_copy(here, here, c_recv.at[n]).wait()


def on_device(queries, keys, values, segments, owners):
    whole = pl.BlockSpec(memory_space=pl.ANY)
    attended, cache = pl.pallas_call(
        kernel,
        out_shape=(
            jax.ShapeDtypeStruct((TOK, HEADS * SIZE), BF16),
            jax.ShapeDtypeStruct((4, 2, 64, 2048), BF16),
        ),
        in_specs=[whole] * 5,
        out_specs=(pl.BlockSpec(memory_space=pltpu.VMEM), whole),
        scratch_shapes=[
            pltpu.VMEM((HEADS, TOK, 2 * SIZE), BF16),
            pltpu.VMEM((TOK, 2 * SIZE), BF16),
            pltpu.VMEM((TOK, 2 * SIZE), BF16),
            pltpu.VMEM((1, TOK), jnp.int32),
            pltpu.VMEM((1, TOK), jnp.int32),
            pltpu.VMEM((2, REACH + 1, ALL_ROWS, TOK), BF16),
            pltpu.VMEM((TOK, TOK), F32),
            pltpu.VMEM((HEADS, TOK, SIZE), F32),
            pltpu.VMEM((HEADS, TOK, SIZE), F32),
            pltpu.VMEM((HEADS, TOK, SIZE), F32),
            pltpu.VMEM((TOK, STEP * TOK), F32),
            pltpu.VMEM((TOK, STEP * TOK), F32),
            pltpu.VMEM((TOK, STEP * TOK), BF16),
            pltpu.VMEM((TOK, STEP * TOK), BF16),
            pltpu.VMEM((TOK, SIZE), F32),
            pltpu.VMEM((TOK, SIZE), F32),
            pltpu.VMEM((4, 2, 8, 2 * SLOT, 2 * SIZE), BF16),
            pltpu.VMEM((8, 4, 2, 2 * SLOT, 2 * SIZE), BF16),
            pltpu.VMEM((4, 8, 2, 2 * SLOT, 2 * SIZE), BF16),
            pltpu.VMEM((2, 4, 64, 4 * SIZE), BF16),
            pltpu.SemaphoreType.DMA((4,)),
            pltpu.SemaphoreType.DMA((HEADS,)),
            pltpu.SemaphoreType.DMA((8, REACH + 1)),
            pltpu.SemaphoreType.DMA((2, REACH + 1)),
            pltpu.SemaphoreType.DMA((8,)),
            pltpu.SemaphoreType.DMA((8,)),
            pltpu.SemaphoreType.DMA((4,)),
            pltpu.SemaphoreType.DMA((4,)),
            pltpu.SemaphoreType.DMA((3,)),
            pltpu.SemaphoreType.DMA((3,)),
            pltpu.SemaphoreType.DMA((4,)),
            pltpu.SemaphoreType.DMA((4,)),
            pltpu.SemaphoreType.DMA(()),
        ],
        compiler_params=pltpu.CompilerParams(
            collective_id=0, has_side_effects=True, vmem_limit_bytes=56 * 1024 * 1024
        ),
        cost_estimate=pl.CostEstimate(flops=12_000_000_000, bytes_accessed=6_000_000, transcendentals=22_000_000),
        name="attend_and_send",
    )(queries, keys, values, segments.reshape(1, TOK), owners.reshape(1, TOK))
    return attended, cache.reshape(64 * SLOT, 2048)


def solution(mesh):
    return jax.shard_map(
        on_device,
        mesh=mesh,
        in_specs=(
            P("inst", "head"),
            P("inst", "head"),
            P("inst", "head"),
            P("inst"),
            P("inst", None),
        ),
        out_specs=(P("inst", "head"), P("inst", None)),
        check_vma=False,
    )
```

```python
import functools

import jax
import jax.numpy as jnp
from jax import lax
from jax.experimental import pallas as pl
from jax.experimental.pallas import tpu as pltpu
from jax.sharding import PartitionSpec as P

MESH = pl.DeviceIdType.MESH
F32, BF16 = jnp.float32, jnp.bfloat16

HEADS, SIZE, RATIO = 16, 128, 8
TOK = 256
REACH = 20
SLOT = 8
STEP = 4
KEY_ROW, ALL_ROWS = SIZE + 16, 2 * SIZE + 16
HIDDEN = 1e30
TO_LOG2 = SIZE ** -0.5 * 1.4426950408889634

ARRIVALS = (
    ((16, 215, 308, 109, 214, 307, 101, 206, 102, 213, 17, 305, 18, 310, 212, 311, 204, 103, 20, 19),
     (16, 308, 109, 215, 301, 110, 214, 17, 307, 102, 213, 306, 205, 103, 18, 112, 19, 304, 211, 20)),
    ((16, 101, 308, 215, 117, 307, 214, 110, 213, 309, 102, 103, 305, 212, 18, 19, 306, 211, 204, 20),
     (101, 16, 17, 308, 215, 110, 309, 214, 302, 111, 206, 18, 307, 212, 305, 213, 103, 104, 19, 120)),
    ((16, 101, 308, 215, 17, 307, 214, 102, 109, 18, 306, 213, 111, 310, 212, 103, 305, 104, 19, 20),
     (101, 16, 17, 308, 215, 102, 18, 307, 214, 213, 111, 309, 306, 212, 103, 305, 19, 210, 104, 120)),
    ((16, 101, 308, 215, 17, 102, 307, 214, 18, 103, 309, 213, 110, 19, 205, 112, 311, 206, 104, 120),
     (101, 16, 17, 308, 215, 102, 309, 214, 18, 103, 306, 213, 19, 310, 212, 311, 104, 305, 207, 20)),
    ((16, 101, 308, 215, 17, 102, 307, 214, 18, 309, 103, 306, 204, 310, 19, 20, 311, 213, 205, 212),
     (101, 16, 215, 17, 308, 102, 309, 214, 18, 103, 213, 19, 104, 207, 110, 20, 306, 111, 312, 205)),
    ((101, 16, 17, 215, 308, 307, 102, 205, 309, 18, 103, 214, 306, 19, 104, 213, 110, 20, 212, 311),
     (16, 101, 215, 308, 102, 17, 214, 18, 103, 205, 309, 19, 104, 213, 307, 311, 20, 206, 310, 112)),
    ((101, 16, 308, 17, 206, 102, 18, 309, 215, 307, 103, 310, 214, 19, 104, 213, 311, 212, 20, 105),
     (16, 101, 215, 308, 17, 307, 206, 102, 103, 18, 214, 19, 104, 310, 209, 311, 20, 105, 312, 213)),
    ((207, 16, 101, 308, 102, 17, 309, 18, 215, 103, 214, 19, 213, 306, 104, 310, 212, 311, 20, 105),
     (16, 101, 207, 308, 17, 215, 102, 309, 18, 310, 103, 306, 104, 19, 214, 20, 105, 213, 311, 212)),
    ((308, 16, 215, 101, 207, 317, 102, 213, 103, 18, 309, 314, 19, 206, 310, 212, 104, 205, 111, 20),
     (16, 308, 109, 207, 317, 102, 215, 318, 214, 206, 103, 101, 19, 212, 310, 104, 311, 20, 313, 205)),
    ((16, 308, 101, 215, 109, 17, 214, 102, 207, 213, 318, 103, 104, 19, 206, 310, 20, 311, 212, 205),
     (308, 101, 16, 17, 309, 215, 110, 207, 318, 103, 213, 319, 206, 314, 104, 212, 102, 20, 311, 105)),
    ((16, 101, 308, 215, 17, 309, 214, 102, 207, 110, 18, 103, 213, 319, 206, 104, 212, 105, 320, 311),
     (308, 16, 101, 309, 215, 102, 17, 18, 310, 214, 111, 207, 213, 319, 104, 320, 212, 105, 206, 103)),
    ((16, 308, 101, 215, 102, 17, 309, 18, 207, 310, 214, 103, 111, 213, 19, 206, 104, 212, 320, 105),
     (101, 16, 308, 17, 309, 215, 214, 102, 310, 103, 18, 19, 311, 207, 112, 213, 320, 105, 206, 204)),
    ((16, 308, 101, 215, 17, 309, 214, 102, 207, 103, 18, 310, 19, 213, 311, 104, 206, 312, 20, 205),
     (101, 16, 308, 215, 17, 309, 102, 18, 310, 207, 103, 311, 214, 104, 19, 20, 206, 112, 205, 113)),
    ((101, 16, 308, 215, 17, 309, 207, 102, 214, 18, 310, 103, 313, 104, 19, 311, 206, 20, 205, 212),
     (16, 308, 101, 215, 102, 17, 309, 18, 310, 103, 214, 19, 207, 313, 206, 104, 311, 105, 20, 312)),
    ((16, 308, 101, 309, 215, 102, 17, 18, 314, 310, 207, 103, 206, 19, 213, 104, 311, 105, 20, 312),
     (308, 101, 16, 215, 17, 309, 206, 102, 207, 103, 18, 314, 19, 310, 104, 311, 213, 20, 312, 105)),
    ((308, 101, 16, 207, 17, 215, 309, 102, 310, 103, 214, 18, 19, 311, 220, 104, 312, 213, 105, 106),
     (16, 207, 308, 101, 309, 102, 17, 215, 18, 214, 310, 103, 104, 19, 311, 20, 312, 213, 105, 106)),
)


def offset_of(kind, link):
    y, z = divmod(kind, 8)
    return (16, 1 if z > 0 else -7, -1 if z < 7 else 7, 8 if y == 1 else -8)[link]


def target_of(kind, link):
    y, z = divmod(kind, 8)
    return (kind, y * 8 + (z + 1) % 8, y * 8 + (z + 7) % 8, (1 - y) * 8 + z)[link]


def forward_table():
    table = []
    for kind in range(16):
        halves = []
        for half in range(2):
            held = [0] + [a % 100 for a in ARRIVALS[kind][half]]
            rows = []
            for distance in held:
                row = []
                for link in range(4):
                    there = target_of(kind, link)
                    far = distance + offset_of(there, link)
                    order = ARRIVALS[there][half]
                    wanted = link * 100 + far
                    row.append(order.index(wanted) + 1 if 1 <= far <= REACH and wanted in order else 0)
                rows.append(row)
            halves.append(rows)
        table.append(halves)
    return table


TABLE = forward_table()


def kernel(q_hbm, k_hbm, v_hbm, seg_hbm, own_hbm, out_ref, cache_ref,
           q_own, q_turned, k_own, v_own, own_values, seg_ref, own_ref, kv, bias, top, acc, scores_a, scores_b, weights_a, weights_b,
           peaks_a, peaks_b, shrink_a, shrink_b,
           outgoing, mid, recv, block,
           in_sem, kv_send, kv_recv, z_send, z_recv, x_send, x_recv, y_send, y_recv, c_send, c_recv, own_sem):
    me, g = lax.axis_index("inst"), lax.axis_index("head")
    kind = me % 16
    x, y, z = me // 16, (me // 8) % 2, me % 8
    other_y = x * 16 + (1 - y) * 8 + z
    other_chip, other_core = (g + 2) % 4, g + 1 - 2 * (g % 2)
    near = (
        ((x + 1) % 4) * 16 + kind,
        me - z + (z + 1) % 8,
        me - z + (z + 7) % 8,
        other_y,
    )

    inputs = [
        pltpu.make_async_copy(src, dst, in_sem.at[n])
        for n, (src, dst) in enumerate(
            ((k_hbm, k_own), (v_hbm, v_own), (seg_hbm, seg_ref), (own_hbm, own_ref), (q_hbm, q_own)))
    ]
    for copy in inputs:
        copy.start()

    def along_z(by):
        return (me - z + (z + by) % 8, g)

    def along_x(by):
        return (((x + by) % 4) * 16 + kind, g)

    beside = ((me, other_chip), (other_y, g), (other_y, other_chip))
    sibling = (me, other_core)
    barrier = pltpu.get_barrier_semaphore()
    partners = [along_z(by) for by in range(1, 8)] + [along_x(by) for by in range(1, 4)] + list(beside) + [sibling]
    for partner in partners:
        pl.semaphore_signal(barrier, inc=1, device_id=partner, device_id_type=MESH)

    def pick(values):
        chosen = jnp.int32(values[0])
        if len(set(values)) == 1:
            return chosen
        for t in range(1, 16):
            chosen = jnp.where(kind == t, jnp.int32(values[t]), chosen)
        return chosen

    first = [[pick([TABLE[t][half][0][link] for t in range(16)]) for link in range(4)] for half in range(2)]
    codes = [
        [
            [pick([sum(TABLE[t][half][STEP * k + jj + 1][link] * 64 ** k for k in range(5)) for t in range(16)]) for link in range(4)]
            for jj in range(STEP)
        ]
        for half in range(2)
    ]

    def digits(half, jj, k):
        return [(codes[half][jj][link] >> (6 * k)) & 63 for link in range(4)]

    def forward(half, slot, theres, wait=False):
        for link in range(4):
            there = theres[link]

            @pl.when(there > 0)
            def _():
                copy = pltpu.make_async_remote_copy(
                    src_ref=kv.at[half, slot],
                    dst_ref=kv.at[half, there],
                    send_sem=kv_send.at[half * 4 + link, slot],
                    recv_sem=kv_recv.at[half, there],
                    device_id=(near[link], g),
                    device_id_type=MESH,
                )
                if wait:
                    copy.wait_send()
                else:
                    copy.start()

    def arrive(k, h, j):
        half, jj = j % 2, 2 * h + j // 2
        slot = STEP * k + jj + 1
        here = kv.at[half, slot]
        pltpu.make_async_copy(here, here, kv_recv.at[half, slot]).wait()
        forward(half, slot, digits(half, jj, k))

    for copy in inputs[:3]:
        copy.wait()
    at0 = lax.broadcasted_iota(jnp.int32, (TOK, TOK), 0)
    at1 = lax.broadcasted_iota(jnp.int32, (TOK, TOK), 1)
    seg_row = seg_ref[...].astype(F32)
    seg_wide = jnp.broadcast_to(seg_row, (TOK, TOK))
    seg_tall = jnp.broadcast_to(jnp.sum(jnp.where(at0 == at1, seg_wide, 0.0), axis=1, keepdims=True), (TOK, TOK))
    first_seg, last_seg = jnp.min(seg_tall, axis=0, keepdims=True), jnp.max(seg_tall, axis=0, keepdims=True)
    reaches = (seg_row == last_seg).astype(F32)
    extra = lax.broadcasted_iota(jnp.int32, (16, TOK), 0)
    extra_rows = jnp.where(extra == 0, reaches, jnp.where(extra == 1, last_seg, 0.0)).astype(BF16)
    for half in range(2):
        feat = slice(half * SIZE, (half + 1) * SIZE)
        turned = v_own[:, feat].astype(F32).T
        own_values[half, 0:SIZE, :] = turned.astype(BF16)
        own_values[half, SIZE:KEY_ROW, :] = jnp.where(extra == 0, 1.0, 0.0).astype(BF16)
        kv[half, 0, 0:SIZE, :] = (turned * reaches).astype(BF16)
        kv[half, 0, SIZE:KEY_ROW, :] = extra_rows
        keys = k_own[:, feat].astype(F32)
        last_key = jnp.broadcast_to(keys[TOK - 1:TOK, :], (TOK, SIZE))
        keys = jnp.where(seg_tall[:, 0:SIZE] == last_seg[:, 0:SIZE], keys, last_key).astype(BF16)
        kv[half, 0, KEY_ROW:ALL_ROWS, 0:SIZE] = keys[0:SIZE]
        kv[half, 0, KEY_ROW:ALL_ROWS, SIZE:TOK] = keys[SIZE:TOK]
    inputs[4].wait()
    for h in range(HEADS):
        q_turned[h] = q_own[:, h * SIZE:(h + 1) * SIZE].astype(F32).T.astype(BF16)
    bias[...] = jnp.where((at0 <= at1) & (seg_tall == seg_wide), 0.0, -HIDDEN)
    pl.semaphore_wait(barrier, len(partners))
    forward(0, 0, first[0])
    forward(1, 0, first[1])

    inputs[3].wait()
    dest = own_ref[...]
    owner = lax.broadcasted_iota(jnp.int32, (64, TOK), 0)
    hot = (owner == dest).astype(F32)
    before = (lax.broadcasted_iota(jnp.int32, (TOK, TOK), 0) < lax.broadcasted_iota(jnp.int32, (TOK, TOK), 1)).astype(BF16)
    count = jnp.dot(hot.astype(BF16), before, preferred_element_type=F32)
    place = jnp.sum(hot * count, axis=0, keepdims=True).astype(jnp.int32)
    target = dest * (2 * SLOT) + place
    row = lax.broadcasted_iota(jnp.int32, (1024, TOK), 0)
    of_keys = (row == target).astype(BF16)
    of_values = (row == target + SLOT).astype(BF16)
    rows = jnp.dot(of_keys, k_own[...], preferred_element_type=F32)
    rows += jnp.dot(of_values, v_own[...], preferred_element_type=F32)
    outgoing[...] = rows.astype(BF16).reshape(4, 2, 8, 2 * SLOT, 2 * SIZE)

    def z_copy(by):
        return pltpu.make_async_remote_copy(
            src_ref=outgoing.at[:, :, (z + by) % 8], dst_ref=mid.at[z], send_sem=z_send.at[by], recv_sem=z_recv.at[z],
            device_id=along_z(by), device_id_type=MESH)

    def x_copy(by):
        return pltpu.make_async_remote_copy(
            src_ref=mid.at[:, (x + by) % 4], dst_ref=recv.at[x], send_sem=x_send.at[by], recv_sem=x_recv.at[x],
            device_id=along_x(by), device_id_type=MESH)

    def rows_of(source_y, group):
        return cache_ref.at[:, source_y, :, pl.ds(pl.multiple_of(group * 512, 512), 512)]

    def y_copy(n):
        return pltpu.make_async_remote_copy(
            src_ref=block.at[y if n == 0 else 1 - y], dst_ref=rows_of(y, g), send_sem=y_send.at[n], recv_sem=y_recv.at[n],
            device_id=beside[n], device_id_type=MESH)

    from_y = ((y, other_chip), (1 - y, g), (1 - y, other_chip))

    def c_copy(n):
        if n == 3:
            src, place = block.at[y], rows_of(y, g)
        else:
            src = place = rows_of(*from_y[n])
        return pltpu.make_async_remote_copy(
            src_ref=src, dst_ref=place, send_sem=c_send.at[n], recv_sem=c_recv.at[n],
            device_id=sibling, device_id_type=MESH)

    def own_copy():
        return pltpu.make_async_copy(block.at[y], rows_of(y, g), own_sem)

    def first_leg():
        for by in (1, 7, 2, 6, 3, 5, 4):
            z_copy(by).start()
        for i in range(4):
            for j in range(2):
                mid[z, i, j] = outgoing[i, j, z]

    def second_leg():
        for by in range(1, 8):
            src = (z + 8 - by) % 8
            pltpu.make_async_copy(mid.at[src], mid.at[src], z_recv.at[src]).wait()
        for by in (1, 3, 2):
            x_copy(by).start()
        for i in range(8):
            recv[x, i] = mid[i, x]

    def third_leg():
        for by in range(1, 4):
            src = (x + 4 - by) % 4
            pltpu.make_async_copy(recv.at[src], recv.at[src], x_recv.at[src]).wait()
        a = lax.broadcasted_iota(jnp.int32, (64, 128), 0)
        b = lax.broadcasted_iota(jnp.int32, (64, 128), 1)
        key_rows = (b == 2 * a - (a & 7)).astype(BF16)
        value_rows = (b == 2 * a - (a & 7) + 8).astype(BF16)
        for src in range(4):
            for j in range(2):
                arrived = recv[src, :, j].reshape(128, 2 * SIZE)
                block[j, src, :, 0:256] = jnp.dot(key_rows, arrived, preferred_element_type=F32).astype(BF16)
                block[j, src, :, 256:512] = jnp.dot(value_rows, arrived, preferred_element_type=F32).astype(BF16)
        for n in range(3):
            y_copy(n).start()
        c_copy(3).start()
        own_copy().start()

    def fourth_leg():
        for n in range(3):
            here = rows_of(*from_y[n])
            pltpu.make_async_copy(here, here, y_recv.at[n]).wait()
            c_copy(n).start()

    scores_of, weights_of = (scores_a, scores_b), (weights_a, weights_b)
    peaks_of, shrink_of = (peaks_a, peaks_b), (shrink_a, shrink_b)

    def score(n, h, slots):
        if slots is None:
            keys = k_own[:, (h // RATIO) * SIZE:(h // RATIO + 1) * SIZE]
        else:
            keys = jnp.concatenate(
                [kv[h // RATIO, slot, KEY_ROW:ALL_ROWS, lanes:lanes + SIZE] for slot in slots for lanes in (0, SIZE)], axis=0)
        product = jnp.dot(keys, q_turned[h], preferred_element_type=F32)
        if slots is None:
            product += bias[...]
        scores_of[n % 2][0:product.shape[0], :] = product
        for c in range(product.shape[0] // TOK):
            peaks_of[n % 2][c] = jnp.max(product[c * TOK:(c + 1) * TOK], axis=0, keepdims=True)

    def peak_rows(n, h, slots):
        if slots is None:
            top[h] = peaks_of[n % 2][0]
            return [top[h]]
        seen = []
        for slot in slots:
            block_seg = kv[h // RATIO, slot, SIZE:KEY_ROW, :].astype(F32)[1:2, :]
            seen.append((block_seg == first_seg) & (seg_row == first_seg))
        old = top[h]
        peak = old
        for c in range(len(slots)):
            peak = jnp.maximum(peak, jnp.where(seen[c], peaks_of[n % 2][c], -HIDDEN))
        top[h] = peak
        shrink_of[n % 2][...] = jnp.exp2((old - peak) * TO_LOG2)
        return [jnp.where(seen[c], peak, HIDDEN) for c in range(len(slots))]

    def soften(n, peaks, c, start, rows):
        at = slice(c * TOK + start, c * TOK + start + rows)
        weights_of[n % 2][at, :] = jnp.exp2((scores_of[n % 2][at, :] - peaks[c]) * TO_LOG2).astype(BF16)

    def combine(n, h, slots):
        if slots is None:
            acc[h] = jnp.dot(own_values[h // RATIO], weights_of[n % 2][0:TOK, :], preferred_element_type=F32)
        else:
            values = jnp.concatenate([kv[h // RATIO, slot, 0:KEY_ROW, :] for slot in slots], axis=1)
            product = jnp.dot(values, weights_of[n % 2][...], preferred_element_type=F32)
            acc[h] = acc[h] * shrink_of[n % 2][...] + product

    def turn(n, before, now, after):
        peaks = peak_rows(n, *now)
        if before is not None:
            combine(n - 1, *before)
        for c in range(len(peaks)):
            if after is not None and c == len(peaks) // 2:
                score(n + 1, *after)
            for start in range(0, TOK, 64):
                soften(n, peaks, c, start, 64)

    for half in range(2):
        heads = [(half * RATIO + i, None) for i in range(RATIO)]
        score(0, *heads[0])
        for n in range(RATIO):
            turn(n, heads[n - 1] if n > 0 else None, heads[n], heads[n + 1] if n + 1 < RATIO else None)
        combine(RATIO - 1, *heads[-1])
        for j in range(4):
            arrive(0, half, j)
        if half == 0:
            first_leg()

    def slots_of(k):
        return [STEP * k + 1 + c for c in range(STEP)]

    score(0, 0, slots_of(0))

    def step(k, carry):
        now = slots_of(k)
        turns = [(h, now) for h in range(HEADS)] + [(0, slots_of(jnp.minimum(k + 1, 4)))]
        for n in range(HEADS):
            turn(n, turns[n - 1] if n > 0 else None, turns[n], turns[n + 1])
            if n == HEADS - 1:
                combine(n, *turns[n])
            if n % 2 == 1:
                @pl.when(k < 4)
                def _():
                    arrive(k + 1, n // 8, (n // 2) % 4)
            if n % 8 == 7:
                @pl.when(k == (3, 1)[n // 8])
                def _():
                    (third_leg, second_leg)[n // 8]()
        return carry

    lax.fori_loop(0, 5, step, 0)
    fourth_leg()

    for h in range(HEADS):
        out_ref[:, h * SIZE:(h + 1) * SIZE] = (acc[h, 0:SIZE, :] / acc[h, SIZE:SIZE + 1, :]).T.astype(BF16)

    for half in range(2):
        forward(half, 0, first[half], wait=True)

    def drain(k, carry):
        for half in range(2):
            for jj in range(STEP):
                forward(half, STEP * k + jj + 1, digits(half, jj, k), wait=True)
        return carry

    lax.fori_loop(0, 5, drain, 0)
    for by in range(1, 8):
        z_copy(by).wait_send()
    for by in range(1, 4):
        x_copy(by).wait_send()
    for n in range(3):
        y_copy(n).wait_send()
    own_copy().wait()
    across = (other_core + 2) % 4
    from_core = ((y, across), (1 - y, other_core), (1 - y, across), (y, other_core))
    for n in range(4):
        c_copy(n).wait_send()
        here = rows_of(*from_core[n])
        pltpu.make_async_copy(here, here, c_recv.at[n]).wait()


def on_device(queries, keys, values, segments, owners):
    whole = pl.BlockSpec(memory_space=pl.ANY)
    attended, cache = pl.pallas_call(
        kernel,
        out_shape=(
            jax.ShapeDtypeStruct((TOK, HEADS * SIZE), BF16),
            jax.ShapeDtypeStruct((4, 2, 64, 2048), BF16),
        ),
        in_specs=[whole] * 5,
        out_specs=(pl.BlockSpec(memory_space=pltpu.VMEM), whole),
        scratch_shapes=[
            pltpu.VMEM((TOK, HEADS * SIZE), BF16),
            pltpu.VMEM((HEADS, SIZE, TOK), BF16),
            pltpu.VMEM((TOK, 2 * SIZE), BF16),
            pltpu.VMEM((TOK, 2 * SIZE), BF16),
            pltpu.VMEM((2, KEY_ROW, TOK), BF16),
            pltpu.VMEM((1, TOK), jnp.int32),
            pltpu.VMEM((1, TOK), jnp.int32),
            pltpu.VMEM((2, REACH + 1, ALL_ROWS, TOK), BF16),
            pltpu.VMEM((TOK, TOK), F32),
            pltpu.VMEM((HEADS, 1, TOK), F32),
            pltpu.VMEM((HEADS, KEY_ROW, TOK), F32),
            pltpu.VMEM((STEP * TOK, TOK), F32),
            pltpu.VMEM((STEP * TOK, TOK), F32),
            pltpu.VMEM((STEP * TOK, TOK), BF16),
            pltpu.VMEM((STEP * TOK, TOK), BF16),
            pltpu.VMEM((STEP, 1, TOK), F32),
            pltpu.VMEM((STEP, 1, TOK), F32),
            pltpu.VMEM((1, TOK), F32),
            pltpu.VMEM((1, TOK), F32),
            pltpu.VMEM((4, 2, 8, 2 * SLOT, 2 * SIZE), BF16),
            pltpu.VMEM((8, 4, 2, 2 * SLOT, 2 * SIZE), BF16),
            pltpu.VMEM((4, 8, 2, 2 * SLOT, 2 * SIZE), BF16),
            pltpu.VMEM((2, 4, 64, 4 * SIZE), BF16),
            pltpu.SemaphoreType.DMA((5,)),
            pltpu.SemaphoreType.DMA((8, REACH + 1)),
            pltpu.SemaphoreType.DMA((2, REACH + 1)),
            pltpu.SemaphoreType.DMA((8,)),
            pltpu.SemaphoreType.DMA((8,)),
            pltpu.SemaphoreType.DMA((4,)),
            pltpu.SemaphoreType.DMA((4,)),
            pltpu.SemaphoreType.DMA((3,)),
            pltpu.SemaphoreType.DMA((3,)),
            pltpu.SemaphoreType.DMA((4,)),
            pltpu.SemaphoreType.DMA((4,)),
            pltpu.SemaphoreType.DMA(()),
        ],
        compiler_params=pltpu.CompilerParams(
            collective_id=0, has_side_effects=True, vmem_limit_bytes=56 * 1024 * 1024
        ),
        cost_estimate=pl.CostEstimate(flops=12_000_000_000, bytes_accessed=6_000_000, transcendentals=22_000_000),
        name="attend_and_send",
    )(queries, keys, values, segments.reshape(1, TOK), owners.reshape(1, TOK))
    return attended, cache.reshape(64 * SLOT, 2048)


def solution(mesh):
    return jax.shard_map(
        on_device,
        mesh=mesh,
        in_specs=(
            P("inst", "head"),
            P("inst", "head"),
            P("inst", "head"),
            P("inst"),
            P("inst", None),
        ),
        out_specs=(P("inst", "head"), P("inst", None)),
        check_vma=False,
    )
```

```python
import functools

import jax
import jax.numpy as jnp
from jax import lax
from jax.experimental import pallas as pl
from jax.experimental.pallas import tpu as pltpu
from jax.sharding import PartitionSpec as P

MESH = pl.DeviceIdType.MESH
F32, BF16 = jnp.float32, jnp.bfloat16

HEADS, SIZE, RATIO = 16, 128, 8
TOK = 256
REACH = 20
SLOT = 8
STEP = 4
KEY_ROW, ALL_ROWS = SIZE + 16, 2 * SIZE + 16
HIDDEN = 1e30
TO_LOG2 = SIZE ** -0.5 * 1.4426950408889634

ARRIVALS = (
    ((16, 109, 308, 215, 214, 101, 307, 17, 206, 102, 310, 205, 103, 18, 19, 311, 204, 113, 312, 20),
     (16, 215, 109, 308, 307, 214, 101, 102, 17, 310, 206, 18, 311, 205, 103, 104, 19, 312, 213, 20)),
    ((101, 16, 215, 17, 308, 110, 207, 309, 102, 306, 18, 213, 212, 305, 103, 104, 19, 311, 20, 214),
     (16, 101, 308, 215, 17, 309, 110, 207, 214, 102, 306, 103, 18, 19, 205, 311, 213, 104, 312, 20)),
    ((101, 16, 308, 102, 17, 215, 307, 18, 214, 111, 213, 306, 310, 103, 205, 19, 109, 212, 304, 20),
     (101, 16, 215, 308, 102, 17, 214, 109, 307, 18, 111, 206, 212, 305, 103, 310, 304, 19, 213, 20)),
    ((101, 16, 308, 102, 17, 215, 214, 103, 18, 307, 19, 206, 310, 112, 213, 311, 109, 204, 305, 20),
     (16, 101, 215, 308, 102, 17, 309, 207, 103, 18, 213, 306, 110, 19, 311, 112, 214, 205, 304, 20)),
    ((101, 16, 215, 308, 102, 17, 309, 103, 18, 207, 214, 104, 19, 310, 305, 111, 20, 212, 306, 213),
     (16, 101, 215, 308, 102, 17, 214, 309, 103, 18, 306, 204, 110, 19, 213, 305, 107, 20, 212, 311)),
    ((16, 101, 102, 215, 308, 17, 103, 18, 214, 307, 104, 19, 213, 105, 20, 309, 210, 312, 206, 311),
     (101, 16, 215, 308, 17, 102, 205, 307, 103, 18, 214, 309, 306, 104, 19, 213, 311, 212, 110, 20)),
    ((101, 16, 215, 308, 102, 17, 309, 103, 214, 18, 104, 19, 310, 207, 311, 105, 20, 206, 213, 312),
     (101, 16, 206, 308, 102, 17, 215, 18, 309, 103, 214, 310, 213, 104, 19, 311, 107, 20, 312, 205)),
    ((16, 207, 101, 308, 215, 102, 17, 309, 103, 18, 310, 104, 214, 19, 213, 20, 306, 111, 212, 305),
     (207, 101, 16, 102, 17, 308, 309, 215, 103, 18, 214, 19, 310, 111, 306, 104, 213, 305, 20, 212)),
    ((16, 308, 101, 17, 215, 207, 102, 309, 206, 18, 103, 212, 310, 19, 104, 314, 20, 213, 105, 311),
     (308, 16, 215, 207, 101, 102, 17, 18, 103, 309, 206, 310, 19, 104, 205, 20, 211, 112, 313, 314)),
    ((308, 101, 16, 207, 309, 102, 17, 214, 18, 315, 213, 103, 310, 19, 104, 206, 20, 105, 211, 312),
     (308, 101, 16, 17, 207, 309, 102, 214, 103, 18, 315, 19, 206, 104, 212, 310, 20, 105, 211, 313)),
    ((308, 101, 16, 215, 309, 17, 102, 214, 310, 103, 18, 19, 207, 104, 212, 311, 20, 105, 206, 313),
     (308, 101, 16, 102, 215, 309, 17, 18, 207, 310, 103, 213, 104, 19, 212, 314, 20, 105, 311, 206)),
    ((16, 308, 101, 215, 309, 102, 207, 17, 310, 18, 103, 311, 104, 213, 19, 314, 20, 105, 206, 212),
     (308, 101, 16, 17, 309, 102, 214, 103, 207, 310, 18, 213, 19, 315, 104, 206, 105, 212, 311, 20)),
    ((308, 101, 16, 309, 17, 102, 310, 103, 214, 18, 213, 311, 19, 315, 104, 207, 112, 20, 205, 206),
     (308, 101, 16, 215, 102, 207, 309, 17, 214, 18, 310, 103, 104, 213, 19, 312, 20, 206, 311, 105)),
    ((308, 101, 16, 102, 215, 309, 17, 214, 310, 18, 103, 206, 311, 104, 19, 207, 312, 20, 105, 213),
     (101, 16, 308, 215, 309, 17, 102, 103, 214, 310, 18, 19, 207, 311, 104, 105, 213, 312, 20, 206)),
    ((308, 101, 16, 215, 17, 309, 102, 207, 103, 214, 310, 18, 311, 19, 104, 213, 312, 105, 20, 206),
     (16, 308, 101, 309, 102, 215, 17, 310, 18, 103, 207, 104, 214, 311, 19, 20, 213, 312, 105, 206)),
    ((308, 16, 207, 101, 102, 309, 215, 17, 18, 310, 103, 214, 104, 213, 311, 19, 312, 20, 105, 106),
     (207, 101, 308, 16, 309, 215, 17, 102, 310, 214, 103, 18, 311, 19, 104, 213, 105, 20, 312, 106)),
)


def offset_of(kind, link):
    y, z = divmod(kind, 8)
    return (16, 1 if z > 0 else -7, -1 if z < 7 else 7, 8 if y == 1 else -8)[link]


def target_of(kind, link):
    y, z = divmod(kind, 8)
    return (kind, y * 8 + (z + 1) % 8, y * 8 + (z + 7) % 8, (1 - y) * 8 + z)[link]


def forward_table():
    table = []
    for kind in range(16):
        halves = []
        for half in range(2):
            held = [0] + [a % 100 for a in ARRIVALS[kind][half]]
            rows = []
            for distance in held:
                row = []
                for link in range(4):
                    there = target_of(kind, link)
                    far = distance + offset_of(there, link)
                    order = ARRIVALS[there][half]
                    wanted = link * 100 + far
                    row.append(order.index(wanted) + 1 if 1 <= far <= REACH and wanted in order else 0)
                rows.append(row)
            halves.append(rows)
        table.append(halves)
    return table


TABLE = forward_table()


def kernel(q_hbm, k_hbm, v_hbm, seg_hbm, own_hbm, out_ref, cache_ref,
           q_own, q_turned, k_own, v_own, own_values, seg_ref, own_ref, kv, bias, top, acc, scores_a, scores_b, weights_a, weights_b,
           peaks_a, peaks_b, shrink_a, shrink_b,
           outgoing, mid, recv, block,
           in_sem, kv_send, kv_recv, z_send, z_recv, x_send, x_recv, y_send, y_recv, c_send, c_recv, own_sem):
    me, g = lax.axis_index("inst"), lax.axis_index("head")
    kind = me % 16
    x, y, z = me // 16, (me // 8) % 2, me % 8
    other_y = x * 16 + (1 - y) * 8 + z
    other_chip, other_core = (g + 2) % 4, g + 1 - 2 * (g % 2)
    near = (
        ((x + 1) % 4) * 16 + kind,
        me - z + (z + 1) % 8,
        me - z + (z + 7) % 8,
        other_y,
    )

    inputs = [
        pltpu.make_async_copy(src, dst, in_sem.at[n])
        for n, (src, dst) in enumerate(
            ((k_hbm, k_own), (v_hbm, v_own), (seg_hbm, seg_ref), (own_hbm, own_ref), (q_hbm, q_own)))
    ]
    for copy in inputs:
        copy.start()

    def along_z(by):
        return (me - z + (z + by) % 8, g)

    def along_x(by):
        return (((x + by) % 4) * 16 + kind, g)

    beside = ((me, other_chip), (other_y, g), (other_y, other_chip))
    sibling = (me, other_core)
    barrier = pltpu.get_barrier_semaphore()
    partners = [along_z(by) for by in range(1, 8)] + [along_x(by) for by in range(1, 4)] + list(beside) + [sibling]
    for partner in partners:
        pl.semaphore_signal(barrier, inc=1, device_id=partner, device_id_type=MESH)

    def pick(values):
        chosen = jnp.int32(values[0])
        if len(set(values)) == 1:
            return chosen
        for t in range(1, 16):
            chosen = jnp.where(kind == t, jnp.int32(values[t]), chosen)
        return chosen

    first = [[pick([TABLE[t][half][0][link] for t in range(16)]) for link in range(4)] for half in range(2)]
    def digits(half, jj, k):
        return [(codes[half][jj][link] >> (6 * k)) & 63 for link in range(4)]

    def forward(half, slot, theres, wait=False):
        for link in range(4):
            there = theres[link]

            @pl.when(there > 0)
            def _():
                copy = pltpu.make_async_remote_copy(
                    src_ref=kv.at[half, slot],
                    dst_ref=kv.at[half, there],
                    send_sem=kv_send.at[half * 4 + link, slot],
                    recv_sem=kv_recv.at[half, there],
                    device_id=(near[link], g),
                    device_id_type=MESH,
                )
                if wait:
                    copy.wait_send()
                else:
                    copy.start()

    def arrive(k, h, j):
        half, jj = j % 2, 2 * h + j // 2
        slot = STEP * k + jj + 1
        here = kv.at[half, slot]
        pltpu.make_async_copy(here, here, kv_recv.at[half, slot]).wait()
        forward(half, slot, digits(half, jj, k))

    def drain(k, half, jj):
        forward(half, STEP * k + jj + 1, digits(half, jj, k), wait=True)

    for copy in inputs[:3]:
        copy.wait()
    at0 = lax.broadcasted_iota(jnp.int32, (TOK, TOK), 0)
    at1 = lax.broadcasted_iota(jnp.int32, (TOK, TOK), 1)
    seg_row = seg_ref[...].astype(F32)
    seg_wide = jnp.broadcast_to(seg_row, (TOK, TOK))
    seg_tall = jnp.broadcast_to(jnp.sum(jnp.where(at0 == at1, seg_wide, 0.0), axis=1, keepdims=True), (TOK, TOK))
    first_seg, last_seg = jnp.min(seg_tall, axis=0, keepdims=True), jnp.max(seg_tall, axis=0, keepdims=True)
    reaches = (seg_row == last_seg).astype(F32)
    extra = lax.broadcasted_iota(jnp.int32, (16, TOK), 0)
    extra_rows = jnp.where(extra == 0, reaches, jnp.where(extra == 1, last_seg, 0.0)).astype(BF16)
    for half in range(2):
        feat = slice(half * SIZE, (half + 1) * SIZE)
        turned = v_own[:, feat].astype(F32).T
        kv[half, 0, 0:SIZE, :] = (turned * reaches).astype(BF16)
        kv[half, 0, SIZE:KEY_ROW, :] = extra_rows
        keys = k_own[:, feat].astype(F32)
        last_key = jnp.broadcast_to(keys[TOK - 1:TOK, :], (TOK, SIZE))
        keys = jnp.where(seg_tall[:, 0:SIZE] == last_seg[:, 0:SIZE], keys, last_key).astype(BF16)
        kv[half, 0, KEY_ROW:ALL_ROWS, 0:SIZE] = keys[0:SIZE]
        kv[half, 0, KEY_ROW:ALL_ROWS, SIZE:TOK] = keys[SIZE:TOK]
    pl.semaphore_wait(barrier, len(partners))
    forward(0, 0, first[0])
    forward(1, 0, first[1])

    codes = [
        [
            [pick([sum(TABLE[t][half][STEP * k + jj + 1][link] * 64 ** k for k in range(5)) for t in range(16)]) for link in range(4)]
            for jj in range(STEP)
        ]
        for half in range(2)
    ]

    for half in range(2):
        own_values[half, 0:SIZE, :] = v_own[:, half * SIZE:(half + 1) * SIZE].astype(F32).T.astype(BF16)
        own_values[half, SIZE:KEY_ROW, :] = jnp.where(extra == 0, 1.0, 0.0).astype(BF16)
    inputs[4].wait()
    for h in range(HEADS):
        q_turned[h] = q_own[:, h * SIZE:(h + 1) * SIZE].astype(F32).T.astype(BF16)
    bias[...] = jnp.where((at0 <= at1) & (seg_tall == seg_wide), 0.0, -HIDDEN)

    inputs[3].wait()
    dest = own_ref[...]
    owner = lax.broadcasted_iota(jnp.int32, (64, TOK), 0)
    hot = (owner == dest).astype(F32)
    before = (lax.broadcasted_iota(jnp.int32, (TOK, TOK), 0) < lax.broadcasted_iota(jnp.int32, (TOK, TOK), 1)).astype(BF16)
    count = jnp.dot(hot.astype(BF16), before, preferred_element_type=F32)
    place = jnp.sum(hot * count, axis=0, keepdims=True).astype(jnp.int32)
    target = dest * (2 * SLOT) + place
    row = lax.broadcasted_iota(jnp.int32, (1024, TOK), 0)
    of_keys = (row == target).astype(BF16)
    of_values = (row == target + SLOT).astype(BF16)
    rows = jnp.dot(of_keys, k_own[...], preferred_element_type=F32)
    rows += jnp.dot(of_values, v_own[...], preferred_element_type=F32)
    outgoing[...] = rows.astype(BF16).reshape(4, 2, 8, 2 * SLOT, 2 * SIZE)

    def z_copy(by):
        return pltpu.make_async_remote_copy(
            src_ref=outgoing.at[:, :, (z + by) % 8], dst_ref=mid.at[z], send_sem=z_send.at[by], recv_sem=z_recv.at[z],
            device_id=along_z(by), device_id_type=MESH)

    def x_copy(by):
        return pltpu.make_async_remote_copy(
            src_ref=mid.at[:, (x + by) % 4], dst_ref=recv.at[x], send_sem=x_send.at[by], recv_sem=x_recv.at[x],
            device_id=along_x(by), device_id_type=MESH)

    def rows_of(source_y, group):
        return cache_ref.at[:, source_y, :, pl.ds(pl.multiple_of(group * 512, 512), 512)]

    def y_copy(n):
        return pltpu.make_async_remote_copy(
            src_ref=block.at[y if n == 0 else 1 - y], dst_ref=rows_of(y, g), send_sem=y_send.at[n], recv_sem=y_recv.at[n],
            device_id=beside[n], device_id_type=MESH)

    from_y = ((y, other_chip), (1 - y, g), (1 - y, other_chip))

    def c_copy(n):
        if n == 3:
            src, place = block.at[y], rows_of(y, g)
        else:
            src = place = rows_of(*from_y[n])
        return pltpu.make_async_remote_copy(
            src_ref=src, dst_ref=place, send_sem=c_send.at[n], recv_sem=c_recv.at[n],
            device_id=sibling, device_id_type=MESH)

    def own_copy():
        return pltpu.make_async_copy(block.at[y], rows_of(y, g), own_sem)

    def first_leg():
        for by in (1, 7, 2, 6, 3, 5, 4):
            z_copy(by).start()
        for i in range(4):
            for j in range(2):
                mid[z, i, j] = outgoing[i, j, z]

    def second_leg():
        for by in range(1, 8):
            src = (z + 8 - by) % 8
            pltpu.make_async_copy(mid.at[src], mid.at[src], z_recv.at[src]).wait()
        for by in (1, 3, 2):
            x_copy(by).start()
        for i in range(8):
            recv[x, i] = mid[i, x]

    def third_leg():
        for by in range(1, 4):
            src = (x + 4 - by) % 4
            pltpu.make_async_copy(recv.at[src], recv.at[src], x_recv.at[src]).wait()
        a = lax.broadcasted_iota(jnp.int32, (64, 128), 0)
        b = lax.broadcasted_iota(jnp.int32, (64, 128), 1)
        key_rows = (b == 2 * a - (a & 7)).astype(BF16)
        value_rows = (b == 2 * a - (a & 7) + 8).astype(BF16)
        for src in range(4):
            for j in range(2):
                arrived = recv[src, :, j].reshape(128, 2 * SIZE)
                block[j, src, :, 0:256] = jnp.dot(key_rows, arrived, preferred_element_type=F32).astype(BF16)
                block[j, src, :, 256:512] = jnp.dot(value_rows, arrived, preferred_element_type=F32).astype(BF16)
        for n in range(3):
            y_copy(n).start()
        c_copy(3).start()
        own_copy().start()

    def fourth_leg():
        for n in range(3):
            here = rows_of(*from_y[n])
            pltpu.make_async_copy(here, here, y_recv.at[n]).wait()
            c_copy(n).start()

    scores_of, weights_of = (scores_a, scores_b), (weights_a, weights_b)
    peaks_of, shrink_of = (peaks_a, peaks_b), (shrink_a, shrink_b)

    def score(n, h, slots):
        if slots is None:
            keys = k_own[:, (h // RATIO) * SIZE:(h // RATIO + 1) * SIZE]
        else:
            keys = jnp.concatenate(
                [kv[h // RATIO, slot, KEY_ROW:ALL_ROWS, lanes:lanes + SIZE] for slot in slots for lanes in (0, SIZE)], axis=0)
        product = jnp.dot(keys, q_turned[h], preferred_element_type=F32)
        if slots is None:
            product += bias[...]
        scores_of[n % 2][0:product.shape[0], :] = product
        for c in range(product.shape[0] // TOK):
            peaks_of[n % 2][c] = jnp.max(product[c * TOK:(c + 1) * TOK], axis=0, keepdims=True)

    def peak_rows(n, h, slots):
        if slots is None:
            top[h] = peaks_of[n % 2][0]
            return [top[h]]
        seen = []
        for slot in slots:
            block_seg = kv[h // RATIO, slot, SIZE:KEY_ROW, :].astype(F32)[1:2, :]
            seen.append((block_seg == first_seg) & (seg_row == first_seg))
        old = top[h]
        peak = old
        for c in range(len(slots)):
            peak = jnp.maximum(peak, jnp.where(seen[c], peaks_of[n % 2][c], -HIDDEN))
        top[h] = peak
        shrink_of[n % 2][...] = jnp.exp2((old - peak) * TO_LOG2)
        return [jnp.where(seen[c], peak, HIDDEN) for c in range(len(slots))]

    def soften(n, peaks, c, start, rows):
        at = slice(c * TOK + start, c * TOK + start + rows)
        weights_of[n % 2][at, :] = jnp.exp2((scores_of[n % 2][at, :] - peaks[c]) * TO_LOG2).astype(BF16)

    def combine(n, h, slots):
        if slots is None:
            acc[h] = jnp.dot(own_values[h // RATIO], weights_of[n % 2][0:TOK, :], preferred_element_type=F32)
        else:
            values = jnp.concatenate([kv[h // RATIO, slot, 0:KEY_ROW, :] for slot in slots], axis=1)
            product = jnp.dot(values, weights_of[n % 2][...], preferred_element_type=F32)
            acc[h] = acc[h] * shrink_of[n % 2][...] + product

    def turn(n, before, now, after):
        peaks = peak_rows(n, *now)
        if before is not None:
            combine(n - 1, *before)
        for c in range(len(peaks)):
            if after is not None and c == len(peaks) // 2:
                score(n + 1, *after)
            for start in range(0, TOK, 64):
                soften(n, peaks, c, start, 64)

    for half in range(2):
        heads = [(half * RATIO + i, None) for i in range(RATIO)]
        score(0, *heads[0])
        for n in range(RATIO):
            turn(n, heads[n - 1] if n > 0 else None, heads[n], heads[n + 1] if n + 1 < RATIO else None)
        combine(RATIO - 1, *heads[-1])
        for j in range(4):
            arrive(0, half, j)
        if half == 0:
            first_leg()

    def slots_of(k):
        return [STEP * k + 1 + c for c in range(STEP)]

    score(0, 0, slots_of(0))

    def step(k, carry):
        now = slots_of(k)
        turns = [(h, now) for h in range(HEADS)] + [(0, slots_of(jnp.minimum(k + 1, 4)))]
        for n in range(HEADS):
            turn(n, turns[n - 1] if n > 0 else None, turns[n], turns[n + 1])
            if n == HEADS - 1:
                combine(n, *turns[n])
            if n % 2 == 1:
                @pl.when(k < 4)
                def _():
                    arrive(k + 1, n // 8, (n // 2) % 4)

                @pl.when(k > 0)
                def _():
                    drain(k - 1, n // 8, (n // 2) % 4)
            if n % 8 == 7:
                @pl.when(k == (3, 1)[n // 8])
                def _():
                    (third_leg, second_leg)[n // 8]()
        return carry

    lax.fori_loop(0, 5, step, 0)
    fourth_leg()

    for h in range(HEADS):
        out_ref[:, h * SIZE:(h + 1) * SIZE] = (acc[h, 0:SIZE, :] * (1.0 / acc[h, SIZE:SIZE + 1, :])).T.astype(BF16)

    for half in range(2):
        forward(half, 0, first[half], wait=True)
        for jj in range(STEP):
            drain(4, half, jj)
    for by in range(1, 8):
        z_copy(by).wait_send()
    for by in range(1, 4):
        x_copy(by).wait_send()
    for n in range(3):
        y_copy(n).wait_send()
    own_copy().wait()
    across = (other_core + 2) % 4
    from_core = ((y, across), (1 - y, other_core), (1 - y, across), (y, other_core))
    for n in range(4):
        c_copy(n).wait_send()
        here = rows_of(*from_core[n])
        pltpu.make_async_copy(here, here, c_recv.at[n]).wait()


def on_device(queries, keys, values, segments, owners):
    whole = pl.BlockSpec(memory_space=pl.ANY)
    operands = (queries, keys, values, segments.reshape(1, TOK), owners.reshape(1, TOK))
    attended, cache = pl.pallas_call(
        kernel,
        out_shape=(
            jax.ShapeDtypeStruct((TOK, HEADS * SIZE), BF16),
            jax.ShapeDtypeStruct((4, 2, 64, 2048), BF16),
        ),
        in_specs=[whole] * 5,
        out_specs=(pl.BlockSpec(memory_space=pltpu.VMEM), whole),
        scratch_shapes=[
            pltpu.VMEM((TOK, HEADS * SIZE), BF16),
            pltpu.VMEM((HEADS, SIZE, TOK), BF16),
            pltpu.VMEM((TOK, 2 * SIZE), BF16),
            pltpu.VMEM((TOK, 2 * SIZE), BF16),
            pltpu.VMEM((2, KEY_ROW, TOK), BF16),
            pltpu.VMEM((1, TOK), jnp.int32),
            pltpu.VMEM((1, TOK), jnp.int32),
            pltpu.VMEM((2, REACH + 1, ALL_ROWS, TOK), BF16),
            pltpu.VMEM((TOK, TOK), F32),
            pltpu.VMEM((HEADS, 1, TOK), F32),
            pltpu.VMEM((HEADS, KEY_ROW, TOK), F32),
            pltpu.VMEM((STEP * TOK, TOK), F32),
            pltpu.VMEM((STEP * TOK, TOK), F32),
            pltpu.VMEM((STEP * TOK, TOK), BF16),
            pltpu.VMEM((STEP * TOK, TOK), BF16),
            pltpu.VMEM((STEP, 1, TOK), F32),
            pltpu.VMEM((STEP, 1, TOK), F32),
            pltpu.VMEM((1, TOK), F32),
            pltpu.VMEM((1, TOK), F32),
            pltpu.VMEM((4, 2, 8, 2 * SLOT, 2 * SIZE), BF16),
            pltpu.VMEM((8, 4, 2, 2 * SLOT, 2 * SIZE), BF16),
            pltpu.VMEM((4, 8, 2, 2 * SLOT, 2 * SIZE), BF16),
            pltpu.VMEM((2, 4, 64, 4 * SIZE), BF16),
            pltpu.SemaphoreType.DMA((5,)),
            pltpu.SemaphoreType.DMA((8, REACH + 1)),
            pltpu.SemaphoreType.DMA((2, REACH + 1)),
            pltpu.SemaphoreType.DMA((8,)),
            pltpu.SemaphoreType.DMA((8,)),
            pltpu.SemaphoreType.DMA((4,)),
            pltpu.SemaphoreType.DMA((4,)),
            pltpu.SemaphoreType.DMA((3,)),
            pltpu.SemaphoreType.DMA((3,)),
            pltpu.SemaphoreType.DMA((4,)),
            pltpu.SemaphoreType.DMA((4,)),
            pltpu.SemaphoreType.DMA(()),
        ],
        compiler_params=pltpu.CompilerParams(
            collective_id=0, has_side_effects=True, vmem_limit_bytes=40 * 1024 * 1024
        ),
        cost_estimate=pl.CostEstimate(flops=12_000_000_000, bytes_accessed=6_000_000, transcendentals=22_000_000),
        name="attend_and_send",
    )(*(pltpu.with_memory_space_constraint(a, pltpu.HBM) for a in operands))
    return attended, cache.reshape(64 * SLOT, 2048)


def solution(mesh):
    return jax.shard_map(
        on_device,
        mesh=mesh,
        in_specs=(
            P("inst", "head"),
            P("inst", "head"),
            P("inst", "head"),
            P("inst"),
            P("inst", None),
        ),
        out_specs=(P("inst", "head"), P("inst", None)),
        check_vma=False,
    )
```

```python
import functools

import jax
import jax.numpy as jnp
from jax import lax
from jax.experimental import pallas as pl
from jax.experimental.pallas import tpu as pltpu
from jax.sharding import PartitionSpec as P

MESH = pl.DeviceIdType.MESH
F32, BF16 = jnp.float32, jnp.bfloat16

HEADS, SIZE, RATIO = 16, 128, 8
TOK = 256
REACH = 20
SLOT = 8
STEP = 4
KEY_ROW, ALL_ROWS = SIZE + 16, 2 * SIZE + 16
HIDDEN = 1e30
GROUP = 4
WIDE = GROUP * TOK
TO_LOG2 = SIZE ** -0.5 * 1.4426950408889634

ARRIVALS = (
    ((16, 109, 308, 215, 214, 101, 307, 17, 206, 102, 310, 205, 103, 18, 19, 311, 204, 113, 312, 20),
     (16, 215, 109, 308, 307, 214, 101, 102, 17, 310, 206, 18, 311, 205, 103, 104, 19, 312, 213, 20)),
    ((101, 16, 215, 17, 308, 110, 207, 309, 102, 306, 18, 213, 212, 305, 103, 104, 19, 311, 20, 214),
     (16, 101, 308, 215, 17, 309, 110, 207, 214, 102, 306, 103, 18, 19, 205, 311, 213, 104, 312, 20)),
    ((101, 16, 308, 102, 17, 215, 307, 18, 214, 111, 213, 306, 310, 103, 205, 19, 109, 212, 304, 20),
     (101, 16, 215, 308, 102, 17, 214, 109, 307, 18, 111, 206, 212, 305, 103, 310, 304, 19, 213, 20)),
    ((101, 16, 308, 102, 17, 215, 214, 103, 18, 307, 19, 206, 310, 112, 213, 311, 109, 204, 305, 20),
     (16, 101, 215, 308, 102, 17, 309, 207, 103, 18, 213, 306, 110, 19, 311, 112, 214, 205, 304, 20)),
    ((101, 16, 215, 308, 102, 17, 309, 103, 18, 207, 214, 104, 19, 310, 305, 111, 20, 212, 306, 213),
     (16, 101, 215, 308, 102, 17, 214, 309, 103, 18, 306, 204, 110, 19, 213, 305, 107, 20, 212, 311)),
    ((16, 101, 102, 215, 308, 17, 103, 18, 214, 307, 104, 19, 213, 105, 20, 309, 210, 312, 206, 311),
     (101, 16, 215, 308, 17, 102, 205, 307, 103, 18, 214, 309, 306, 104, 19, 213, 311, 212, 110, 20)),
    ((101, 16, 215, 308, 102, 17, 309, 103, 214, 18, 104, 19, 310, 207, 311, 105, 20, 206, 213, 312),
     (101, 16, 206, 308, 102, 17, 215, 18, 309, 103, 214, 310, 213, 104, 19, 311, 107, 20, 312, 205)),
    ((16, 207, 101, 308, 215, 102, 17, 309, 103, 18, 310, 104, 214, 19, 213, 20, 306, 111, 212, 305),
     (207, 101, 16, 102, 17, 308, 309, 215, 103, 18, 214, 19, 310, 111, 306, 104, 213, 305, 20, 212)),
    ((16, 308, 101, 17, 215, 207, 102, 309, 206, 18, 103, 212, 310, 19, 104, 314, 20, 213, 105, 311),
     (308, 16, 215, 207, 101, 102, 17, 18, 103, 309, 206, 310, 19, 104, 205, 20, 211, 112, 313, 314)),
    ((308, 101, 16, 207, 309, 102, 17, 214, 18, 315, 213, 103, 310, 19, 104, 206, 20, 105, 211, 312),
     (308, 101, 16, 17, 207, 309, 102, 214, 103, 18, 315, 19, 206, 104, 212, 310, 20, 105, 211, 313)),
    ((308, 101, 16, 215, 309, 17, 102, 214, 310, 103, 18, 19, 207, 104, 212, 311, 20, 105, 206, 313),
     (308, 101, 16, 102, 215, 309, 17, 18, 207, 310, 103, 213, 104, 19, 212, 314, 20, 105, 311, 206)),
    ((16, 308, 101, 215, 309, 102, 207, 17, 310, 18, 103, 311, 104, 213, 19, 314, 20, 105, 206, 212),
     (308, 101, 16, 17, 309, 102, 214, 103, 207, 310, 18, 213, 19, 315, 104, 206, 105, 212, 311, 20)),
    ((308, 101, 16, 309, 17, 102, 310, 103, 214, 18, 213, 311, 19, 315, 104, 207, 112, 20, 205, 206),
     (308, 101, 16, 215, 102, 207, 309, 17, 214, 18, 310, 103, 104, 213, 19, 312, 20, 206, 311, 105)),
    ((308, 101, 16, 102, 215, 309, 17, 214, 310, 18, 103, 206, 311, 104, 19, 207, 312, 20, 105, 213),
     (101, 16, 308, 215, 309, 17, 102, 103, 214, 310, 18, 19, 207, 311, 104, 105, 213, 312, 20, 206)),
    ((308, 101, 16, 215, 17, 309, 102, 207, 103, 214, 310, 18, 311, 19, 104, 213, 312, 105, 20, 206),
     (16, 308, 101, 309, 102, 215, 17, 310, 18, 103, 207, 104, 214, 311, 19, 20, 213, 312, 105, 206)),
    ((308, 16, 207, 101, 102, 309, 215, 17, 18, 310, 103, 214, 104, 213, 311, 19, 312, 20, 105, 106),
     (207, 101, 308, 16, 309, 215, 17, 102, 310, 214, 103, 18, 311, 19, 104, 213, 105, 20, 312, 106)),
)


def offset_of(kind, link):
    y, z = divmod(kind, 8)
    return (16, 1 if z > 0 else -7, -1 if z < 7 else 7, 8 if y == 1 else -8)[link]


def target_of(kind, link):
    y, z = divmod(kind, 8)
    return (kind, y * 8 + (z + 1) % 8, y * 8 + (z + 7) % 8, (1 - y) * 8 + z)[link]


def forward_table():
    table = []
    for kind in range(16):
        halves = []
        for half in range(2):
            held = [0] + [a % 100 for a in ARRIVALS[kind][half]]
            rows = []
            for distance in held:
                row = []
                for link in range(4):
                    there = target_of(kind, link)
                    far = distance + offset_of(there, link)
                    order = ARRIVALS[there][half]
                    wanted = link * 100 + far
                    row.append(order.index(wanted) + 1 if 1 <= far <= REACH and wanted in order else 0)
                rows.append(row)
            halves.append(rows)
        table.append(halves)
    return table


TABLE = forward_table()


def kernel(q_hbm, k_hbm, v_hbm, seg_hbm, own_hbm, out_ref, cache_ref,
           q_own, q_turned, k_own, v_own, own_values, seg_ref, own_ref, kv, bias, top, acc, scores_a, scores_b, weights_a, weights_b,
           peaks_a, peaks_b, shrink_a, shrink_b,
           outgoing, mid, recv, block,
           in_sem, kv_send, kv_recv, z_send, z_recv, x_send, x_recv, y_send, y_recv, c_send, c_recv, own_sem):
    me, g = lax.axis_index("inst"), lax.axis_index("head")
    kind = me % 16
    x, y, z = me // 16, (me // 8) % 2, me % 8
    other_y = x * 16 + (1 - y) * 8 + z
    other_chip, other_core = (g + 2) % 4, g + 1 - 2 * (g % 2)
    near = (
        ((x + 1) % 4) * 16 + kind,
        me - z + (z + 1) % 8,
        me - z + (z + 7) % 8,
        other_y,
    )

    inputs = [
        pltpu.make_async_copy(src, dst, in_sem.at[n])
        for n, (src, dst) in enumerate(
            ((k_hbm, k_own), (v_hbm, v_own), (seg_hbm, seg_ref), (own_hbm, own_ref), (q_hbm, q_own)))
    ]
    for copy in inputs:
        copy.start()

    def along_z(by):
        return (me - z + (z + by) % 8, g)

    def along_x(by):
        return (((x + by) % 4) * 16 + kind, g)

    beside = ((me, other_chip), (other_y, g), (other_y, other_chip))
    sibling = (me, other_core)
    barrier = pltpu.get_barrier_semaphore()
    partners = [along_z(by) for by in range(1, 8)] + [along_x(by) for by in range(1, 4)] + list(beside) + [sibling]
    for partner in partners:
        pl.semaphore_signal(barrier, inc=1, device_id=partner, device_id_type=MESH)

    def pick(values):
        chosen = jnp.int32(values[0])
        if len(set(values)) == 1:
            return chosen
        for t in range(1, 16):
            chosen = jnp.where(kind == t, jnp.int32(values[t]), chosen)
        return chosen

    first = [[pick([TABLE[t][half][0][link] for t in range(16)]) for link in range(4)] for half in range(2)]
    def digits(half, jj, k):
        return [(codes[half][jj][link] >> (6 * k)) & 63 for link in range(4)]

    def forward(half, slot, theres, wait=False):
        for link in range(4):
            there = theres[link]

            @pl.when(there > 0)
            def _():
                copy = pltpu.make_async_remote_copy(
                    src_ref=kv.at[half, slot],
                    dst_ref=kv.at[half, there],
                    send_sem=kv_send.at[half * 4 + link, slot],
                    recv_sem=kv_recv.at[half, there],
                    device_id=(near[link], g),
                    device_id_type=MESH,
                )
                if wait:
                    copy.wait_send()
                else:
                    copy.start()

    def arrive(k, h, j):
        half, jj = j % 2, 2 * h + j // 2
        slot = STEP * k + jj + 1
        here = kv.at[half, slot]
        pltpu.make_async_copy(here, here, kv_recv.at[half, slot]).wait()
        forward(half, slot, digits(half, jj, k))

    def drain(k, half, jj):
        forward(half, STEP * k + jj + 1, digits(half, jj, k), wait=True)

    for copy in inputs[:3]:
        copy.wait()
    at0 = lax.broadcasted_iota(jnp.int32, (TOK, TOK), 0)
    at1 = lax.broadcasted_iota(jnp.int32, (TOK, TOK), 1)
    seg_row = seg_ref[...].astype(F32)
    seg_wide = jnp.broadcast_to(seg_row, (TOK, TOK))
    seg_tall = jnp.broadcast_to(jnp.sum(jnp.where(at0 == at1, seg_wide, 0.0), axis=1, keepdims=True), (TOK, TOK))
    first_seg, last_seg = jnp.min(seg_tall, axis=0, keepdims=True), jnp.max(seg_tall, axis=0, keepdims=True)
    reaches = (seg_row == last_seg).astype(F32)
    extra = lax.broadcasted_iota(jnp.int32, (16, TOK), 0)
    extra_rows = jnp.where(extra == 0, reaches, jnp.where(extra == 1, last_seg, 0.0)).astype(BF16)
    for half in range(2):
        feat = slice(half * SIZE, (half + 1) * SIZE)
        turned = v_own[:, feat].astype(F32).T
        kv[half, 0, 0:SIZE, :] = (turned * reaches).astype(BF16)
        kv[half, 0, SIZE:KEY_ROW, :] = extra_rows
        keys = k_own[:, feat].astype(F32)
        last_key = jnp.broadcast_to(keys[TOK - 1:TOK, :], (TOK, SIZE))
        keys = jnp.where(seg_tall[:, 0:SIZE] == last_seg[:, 0:SIZE], keys, last_key).astype(BF16)
        kv[half, 0, KEY_ROW:ALL_ROWS, 0:SIZE] = keys[0:SIZE]
        kv[half, 0, KEY_ROW:ALL_ROWS, SIZE:TOK] = keys[SIZE:TOK]
    pl.semaphore_wait(barrier, len(partners))
    forward(0, 0, first[0])
    forward(1, 0, first[1])

    codes = [
        [
            [pick([sum(TABLE[t][half][STEP * k + jj + 1][link] * 64 ** k for k in range(5)) for t in range(16)]) for link in range(4)]
            for jj in range(STEP)
        ]
        for half in range(2)
    ]

    for half in range(2):
        own_values[half, 0:SIZE, :] = v_own[:, half * SIZE:(half + 1) * SIZE].astype(F32).T.astype(BF16)
        own_values[half, SIZE:KEY_ROW, :] = jnp.where(extra == 0, 1.0, 0.0).astype(BF16)
    inputs[4].wait()
    for h in range(HEADS):
        turned = q_own[:, h * SIZE:(h + 1) * SIZE].astype(F32).T.astype(BF16)
        q_turned[h // GROUP, :, (h % GROUP) * TOK:(h % GROUP + 1) * TOK] = turned
    bias[...] = jnp.where((at0 <= at1) & (seg_tall == seg_wide), 0.0, -HIDDEN)

    inputs[3].wait()
    dest = own_ref[...]
    owner = lax.broadcasted_iota(jnp.int32, (64, TOK), 0)
    hot = (owner == dest).astype(F32)
    before = (lax.broadcasted_iota(jnp.int32, (TOK, TOK), 0) < lax.broadcasted_iota(jnp.int32, (TOK, TOK), 1)).astype(BF16)
    count = jnp.dot(hot.astype(BF16), before, preferred_element_type=F32)
    place = jnp.sum(hot * count, axis=0, keepdims=True).astype(jnp.int32)
    target = dest * (2 * SLOT) + place
    row = lax.broadcasted_iota(jnp.int32, (1024, TOK), 0)
    of_keys = (row == target).astype(BF16)
    of_values = (row == target + SLOT).astype(BF16)
    rows = jnp.dot(of_keys, k_own[...], preferred_element_type=F32)
    rows += jnp.dot(of_values, v_own[...], preferred_element_type=F32)
    outgoing[...] = rows.astype(BF16).reshape(4, 2, 8, 2 * SLOT, 2 * SIZE)

    def z_copy(by):
        return pltpu.make_async_remote_copy(
            src_ref=outgoing.at[:, :, (z + by) % 8], dst_ref=mid.at[z], send_sem=z_send.at[by], recv_sem=z_recv.at[z],
            device_id=along_z(by), device_id_type=MESH)

    def x_copy(by):
        return pltpu.make_async_remote_copy(
            src_ref=mid.at[:, (x + by) % 4], dst_ref=recv.at[x], send_sem=x_send.at[by], recv_sem=x_recv.at[x],
            device_id=along_x(by), device_id_type=MESH)

    def rows_of(source_y, group):
        return cache_ref.at[:, source_y, :, pl.ds(pl.multiple_of(group * 512, 512), 512)]

    def y_copy(n):
        return pltpu.make_async_remote_copy(
            src_ref=block.at[y if n == 0 else 1 - y], dst_ref=rows_of(y, g), send_sem=y_send.at[n], recv_sem=y_recv.at[n],
            device_id=beside[n], device_id_type=MESH)

    from_y = ((y, other_chip), (1 - y, g), (1 - y, other_chip))

    def c_copy(n):
        if n == 3:
            src, place = block.at[y], rows_of(y, g)
        else:
            src = place = rows_of(*from_y[n])
        return pltpu.make_async_remote_copy(
            src_ref=src, dst_ref=place, send_sem=c_send.at[n], recv_sem=c_recv.at[n],
            device_id=sibling, device_id_type=MESH)

    def own_copy():
        return pltpu.make_async_copy(block.at[y], rows_of(y, g), own_sem)

    def first_leg():
        for by in (1, 7, 2, 6, 3, 5, 4):
            z_copy(by).start()
        for i in range(4):
            for j in range(2):
                mid[z, i, j] = outgoing[i, j, z]

    def second_leg():
        for by in range(1, 8):
            src = (z + 8 - by) % 8
            pltpu.make_async_copy(mid.at[src], mid.at[src], z_recv.at[src]).wait()
        for by in (1, 3, 2):
            x_copy(by).start()
        for i in range(8):
            recv[x, i] = mid[i, x]

    def third_leg():
        for by in range(1, 4):
            src = (x + 4 - by) % 4
            pltpu.make_async_copy(recv.at[src], recv.at[src], x_recv.at[src]).wait()
        a = lax.broadcasted_iota(jnp.int32, (64, 128), 0)
        b = lax.broadcasted_iota(jnp.int32, (64, 128), 1)
        key_rows = (b == 2 * a - (a & 7)).astype(BF16)
        value_rows = (b == 2 * a - (a & 7) + 8).astype(BF16)
        for src in range(4):
            for j in range(2):
                arrived = recv[src, :, j].reshape(128, 2 * SIZE)
                block[j, src, :, 0:256] = jnp.dot(key_rows, arrived, preferred_element_type=F32).astype(BF16)
                block[j, src, :, 256:512] = jnp.dot(value_rows, arrived, preferred_element_type=F32).astype(BF16)
        for n in range(3):
            y_copy(n).start()
        c_copy(3).start()
        own_copy().start()

    def fourth_leg():
        for n in range(3):
            here = rows_of(*from_y[n])
            pltpu.make_async_copy(here, here, y_recv.at[n]).wait()
            c_copy(n).start()

    scores_of, weights_of = (scores_a, scores_b), (weights_a, weights_b)
    peaks_of, shrink_of = (peaks_a, peaks_b), (shrink_a, shrink_b)
    first_wide = jnp.concatenate([(seg_row == first_seg).astype(F32)] * GROUP, axis=1)

    def half_of(group):
        return group // (RATIO // GROUP)

    def score(n, group, slots, c):
        half = half_of(group)
        if slots is None:
            keys = k_own[:, half * SIZE:(half + 1) * SIZE]
        else:
            keys = jnp.concatenate([kv[half, slots[c], KEY_ROW:ALL_ROWS, lanes:lanes + SIZE] for lanes in (0, SIZE)], axis=0)
        product = jnp.dot(keys, q_turned[group], preferred_element_type=F32)
        if slots is None:
            product += jnp.concatenate([bias[...]] * GROUP, axis=1)
        scores_of[n % 2][c * TOK:(c + 1) * TOK, :] = product
        peaks_of[n % 2][c] = jnp.max(product, axis=0, keepdims=True)

    def peak_rows(n, group, slots):
        if slots is None:
            top[group] = peaks_of[n % 2][0]
            return [top[group]]
        seen = []
        for slot in slots:
            block_seg = kv[half_of(group), slot, SIZE:KEY_ROW, :].astype(F32)[1:2, :]
            same = jnp.concatenate([(block_seg == first_seg).astype(F32)] * GROUP, axis=1)
            seen.append(same * first_wide > 0.5)
        old = top[group]
        peak = old
        for c in range(len(slots)):
            peak = jnp.maximum(peak, jnp.where(seen[c], peaks_of[n % 2][c], -HIDDEN))
        top[group] = peak
        shrink_of[n % 2][...] = jnp.exp2((old - peak) * TO_LOG2)
        return [jnp.where(seen[c], peak, HIDDEN) for c in range(len(slots))]

    def soften(n, peak, c):
        for at in range(c * TOK, (c + 1) * TOK, 16):
            rows = slice(at, at + 16)
            weights_of[n % 2][rows, :] = jnp.exp2((scores_of[n % 2][rows, :] - peak) * TO_LOG2).astype(BF16)

    def combine(n, group, slots, c):
        values = own_values[half_of(group)] if slots is None else kv[half_of(group), slots[c], 0:KEY_ROW, :]
        product = jnp.dot(values, weights_of[n % 2][c * TOK:(c + 1) * TOK, :], preferred_element_type=F32)
        if slots is None:
            acc[group] = product
        elif c == 0:
            acc[group] = acc[group] * shrink_of[n % 2][...] + product
        else:
            acc[group] += product

    def turn(n, before, now, after):
        peaks = peak_rows(n, *now)
        for c in range(len(peaks)):
            if before is not None:
                combine(n - 1, *before, c)
            if after is not None:
                score(n + 1, *after, c)
            soften(n, peaks[c], c)

    groups = HEADS // GROUP
    turns = [(group, None) for group in range(groups)]
    score(0, *turns[0], 0)
    for n in range(groups):
        turn(n, turns[n - 1] if n > 0 else None, turns[n], turns[n + 1] if n + 1 < groups else None)
        for item in (2 * n, 2 * n + 1):
            arrive(0, item // 4, item % 4)
        if n == 1:
            first_leg()
    combine(groups - 1, *turns[-1], 0)

    def slots_of(k):
        return [STEP * k + 1 + c for c in range(STEP)]

    for c in range(STEP):
        score(0, 0, slots_of(0), c)

    def step(k, carry):
        turns = [(group, slots_of(k)) for group in range(groups)] + [(0, slots_of(jnp.minimum(k + 1, 4)))]
        for n in range(groups):
            turn(n, turns[n - 1] if n > 0 else None, turns[n], turns[n + 1])
            if n == groups - 1:
                for c in range(STEP):
                    combine(n, *turns[n], c)
            items = ((0, 1), (2, 3), (4, 5, 6), (7,))[n]

            @pl.when(k < 4)
            def _():
                for item in items:
                    arrive(k + 1, item // 4, item % 4)

            @pl.when(k > 0)
            def _():
                for item in items:
                    drain(k - 1, item % 2, item // 2)
            if n % 2 == 1:
                @pl.when(k == (3, 1)[n // 2])
                def _():
                    (third_leg, second_leg)[n // 2]()
        return carry

    lax.fori_loop(0, 5, step, 0)
    fourth_leg()

    for h in range(HEADS):
        group, lanes = h // GROUP, slice((h % GROUP) * TOK, (h % GROUP + 1) * TOK)
        attended = acc[group, 0:SIZE, lanes] * (1.0 / acc[group, SIZE:SIZE + 1, lanes])
        out_ref[:, h * SIZE:(h + 1) * SIZE] = attended.T.astype(BF16)

    for half in range(2):
        forward(half, 0, first[half], wait=True)
        for jj in range(STEP):
            drain(4, half, jj)
    for by in range(1, 8):
        z_copy(by).wait_send()
    for by in range(1, 4):
        x_copy(by).wait_send()
    for n in range(3):
        y_copy(n).wait_send()
    own_copy().wait()
    across = (other_core + 2) % 4
    from_core = ((y, across), (1 - y, other_core), (1 - y, across), (y, other_core))
    for n in range(4):
        c_copy(n).wait_send()
        here = rows_of(*from_core[n])
        pltpu.make_async_copy(here, here, c_recv.at[n]).wait()


def on_device(queries, keys, values, segments, owners):
    whole = pl.BlockSpec(memory_space=pl.ANY)
    operands = (queries, keys, values, segments.reshape(1, TOK), owners.reshape(1, TOK))
    attended, cache = pl.pallas_call(
        kernel,
        out_shape=(
            jax.ShapeDtypeStruct((TOK, HEADS * SIZE), BF16),
            jax.ShapeDtypeStruct((4, 2, 64, 2048), BF16),
        ),
        in_specs=[whole] * 5,
        out_specs=(pl.BlockSpec(memory_space=pltpu.VMEM), whole),
        scratch_shapes=[
            pltpu.VMEM((TOK, HEADS * SIZE), BF16),
            pltpu.VMEM((HEADS // GROUP, SIZE, WIDE), BF16),
            pltpu.VMEM((TOK, 2 * SIZE), BF16),
            pltpu.VMEM((TOK, 2 * SIZE), BF16),
            pltpu.VMEM((2, KEY_ROW, TOK), BF16),
            pltpu.VMEM((1, TOK), jnp.int32),
            pltpu.VMEM((1, TOK), jnp.int32),
            pltpu.VMEM((2, REACH + 1, ALL_ROWS, TOK), BF16),
            pltpu.VMEM((TOK, TOK), F32),
            pltpu.VMEM((HEADS // GROUP, 1, WIDE), F32),
            pltpu.VMEM((HEADS // GROUP, KEY_ROW, WIDE), F32),
            pltpu.VMEM((STEP * TOK, WIDE), F32),
            pltpu.VMEM((STEP * TOK, WIDE), F32),
            pltpu.VMEM((STEP * TOK, WIDE), BF16),
            pltpu.VMEM((STEP * TOK, WIDE), BF16),
            pltpu.VMEM((STEP, 1, WIDE), F32),
            pltpu.VMEM((STEP, 1, WIDE), F32),
            pltpu.VMEM((1, WIDE), F32),
            pltpu.VMEM((1, WIDE), F32),
            pltpu.VMEM((4, 2, 8, 2 * SLOT, 2 * SIZE), BF16),
            pltpu.VMEM((8, 4, 2, 2 * SLOT, 2 * SIZE), BF16),
            pltpu.VMEM((4, 8, 2, 2 * SLOT, 2 * SIZE), BF16),
            pltpu.VMEM((2, 4, 64, 4 * SIZE), BF16),
            pltpu.SemaphoreType.DMA((5,)),
            pltpu.SemaphoreType.DMA((8, REACH + 1)),
            pltpu.SemaphoreType.DMA((2, REACH + 1)),
            pltpu.SemaphoreType.DMA((8,)),
            pltpu.SemaphoreType.DMA((8,)),
            pltpu.SemaphoreType.DMA((4,)),
            pltpu.SemaphoreType.DMA((4,)),
            pltpu.SemaphoreType.DMA((3,)),
            pltpu.SemaphoreType.DMA((3,)),
            pltpu.SemaphoreType.DMA((4,)),
            pltpu.SemaphoreType.DMA((4,)),
            pltpu.SemaphoreType.DMA(()),
        ],
        compiler_params=pltpu.CompilerParams(
            collective_id=0, has_side_effects=True, vmem_limit_bytes=40 * 1024 * 1024
        ),
        cost_estimate=pl.CostEstimate(flops=12_000_000_000, bytes_accessed=6_000_000, transcendentals=22_000_000),
        name="attend_and_send",
    )(*(pltpu.with_memory_space_constraint(a, pltpu.HBM) for a in operands))
    return attended, cache.reshape(64 * SLOT, 2048)


def solution(mesh):
    return jax.shard_map(
        on_device,
        mesh=mesh,
        in_specs=(
            P("inst", "head"),
            P("inst", "head"),
            P("inst", "head"),
            P("inst"),
            P("inst", None),
        ),
        out_specs=(P("inst", "head"), P("inst", None)),
        check_vma=False,
    )
```

```python
import functools

import jax
import jax.numpy as jnp
from jax import lax
from jax.experimental import pallas as pl
from jax.experimental.pallas import tpu as pltpu
from jax.sharding import PartitionSpec as P

MESH = pl.DeviceIdType.MESH
F32, BF16 = jnp.float32, jnp.bfloat16

HEADS, SIZE, RATIO = 16, 128, 8
TOK = 256
REACH = 20
SLOT = 8
STEP = 4
KEY_ROW, ALL_ROWS = SIZE + 16, 2 * SIZE + 16
HIDDEN = 1e30
GROUP = 2
WIDE = GROUP * TOK

Z_AFTER = {1: 1, 2: 0, 3: 11, 4: 0, 5: 0, 6: 12, 7: 11}
X_AFTER = {1: 25, 2: 26, 3: 29}
Y_AFTER = {2: 38, 1: 38, 0: 35}
TO_LOG2 = SIZE ** -0.5 * 1.4426950408889634

ARRIVALS = (
    ((16, 215, 308, 109, 214, 307, 101, 206, 102, 213, 17, 305, 18, 310, 212, 311, 204, 103, 20, 19),
     (16, 308, 109, 215, 301, 110, 214, 17, 307, 102, 213, 306, 205, 103, 18, 112, 19, 304, 211, 20)),
    ((16, 101, 308, 215, 117, 307, 214, 110, 213, 309, 102, 103, 305, 212, 18, 19, 306, 211, 204, 20),
     (101, 16, 17, 308, 215, 110, 309, 214, 302, 111, 206, 18, 307, 212, 305, 213, 103, 104, 19, 120)),
    ((16, 101, 308, 215, 17, 307, 214, 102, 109, 18, 306, 213, 111, 310, 212, 103, 305, 104, 19, 20),
     (101, 16, 17, 308, 215, 102, 18, 307, 214, 213, 111, 309, 306, 212, 103, 305, 19, 210, 104, 120)),
    ((16, 101, 308, 215, 17, 102, 307, 214, 18, 103, 309, 213, 110, 19, 205, 112, 311, 206, 104, 120),
     (101, 16, 17, 308, 215, 102, 309, 214, 18, 103, 306, 213, 19, 310, 212, 311, 104, 305, 207, 20)),
    ((16, 101, 308, 215, 17, 102, 307, 214, 18, 309, 103, 306, 204, 310, 19, 20, 311, 213, 205, 212),
     (101, 16, 215, 17, 308, 102, 309, 214, 18, 103, 213, 19, 104, 207, 110, 20, 306, 111, 312, 205)),
    ((101, 16, 17, 215, 308, 307, 102, 205, 309, 18, 103, 214, 306, 19, 104, 213, 110, 20, 212, 311),
     (16, 101, 215, 308, 102, 17, 214, 18, 103, 205, 309, 19, 104, 213, 307, 311, 20, 206, 310, 112)),
    ((101, 16, 308, 17, 206, 102, 18, 309, 215, 307, 103, 310, 214, 19, 104, 213, 311, 212, 20, 105),
     (16, 101, 215, 308, 17, 307, 206, 102, 103, 18, 214, 19, 104, 310, 209, 311, 20, 105, 312, 213)),
    ((207, 16, 101, 308, 102, 17, 309, 18, 215, 103, 214, 19, 213, 306, 104, 310, 212, 311, 20, 105),
     (16, 101, 207, 308, 17, 215, 102, 309, 18, 310, 103, 306, 104, 19, 214, 20, 105, 213, 311, 212)),
    ((308, 16, 215, 101, 207, 317, 102, 213, 103, 18, 309, 314, 19, 206, 310, 212, 104, 205, 111, 20),
     (16, 308, 109, 207, 317, 102, 215, 318, 214, 206, 103, 101, 19, 212, 310, 104, 311, 20, 313, 205)),
    ((16, 308, 101, 215, 109, 17, 214, 102, 207, 213, 318, 103, 104, 19, 206, 310, 20, 311, 212, 205),
     (308, 101, 16, 17, 309, 215, 110, 207, 318, 103, 213, 319, 206, 314, 104, 212, 102, 20, 311, 105)),
    ((16, 101, 308, 215, 17, 309, 214, 102, 207, 110, 18, 103, 213, 319, 206, 104, 212, 105, 320, 311),
     (308, 16, 101, 309, 215, 102, 17, 18, 310, 214, 111, 207, 213, 319, 104, 320, 212, 105, 206, 103)),
    ((16, 308, 101, 215, 102, 17, 309, 18, 207, 310, 214, 103, 111, 213, 19, 206, 104, 212, 320, 105),
     (101, 16, 308, 17, 309, 215, 214, 102, 310, 103, 18, 19, 311, 207, 112, 213, 320, 105, 206, 204)),
    ((16, 308, 101, 215, 17, 309, 214, 102, 207, 103, 18, 310, 19, 213, 311, 104, 206, 312, 20, 205),
     (101, 16, 308, 215, 17, 309, 102, 18, 310, 207, 103, 311, 214, 104, 19, 20, 206, 112, 205, 113)),
    ((101, 16, 308, 215, 17, 309, 207, 102, 214, 18, 310, 103, 313, 104, 19, 311, 206, 20, 205, 212),
     (16, 308, 101, 215, 102, 17, 309, 18, 310, 103, 214, 19, 207, 313, 206, 104, 311, 105, 20, 312)),
    ((16, 308, 101, 309, 215, 102, 17, 18, 314, 310, 207, 103, 206, 19, 213, 104, 311, 105, 20, 312),
     (308, 101, 16, 215, 17, 309, 206, 102, 207, 103, 18, 314, 19, 310, 104, 311, 213, 20, 312, 105)),
    ((308, 101, 16, 207, 17, 215, 309, 102, 310, 103, 214, 18, 19, 311, 220, 104, 312, 213, 105, 106),
     (16, 207, 308, 101, 309, 102, 17, 215, 18, 214, 310, 103, 104, 19, 311, 20, 312, 213, 105, 106)),
)


def offset_of(kind, link):
    y, z = divmod(kind, 8)
    return (16, 1 if z > 0 else -7, -1 if z < 7 else 7, 8 if y == 1 else -8)[link]


def target_of(kind, link):
    y, z = divmod(kind, 8)
    return (kind, y * 8 + (z + 1) % 8, y * 8 + (z + 7) % 8, (1 - y) * 8 + z)[link]


def forward_table():
    table = []
    for kind in range(16):
        halves = []
        for half in range(2):
            held = [0] + [a % 100 for a in ARRIVALS[kind][half]]
            rows = []
            for distance in held:
                row = []
                for link in range(4):
                    there = target_of(kind, link)
                    far = distance + offset_of(there, link)
                    order = ARRIVALS[there][half]
                    wanted = link * 100 + far
                    row.append(order.index(wanted) + 1 if 1 <= far <= REACH and wanted in order else 0)
                rows.append(row)
            halves.append(rows)
        table.append(halves)
    return table


TABLE = forward_table()


def kernel(q_hbm, k_hbm, v_hbm, seg_hbm, own_hbm, out_ref, cache_ref,
           q_own, q_turned, k_own, v_own, own_values, seg_ref, own_ref, kv, bias, top, acc, scores_a, scores_b, weights_a, weights_b,
           peaks_a, peaks_b, shrink_a, shrink_b,
           outgoing, mid, recv, block,
           in_sem, kv_send, kv_recv, z_send, z_recv, x_send, x_recv, y_send, y_recv, c_send, c_recv, own_sem):
    me, g = lax.axis_index("inst"), lax.axis_index("head")
    kind = me % 16
    x, y, z = me // 16, (me // 8) % 2, me % 8
    other_y = x * 16 + (1 - y) * 8 + z
    other_chip, other_core = (g + 2) % 4, g + 1 - 2 * (g % 2)
    near = (
        ((x + 1) % 4) * 16 + kind,
        me - z + (z + 1) % 8,
        me - z + (z + 7) % 8,
        other_y,
    )

    inputs = [
        pltpu.make_async_copy(src, dst, in_sem.at[n])
        for n, (src, dst) in enumerate(
            ((k_hbm, k_own), (v_hbm, v_own), (seg_hbm, seg_ref), (own_hbm, own_ref), (q_hbm, q_own)))
    ]
    for copy in inputs:
        copy.start()

    def along_z(by):
        return (me - z + (z + by) % 8, g)

    def along_x(by):
        return (((x + by) % 4) * 16 + kind, g)

    beside = ((me, other_chip), (other_y, g), (other_y, other_chip))
    sibling = (me, other_core)
    barrier = pltpu.get_barrier_semaphore()
    partners = [along_z(by) for by in range(1, 8)] + [along_x(by) for by in range(1, 4)] + list(beside) + [sibling]
    for partner in partners:
        pl.semaphore_signal(barrier, inc=1, device_id=partner, device_id_type=MESH)

    def pick(values):
        chosen = jnp.int32(values[0])
        if len(set(values)) == 1:
            return chosen
        for t in range(1, 16):
            chosen = jnp.where(kind == t, jnp.int32(values[t]), chosen)
        return chosen

    first = [[pick([TABLE[t][half][0][link] for t in range(16)]) for link in range(4)] for half in range(2)]
    def digits(half, jj, k):
        return [(codes[half][jj][link] >> (6 * k)) & 63 for link in range(4)]

    def forward(half, slot, theres, wait=False):
        for link in range(4):
            there = theres[link]

            @pl.when(there > 0)
            def _():
                copy = pltpu.make_async_remote_copy(
                    src_ref=kv.at[half, slot],
                    dst_ref=kv.at[half, there],
                    send_sem=kv_send.at[half * 4 + link, slot],
                    recv_sem=kv_recv.at[half, there],
                    device_id=(near[link], g),
                    device_id_type=MESH,
                )
                if wait:
                    copy.wait_send()
                else:
                    copy.start()

    def arrive(k, h, j):
        half, jj = j % 2, 2 * h + j // 2
        slot = STEP * k + jj + 1
        here = kv.at[half, slot]
        pltpu.make_async_copy(here, here, kv_recv.at[half, slot]).wait()
        forward(half, slot, digits(half, jj, k))

    def drain(k, half, jj):
        forward(half, STEP * k + jj + 1, digits(half, jj, k), wait=True)

    for copy in inputs[:3]:
        copy.wait()
    at0 = lax.broadcasted_iota(jnp.int32, (TOK, TOK), 0)
    at1 = lax.broadcasted_iota(jnp.int32, (TOK, TOK), 1)
    seg_row = seg_ref[...].astype(F32)
    seg_wide = jnp.broadcast_to(seg_row, (TOK, TOK))
    seg_tall = jnp.broadcast_to(jnp.sum(jnp.where(at0 == at1, seg_wide, 0.0), axis=1, keepdims=True), (TOK, TOK))
    first_seg, last_seg = jnp.min(seg_tall, axis=0, keepdims=True), jnp.max(seg_tall, axis=0, keepdims=True)
    reaches = (seg_row == last_seg).astype(F32)
    extra = lax.broadcasted_iota(jnp.int32, (16, TOK), 0)
    extra_rows = jnp.where(extra == 0, reaches, jnp.where(extra == 1, last_seg, 0.0)).astype(BF16)
    for half in range(2):
        feat = slice(half * SIZE, (half + 1) * SIZE)
        turned = v_own[:, feat].astype(F32).T
        kv[half, 0, 0:SIZE, :] = (turned * reaches).astype(BF16)
        kv[half, 0, SIZE:KEY_ROW, :] = extra_rows
        keys = k_own[:, feat].astype(F32)
        last_key = jnp.broadcast_to(keys[TOK - 1:TOK, :], (TOK, SIZE))
        keys = jnp.where(seg_tall[:, 0:SIZE] == last_seg[:, 0:SIZE], keys, last_key).astype(BF16)
        kv[half, 0, KEY_ROW:ALL_ROWS, 0:SIZE] = keys[0:SIZE]
        kv[half, 0, KEY_ROW:ALL_ROWS, SIZE:TOK] = keys[SIZE:TOK]
    pl.semaphore_wait(barrier, len(partners))
    forward(0, 0, first[0])
    forward(1, 0, first[1])

    codes = [
        [
            [pick([sum(TABLE[t][half][STEP * k + jj + 1][link] * 64 ** k for k in range(5)) for t in range(16)]) for link in range(4)]
            for jj in range(STEP)
        ]
        for half in range(2)
    ]

    for half in range(2):
        own_values[half, 0:SIZE, :] = v_own[:, half * SIZE:(half + 1) * SIZE].astype(F32).T.astype(BF16)
        own_values[half, SIZE:KEY_ROW, :] = jnp.where(extra == 0, 1.0, 0.0).astype(BF16)
    inputs[4].wait()
    for h in range(HEADS):
        turned = q_own[:, h * SIZE:(h + 1) * SIZE].astype(F32).T.astype(BF16)
        q_turned[h // GROUP, :, (h % GROUP) * TOK:(h % GROUP + 1) * TOK] = turned
    bias[...] = jnp.where((at0 <= at1) & (seg_tall == seg_wide), 0.0, -HIDDEN)

    inputs[3].wait()
    dest = own_ref[...]
    owner = lax.broadcasted_iota(jnp.int32, (64, TOK), 0)
    hot = (owner == dest).astype(F32)
    before = (lax.broadcasted_iota(jnp.int32, (TOK, TOK), 0) < lax.broadcasted_iota(jnp.int32, (TOK, TOK), 1)).astype(BF16)
    count = jnp.dot(hot.astype(BF16), before, preferred_element_type=F32)
    place = jnp.sum(hot * count, axis=0, keepdims=True).astype(jnp.int32)
    target = dest * (2 * SLOT) + place
    row = lax.broadcasted_iota(jnp.int32, (1024, TOK), 0)
    of_keys = (row == target).astype(BF16)
    of_values = (row == target + SLOT).astype(BF16)
    rows = jnp.dot(of_keys, k_own[...], preferred_element_type=F32)
    rows += jnp.dot(of_values, v_own[...], preferred_element_type=F32)
    outgoing[...] = rows.astype(BF16).reshape(4, 2, 8, 2 * SLOT, 2 * SIZE)

    def z_copy(by):
        return pltpu.make_async_remote_copy(
            src_ref=outgoing.at[:, :, (z + by) % 8], dst_ref=mid.at[z], send_sem=z_send.at[by], recv_sem=z_recv.at[z],
            device_id=along_z(by), device_id_type=MESH)

    def x_copy(by):
        return pltpu.make_async_remote_copy(
            src_ref=mid.at[:, (x + by) % 4], dst_ref=recv.at[x], send_sem=x_send.at[by], recv_sem=x_recv.at[x],
            device_id=along_x(by), device_id_type=MESH)

    def rows_of(source_y, group):
        return cache_ref.at[:, source_y, :, pl.ds(pl.multiple_of(group * 512, 512), 512)]

    def y_copy(n):
        return pltpu.make_async_remote_copy(
            src_ref=block.at[y if n == 0 else 1 - y], dst_ref=rows_of(y, g), send_sem=y_send.at[n], recv_sem=y_recv.at[n],
            device_id=beside[n], device_id_type=MESH)

    from_y = ((y, other_chip), (1 - y, g), (1 - y, other_chip))

    def c_copy(n):
        if n == 3:
            src, place = block.at[y], rows_of(y, g)
        else:
            src = place = rows_of(*from_y[n])
        return pltpu.make_async_remote_copy(
            src_ref=src, dst_ref=place, send_sem=c_send.at[n], recv_sem=c_recv.at[n],
            device_id=sibling, device_id_type=MESH)

    def own_copy():
        return pltpu.make_async_copy(block.at[y], rows_of(y, g), own_sem)

    def keep_first():
        for i in range(4):
            for j in range(2):
                mid[z, i, j] = outgoing[i, j, z]

    def second_leg():
        for by in range(1, 8):
            src = (z + 8 - by) % 8
            pltpu.make_async_copy(mid.at[src], mid.at[src], z_recv.at[src]).wait()
        for i in range(8):
            recv[x, i] = mid[i, x]

    def third_leg():
        for by in range(1, 4):
            src = (x + 4 - by) % 4
            pltpu.make_async_copy(recv.at[src], recv.at[src], x_recv.at[src]).wait()
        a = lax.broadcasted_iota(jnp.int32, (64, 128), 0)
        b = lax.broadcasted_iota(jnp.int32, (64, 128), 1)
        key_rows = (b == 2 * a - (a & 7)).astype(BF16)
        value_rows = (b == 2 * a - (a & 7) + 8).astype(BF16)
        for src in range(4):
            for j in range(2):
                arrived = recv[src, :, j].reshape(128, 2 * SIZE)
                block[j, src, :, 0:256] = jnp.dot(key_rows, arrived, preferred_element_type=F32).astype(BF16)
                block[j, src, :, 256:512] = jnp.dot(value_rows, arrived, preferred_element_type=F32).astype(BF16)
        c_copy(3).start()
        own_copy().start()

    legs = [(after, z_copy(by).start) for by, after in Z_AFTER.items()]
    legs += [(min(X_AFTER.values()), second_leg)] + [(after, x_copy(by).start) for by, after in X_AFTER.items()]
    legs += [(min(Y_AFTER.values()), third_leg)] + [(after, y_copy(n).start) for n, after in Y_AFTER.items()]

    def legs_at(count):
        return [start for after, start in legs if after == count]

    def fourth_leg():
        for n in range(3):
            here = rows_of(*from_y[n])
            pltpu.make_async_copy(here, here, y_recv.at[n]).wait()
            c_copy(n).start()

    scores_of, weights_of = (scores_a, scores_b), (weights_a, weights_b)
    peaks_of, shrink_of = (peaks_a, peaks_b), (shrink_a, shrink_b)
    first_wide = jnp.concatenate([(seg_row == first_seg).astype(F32)] * GROUP, axis=1)

    def half_of(group):
        return group // (RATIO // GROUP)

    def score(n, group, slots, c):
        half = half_of(group)
        if slots is None:
            keys = k_own[:, half * SIZE:(half + 1) * SIZE]
        else:
            keys = jnp.concatenate([kv[half, slots[c], KEY_ROW:ALL_ROWS, lanes:lanes + SIZE] for lanes in (0, SIZE)], axis=0)
        product = jnp.dot(keys, q_turned[group], preferred_element_type=F32)
        if slots is None:
            product += jnp.concatenate([bias[...]] * GROUP, axis=1)
        scores_of[n % 2][c * TOK:(c + 1) * TOK, :] = product
        peaks_of[n % 2][c] = jnp.max(product, axis=0, keepdims=True)

    def peak_rows(n, group, slots):
        if slots is None:
            top[group] = peaks_of[n % 2][0]
            return [top[group]]
        seen = []
        for slot in slots:
            block_seg = kv[half_of(group), slot, SIZE:KEY_ROW, :].astype(F32)[1:2, :]
            same = jnp.concatenate([(block_seg == first_seg).astype(F32)] * GROUP, axis=1)
            seen.append(same * first_wide > 0.5)
        old = top[group]
        peak = old
        for c in range(len(slots)):
            peak = jnp.maximum(peak, jnp.where(seen[c], peaks_of[n % 2][c], -HIDDEN))
        top[group] = peak
        shrink_of[n % 2][...] = jnp.exp2((old - peak) * TO_LOG2)
        return [jnp.where(seen[c], peak, HIDDEN) for c in range(len(slots))]

    def soften(n, peak, c):
        for at in range(c * TOK, (c + 1) * TOK, 16):
            rows = slice(at, at + 16)
            weights_of[n % 2][rows, :] = jnp.exp2((scores_of[n % 2][rows, :] - peak) * TO_LOG2).astype(BF16)

    def combine(n, group, slots, c):
        values = own_values[half_of(group)] if slots is None else kv[half_of(group), slots[c], 0:KEY_ROW, :]
        product = jnp.dot(values, weights_of[n % 2][c * TOK:(c + 1) * TOK, :], preferred_element_type=F32)
        if slots is None:
            acc[group] = product
        elif c == 0:
            acc[group] = acc[group] * shrink_of[n % 2][...] + product
        else:
            acc[group] += product

    def turn(n, before, now, after):
        peaks = peak_rows(n, *now)
        for c in range(len(peaks)):
            if before is not None:
                combine(n - 1, *before, c)
            if after is not None:
                score(n + 1, *after, c)
            soften(n, peaks[c], c)

    groups = HEADS // GROUP
    turns = [(group, None) for group in range(groups)]
    for start in legs_at(0):
        start()
    keep_first()
    score(0, *turns[0], 0)
    for n in range(groups):
        turn(n, turns[n - 1] if n > 0 else None, turns[n], turns[n + 1] if n + 1 < groups else None)
        arrive(0, n // 4, n % 4)
        for start in legs_at(n + 1):
            start()
    combine(groups - 1, *turns[-1], 0)

    def slots_of(k):
        return [STEP * k + 1 + c for c in range(STEP)]

    for c in range(STEP):
        score(0, 0, slots_of(0), c)

    def step(k, carry):
        turns = [(group, slots_of(k)) for group in range(groups)] + [(0, slots_of(jnp.minimum(k + 1, 4)))]
        for n in range(groups):
            turn(n, turns[n - 1] if n > 0 else None, turns[n], turns[n + 1])
            if n == groups - 1:
                for c in range(STEP):
                    combine(n, *turns[n], c)

            @pl.when(k < 4)
            def _():
                arrive(k + 1, n // 4, n % 4)

            @pl.when(k > 0)
            def _():
                drain(k - 1, n % 2, n // 2)

            for at in range(4):
                starts = legs_at(8 * (at + 1) + n + 1)
                if starts:
                    @pl.when(k == at)
                    def _():
                        for start in starts:
                            start()
        return carry

    lax.fori_loop(0, 5, step, 0)
    fourth_leg()

    for h in range(HEADS):
        group, lanes = h // GROUP, slice((h % GROUP) * TOK, (h % GROUP + 1) * TOK)
        attended = acc[group, 0:SIZE, lanes] * (1.0 / acc[group, SIZE:SIZE + 1, lanes])
        out_ref[:, h * SIZE:(h + 1) * SIZE] = attended.T.astype(BF16)

    for half in range(2):
        forward(half, 0, first[half], wait=True)
        for jj in range(STEP):
            drain(4, half, jj)
    for by in range(1, 8):
        z_copy(by).wait_send()
    for by in range(1, 4):
        x_copy(by).wait_send()
    for n in range(3):
        y_copy(n).wait_send()
    own_copy().wait()
    across = (other_core + 2) % 4
    from_core = ((y, across), (1 - y, other_core), (1 - y, across), (y, other_core))
    for n in range(4):
        c_copy(n).wait_send()
        here = rows_of(*from_core[n])
        pltpu.make_async_copy(here, here, c_recv.at[n]).wait()


def on_device(queries, keys, values, segments, owners):
    whole = pl.BlockSpec(memory_space=pl.ANY)
    operands = (queries, keys, values, segments.reshape(1, TOK), owners.reshape(1, TOK))
    attended, cache = pl.pallas_call(
        kernel,
        out_shape=(
            jax.ShapeDtypeStruct((TOK, HEADS * SIZE), BF16),
            jax.ShapeDtypeStruct((4, 2, 64, 2048), BF16),
        ),
        in_specs=[whole] * 5,
        out_specs=(pl.BlockSpec(memory_space=pltpu.VMEM), whole),
        scratch_shapes=[
            pltpu.VMEM((TOK, HEADS * SIZE), BF16),
            pltpu.VMEM((HEADS // GROUP, SIZE, WIDE), BF16),
            pltpu.VMEM((TOK, 2 * SIZE), BF16),
            pltpu.VMEM((TOK, 2 * SIZE), BF16),
            pltpu.VMEM((2, KEY_ROW, TOK), BF16),
            pltpu.VMEM((1, TOK), jnp.int32),
            pltpu.VMEM((1, TOK), jnp.int32),
            pltpu.VMEM((2, REACH + 1, ALL_ROWS, TOK), BF16),
            pltpu.VMEM((TOK, TOK), F32),
            pltpu.VMEM((HEADS // GROUP, 1, WIDE), F32),
            pltpu.VMEM((HEADS // GROUP, KEY_ROW, WIDE), F32),
            pltpu.VMEM((STEP * TOK, WIDE), F32),
            pltpu.VMEM((STEP * TOK, WIDE), F32),
            pltpu.VMEM((STEP * TOK, WIDE), BF16),
            pltpu.VMEM((STEP * TOK, WIDE), BF16),
            pltpu.VMEM((STEP, 1, WIDE), F32),
            pltpu.VMEM((STEP, 1, WIDE), F32),
            pltpu.VMEM((1, WIDE), F32),
            pltpu.VMEM((1, WIDE), F32),
            pltpu.VMEM((4, 2, 8, 2 * SLOT, 2 * SIZE), BF16),
            pltpu.VMEM((8, 4, 2, 2 * SLOT, 2 * SIZE), BF16),
            pltpu.VMEM((4, 8, 2, 2 * SLOT, 2 * SIZE), BF16),
            pltpu.VMEM((2, 4, 64, 4 * SIZE), BF16),
            pltpu.SemaphoreType.DMA((5,)),
            pltpu.SemaphoreType.DMA((8, REACH + 1)),
            pltpu.SemaphoreType.DMA((2, REACH + 1)),
            pltpu.SemaphoreType.DMA((8,)),
            pltpu.SemaphoreType.DMA((8,)),
            pltpu.SemaphoreType.DMA((4,)),
            pltpu.SemaphoreType.DMA((4,)),
            pltpu.SemaphoreType.DMA((3,)),
            pltpu.SemaphoreType.DMA((3,)),
            pltpu.SemaphoreType.DMA((4,)),
            pltpu.SemaphoreType.DMA((4,)),
            pltpu.SemaphoreType.DMA(()),
        ],
        compiler_params=pltpu.CompilerParams(
            collective_id=0, has_side_effects=True, vmem_limit_bytes=40 * 1024 * 1024
        ),
        cost_estimate=pl.CostEstimate(flops=12_000_000_000, bytes_accessed=6_000_000, transcendentals=22_000_000),
        name="attend_and_send",
    )(*(pltpu.with_memory_space_constraint(a, pltpu.HBM) for a in operands))
    return attended, cache.reshape(64 * SLOT, 2048)


def solution(mesh):
    return jax.shard_map(
        on_device,
        mesh=mesh,
        in_specs=(
            P("inst", "head"),
            P("inst", "head"),
            P("inst", "head"),
            P("inst"),
            P("inst", None),
        ),
        out_specs=(P("inst", "head"), P("inst", None)),
        check_vma=False,
    )
```

```python
import functools

import jax
import jax.numpy as jnp
from jax import lax
from jax.experimental import pallas as pl
from jax.experimental.pallas import tpu as pltpu
from jax.sharding import PartitionSpec as P

MESH = pl.DeviceIdType.MESH
F32, BF16 = jnp.float32, jnp.bfloat16

HEADS, SIZE, RATIO = 16, 128, 8
TOK = 256
REACH = 20
SLOT = 8
STEP = 4
KEY_ROW, ALL_ROWS = SIZE + 16, 2 * SIZE + 16
HIDDEN = 1e30
GROUP = 2
WIDE = GROUP * TOK

Z_AFTER = {7: 0, 1: 0, 5: 0, 3: 0, 6: 4, 4: 4, 2: 9}
X_AFTER = {2: 18, 1: 21, 3: 22}
Y_AFTER = {0: 30, 1: 32, 2: 33}
TO_LOG2 = SIZE ** -0.5 * 1.4426950408889634

ARRIVALS = (
    ((215, 109, 101, 16, 206, 307, 308, 205, 102, 310, 18, 213, 17, 111, 204, 203, 214, 20, 19, 112),
     (109, 215, 207, 301, 102, 110, 103, 206, 17, 16, 308, 214, 19, 205, 111, 304, 18, 213, 20, 112)),
    ((101, 16, 307, 213, 110, 215, 206, 102, 205, 17, 308, 214, 309, 204, 312, 18, 20, 111, 303, 219),
     (101, 16, 308, 110, 307, 214, 17, 302, 103, 215, 111, 19, 206, 304, 309, 305, 213, 212, 18, 120)),
    ((16, 101, 214, 102, 307, 206, 215, 103, 305, 111, 309, 19, 17, 204, 213, 208, 110, 20, 312, 18),
     (16, 101, 102, 215, 308, 214, 307, 309, 306, 104, 213, 17, 18, 112, 303, 305, 120, 110, 219, 211)),
    ((101, 215, 207, 16, 102, 306, 103, 108, 18, 214, 305, 213, 309, 104, 112, 120, 311, 19, 17, 210),
     (101, 16, 215, 102, 17, 103, 18, 214, 309, 308, 306, 307, 311, 304, 212, 20, 113, 210, 105, 19)),
    ((16, 101, 308, 17, 215, 102, 103, 104, 214, 19, 306, 309, 311, 307, 205, 113, 110, 18, 312, 120),
     (101, 16, 215, 17, 102, 103, 213, 18, 19, 206, 204, 311, 214, 109, 312, 20, 205, 207, 108, 210)),
    ((16, 101, 102, 206, 215, 103, 308, 310, 17, 19, 104, 205, 211, 120, 307, 218, 109, 112, 114, 213),
     (16, 102, 214, 101, 307, 215, 205, 104, 218, 309, 208, 311, 306, 20, 17, 119, 203, 112, 113, 310)),
    ((101, 102, 16, 207, 308, 17, 215, 206, 303, 104, 212, 19, 305, 310, 111, 18, 214, 120, 213, 109),
     (101, 215, 103, 16, 307, 19, 206, 102, 17, 309, 308, 310, 18, 105, 204, 213, 112, 214, 211, 20)),
    ((16, 101, 102, 308, 207, 103, 309, 18, 213, 306, 215, 212, 214, 19, 310, 17, 304, 105, 111, 220),
     (16, 101, 207, 17, 309, 310, 102, 214, 103, 18, 104, 305, 213, 308, 215, 119, 212, 306, 20, 211)),
    ((16, 215, 207, 101, 308, 103, 102, 213, 19, 18, 314, 206, 104, 17, 205, 111, 309, 112, 210, 20),
     (308, 16, 109, 207, 214, 317, 102, 206, 315, 311, 103, 310, 18, 212, 101, 104, 19, 105, 20, 213)),
    ((16, 101, 308, 215, 214, 206, 17, 104, 309, 207, 102, 313, 20, 211, 103, 318, 105, 19, 210, 112),
     (16, 308, 101, 215, 110, 207, 117, 213, 318, 103, 309, 212, 311, 214, 319, 104, 20, 105, 206, 202)),
    ((16, 101, 215, 102, 207, 308, 213, 314, 17, 212, 204, 209, 103, 311, 20, 110, 205, 319, 18, 106),
     (16, 101, 215, 117, 308, 102, 214, 309, 111, 213, 104, 207, 310, 312, 203, 120, 205, 206, 118, 19)),
    ((16, 308, 101, 102, 214, 215, 213, 17, 205, 103, 310, 311, 309, 206, 19, 207, 104, 118, 212, 20),
     (16, 101, 215, 102, 17, 309, 214, 103, 308, 19, 310, 206, 112, 204, 207, 105, 20, 113, 18, 111)),
    ((16, 101, 215, 17, 214, 102, 206, 103, 207, 19, 308, 104, 209, 18, 311, 112, 20, 213, 210, 105),
     (101, 16, 102, 215, 18, 308, 207, 309, 103, 104, 214, 19, 205, 206, 120, 311, 17, 312, 213, 310)),
    ((16, 101, 215, 207, 308, 310, 102, 103, 18, 104, 311, 314, 309, 213, 212, 206, 105, 19, 17, 120),
     (101, 16, 17, 310, 308, 215, 102, 103, 206, 207, 19, 104, 214, 313, 312, 105, 309, 211, 118, 20)),
    ((16, 308, 101, 102, 18, 17, 111, 213, 103, 314, 207, 215, 210, 309, 105, 312, 104, 320, 106, 219),
     (16, 101, 308, 215, 207, 217, 102, 314, 311, 18, 103, 209, 310, 104, 206, 212, 105, 113, 20, 19)),
    ((308, 16, 309, 101, 310, 207, 17, 214, 311, 103, 102, 112, 118, 104, 19, 320, 213, 105, 106, 215),
     (101, 16, 102, 17, 18, 308, 309, 214, 207, 310, 315, 213, 311, 103, 312, 105, 104, 106, 19, 20)),
)


def offset_of(kind, link):
    y, z = divmod(kind, 8)
    return (16, 1 if z > 0 else -7, -1 if z < 7 else 7, 8 if y == 1 else -8)[link]


def target_of(kind, link):
    y, z = divmod(kind, 8)
    return (kind, y * 8 + (z + 1) % 8, y * 8 + (z + 7) % 8, (1 - y) * 8 + z)[link]


def forward_table():
    table = []
    for kind in range(16):
        halves = []
        for half in range(2):
            held = [0] + [a % 100 for a in ARRIVALS[kind][half]]
            rows = []
            for distance in held:
                row = []
                for link in range(4):
                    there = target_of(kind, link)
                    far = distance + offset_of(there, link)
                    order = ARRIVALS[there][half]
                    wanted = link * 100 + far
                    row.append(order.index(wanted) + 1 if 1 <= far <= REACH and wanted in order else 0)
                rows.append(row)
            halves.append(rows)
        table.append(halves)
    return table


TABLE = forward_table()


def kernel(q_hbm, k_hbm, v_hbm, seg_hbm, own_hbm, out_ref, cache_ref,
           q_own, q_turned, k_own, v_own, own_values, seg_ref, own_ref, kv, bias, top, acc, scores_a, scores_b, weights_a, weights_b,
           peaks_a, peaks_b, shrink_a, shrink_b,
           outgoing, mid, recv, block,
           in_sem, kv_send, kv_recv, z_send, z_recv, x_send, x_recv, y_send, y_recv, c_send, c_recv, own_sem):
    me, g = lax.axis_index("inst"), lax.axis_index("head")
    kind = me % 16
    x, y, z = me // 16, (me // 8) % 2, me % 8
    other_y = x * 16 + (1 - y) * 8 + z
    other_chip, other_core = (g + 2) % 4, g + 1 - 2 * (g % 2)
    near = (
        ((x + 1) % 4) * 16 + kind,
        me - z + (z + 1) % 8,
        me - z + (z + 7) % 8,
        other_y,
    )

    inputs = [
        pltpu.make_async_copy(src, dst, in_sem.at[n])
        for n, (src, dst) in enumerate(
            ((k_hbm, k_own), (v_hbm, v_own), (seg_hbm, seg_ref), (own_hbm, own_ref), (q_hbm, q_own)))
    ]
    for copy in inputs:
        copy.start()

    def along_z(by):
        return (me - z + (z + by) % 8, g)

    def along_x(by):
        return (((x + by) % 4) * 16 + kind, g)

    beside = ((me, other_chip), (other_y, g), (other_y, other_chip))
    sibling = (me, other_core)
    barrier = pltpu.get_barrier_semaphore()
    partners = [along_z(by) for by in range(1, 8)] + [along_x(by) for by in range(1, 4)] + list(beside) + [sibling]
    for partner in partners:
        pl.semaphore_signal(barrier, inc=1, device_id=partner, device_id_type=MESH)

    def pick(values):
        chosen = jnp.int32(values[0])
        if len(set(values)) == 1:
            return chosen
        for t in range(1, 16):
            chosen = jnp.where(kind == t, jnp.int32(values[t]), chosen)
        return chosen

    first = [[pick([TABLE[t][half][0][link] for t in range(16)]) for link in range(4)] for half in range(2)]
    def digits(half, jj, k):
        return [(codes[half][jj][link] >> (6 * k)) & 63 for link in range(4)]

    def forward(half, slot, theres, wait=False):
        for link in range(4):
            there = theres[link]

            @pl.when(there > 0)
            def _():
                copy = pltpu.make_async_remote_copy(
                    src_ref=kv.at[half, slot],
                    dst_ref=kv.at[half, there],
                    send_sem=kv_send.at[half * 4 + link, slot],
                    recv_sem=kv_recv.at[half, there],
                    device_id=(near[link], g),
                    device_id_type=MESH,
                )
                if wait:
                    copy.wait_send()
                else:
                    copy.start()

    def arrive(k, h, j):
        half, jj = j % 2, 2 * h + j // 2
        slot = STEP * k + jj + 1
        here = kv.at[half, slot]
        pltpu.make_async_copy(here, here, kv_recv.at[half, slot]).wait()
        forward(half, slot, digits(half, jj, k))

    def drain(k, half, jj):
        forward(half, STEP * k + jj + 1, digits(half, jj, k), wait=True)

    for copy in inputs[:3]:
        copy.wait()
    at0 = lax.broadcasted_iota(jnp.int32, (TOK, TOK), 0)
    at1 = lax.broadcasted_iota(jnp.int32, (TOK, TOK), 1)
    seg_row = seg_ref[...].astype(F32)
    seg_wide = jnp.broadcast_to(seg_row, (TOK, TOK))
    seg_tall = jnp.broadcast_to(jnp.sum(jnp.where(at0 == at1, seg_wide, 0.0), axis=1, keepdims=True), (TOK, TOK))
    first_seg, last_seg = jnp.min(seg_tall, axis=0, keepdims=True), jnp.max(seg_tall, axis=0, keepdims=True)
    reaches = (seg_row == last_seg).astype(F32)
    extra = lax.broadcasted_iota(jnp.int32, (16, TOK), 0)
    extra_rows = jnp.where(extra == 0, reaches, jnp.where(extra == 1, last_seg, 0.0)).astype(BF16)
    for half in range(2):
        feat = slice(half * SIZE, (half + 1) * SIZE)
        turned = v_own[:, feat].astype(F32).T
        kv[half, 0, 0:SIZE, :] = (turned * reaches).astype(BF16)
        kv[half, 0, SIZE:KEY_ROW, :] = extra_rows
        keys = k_own[:, feat].astype(F32)
        last_key = jnp.broadcast_to(keys[TOK - 1:TOK, :], (TOK, SIZE))
        keys = jnp.where(seg_tall[:, 0:SIZE] == last_seg[:, 0:SIZE], keys, last_key).astype(BF16)
        kv[half, 0, KEY_ROW:ALL_ROWS, 0:SIZE] = keys[0:SIZE]
        kv[half, 0, KEY_ROW:ALL_ROWS, SIZE:TOK] = keys[SIZE:TOK]
        if half == 0:
            pl.semaphore_wait(barrier, len(partners))
        forward(half, 0, first[half])

    codes = [
        [
            [pick([sum(TABLE[t][half][STEP * k + jj + 1][link] * 64 ** k for k in range(5)) for t in range(16)]) for link in range(4)]
            for jj in range(STEP)
        ]
        for half in range(2)
    ]

    for half in range(2):
        own_values[half, 0:SIZE, :] = v_own[:, half * SIZE:(half + 1) * SIZE].astype(F32).T.astype(BF16)
        own_values[half, SIZE:KEY_ROW, :] = jnp.where(extra == 0, 1.0, 0.0).astype(BF16)
    inputs[4].wait()
    for h in range(HEADS):
        turned = q_own[:, h * SIZE:(h + 1) * SIZE].astype(F32).T.astype(BF16)
        q_turned[h // GROUP, :, (h % GROUP) * TOK:(h % GROUP + 1) * TOK] = turned
    bias[...] = jnp.where((at0 <= at1) & (seg_tall == seg_wide), 0.0, -HIDDEN)

    inputs[3].wait()
    dest = own_ref[...]
    owner = lax.broadcasted_iota(jnp.int32, (64, TOK), 0)
    hot = (owner == dest).astype(F32)
    before = (lax.broadcasted_iota(jnp.int32, (TOK, TOK), 0) < lax.broadcasted_iota(jnp.int32, (TOK, TOK), 1)).astype(BF16)
    count = jnp.dot(hot.astype(BF16), before, preferred_element_type=F32)
    place = jnp.sum(hot * count, axis=0, keepdims=True).astype(jnp.int32)
    target = dest * (2 * SLOT) + place
    row = lax.broadcasted_iota(jnp.int32, (1024, TOK), 0)
    of_keys = (row == target).astype(BF16)
    of_values = (row == target + SLOT).astype(BF16)
    rows = jnp.dot(of_keys, k_own[...], preferred_element_type=F32)
    rows += jnp.dot(of_values, v_own[...], preferred_element_type=F32)
    outgoing[...] = rows.astype(BF16).reshape(4, 2, 8, 2 * SLOT, 2 * SIZE)

    def z_copy(by):
        return pltpu.make_async_remote_copy(
            src_ref=outgoing.at[:, :, (z + by) % 8], dst_ref=mid.at[z], send_sem=z_send.at[by], recv_sem=z_recv.at[z],
            device_id=along_z(by), device_id_type=MESH)

    def x_copy(by):
        return pltpu.make_async_remote_copy(
            src_ref=mid.at[:, (x + by) % 4], dst_ref=recv.at[x], send_sem=x_send.at[by], recv_sem=x_recv.at[x],
            device_id=along_x(by), device_id_type=MESH)

    def rows_of(source_y, group):
        return cache_ref.at[:, source_y, :, pl.ds(pl.multiple_of(group * 512, 512), 512)]

    def y_copy(n):
        return pltpu.make_async_remote_copy(
            src_ref=block.at[y if n == 0 else 1 - y], dst_ref=rows_of(y, g), send_sem=y_send.at[n], recv_sem=y_recv.at[n],
            device_id=beside[n], device_id_type=MESH)

    from_y = ((y, other_chip), (1 - y, g), (1 - y, other_chip))

    def c_copy(n):
        if n == 3:
            src, place = block.at[y], rows_of(y, g)
        else:
            src = place = rows_of(*from_y[n])
        return pltpu.make_async_remote_copy(
            src_ref=src, dst_ref=place, send_sem=c_send.at[n], recv_sem=c_recv.at[n],
            device_id=sibling, device_id_type=MESH)

    def own_copy():
        return pltpu.make_async_copy(block.at[y], rows_of(y, g), own_sem)

    def keep_first():
        for i in range(4):
            for j in range(2):
                mid[z, i, j] = outgoing[i, j, z]

    def second_leg():
        for by in range(1, 8):
            src = (z + 8 - by) % 8
            pltpu.make_async_copy(mid.at[src], mid.at[src], z_recv.at[src]).wait()
        for i in range(8):
            recv[x, i] = mid[i, x]

    def third_leg():
        for by in range(1, 4):
            src = (x + 4 - by) % 4
            pltpu.make_async_copy(recv.at[src], recv.at[src], x_recv.at[src]).wait()
        a = lax.broadcasted_iota(jnp.int32, (64, 128), 0)
        b = lax.broadcasted_iota(jnp.int32, (64, 128), 1)
        key_rows = (b == 2 * a - (a & 7)).astype(BF16)
        value_rows = (b == 2 * a - (a & 7) + 8).astype(BF16)
        for src in range(4):
            for j in range(2):
                arrived = recv[src, :, j].reshape(128, 2 * SIZE)
                block[j, src, :, 0:256] = jnp.dot(key_rows, arrived, preferred_element_type=F32).astype(BF16)
                block[j, src, :, 256:512] = jnp.dot(value_rows, arrived, preferred_element_type=F32).astype(BF16)
        c_copy(3).start()
        own_copy().start()

    legs = [(after, z_copy(by).start) for by, after in Z_AFTER.items()]
    legs += [(min(X_AFTER.values()), second_leg)] + [(after, x_copy(by).start) for by, after in X_AFTER.items()]
    legs += [(min(Y_AFTER.values()), third_leg)] + [(after, y_copy(n).start) for n, after in Y_AFTER.items()]

    def legs_at(count):
        return [start for after, start in legs if after == count]

    def fourth_leg():
        for n in range(3):
            here = rows_of(*from_y[n])
            pltpu.make_async_copy(here, here, y_recv.at[n]).wait()
            c_copy(n).start()

    scores_of, weights_of = (scores_a, scores_b), (weights_a, weights_b)
    peaks_of, shrink_of = (peaks_a, peaks_b), (shrink_a, shrink_b)
    first_wide = jnp.concatenate([(seg_row == first_seg).astype(F32)] * GROUP, axis=1)

    def half_of(group):
        return group // (RATIO // GROUP)

    def score(n, group, slots, c):
        half = half_of(group)
        if slots is None:
            keys = k_own[:, half * SIZE:(half + 1) * SIZE]
        else:
            keys = jnp.concatenate([kv[half, slots[c], KEY_ROW:ALL_ROWS, lanes:lanes + SIZE] for lanes in (0, SIZE)], axis=0)
        product = jnp.dot(keys, q_turned[group], preferred_element_type=F32)
        if slots is None:
            product += jnp.concatenate([bias[...]] * GROUP, axis=1)
        scores_of[n % 2][c * TOK:(c + 1) * TOK, :] = product
        peaks_of[n % 2][c] = jnp.max(product, axis=0, keepdims=True)

    def peak_rows(n, group, slots):
        if slots is None:
            top[group] = peaks_of[n % 2][0]
            return [top[group]]
        seen = []
        for slot in slots:
            block_seg = kv[half_of(group), slot, SIZE:KEY_ROW, :].astype(F32)[1:2, :]
            same = jnp.concatenate([(block_seg == first_seg).astype(F32)] * GROUP, axis=1)
            seen.append(same * first_wide > 0.5)
        old = top[group]
        peak = old
        for c in range(len(slots)):
            peak = jnp.maximum(peak, jnp.where(seen[c], peaks_of[n % 2][c], -HIDDEN))
        top[group] = peak
        shrink_of[n % 2][...] = jnp.exp2((old - peak) * TO_LOG2)
        return [jnp.where(seen[c], peak, HIDDEN) for c in range(len(slots))]

    def soften(n, peak, c):
        for at in range(c * TOK, (c + 1) * TOK, 16):
            rows = slice(at, at + 16)
            weights_of[n % 2][rows, :] = jnp.exp2((scores_of[n % 2][rows, :] - peak) * TO_LOG2).astype(BF16)

    def combine(n, group, slots, c):
        values = own_values[half_of(group)] if slots is None else kv[half_of(group), slots[c], 0:KEY_ROW, :]
        product = jnp.dot(values, weights_of[n % 2][c * TOK:(c + 1) * TOK, :], preferred_element_type=F32)
        if slots is None:
            acc[group] = product
        elif c == 0:
            acc[group] = acc[group] * shrink_of[n % 2][...] + product
        else:
            acc[group] += product

    def turn(n, before, now, after):
        peaks = peak_rows(n, *now)
        for c in range(len(peaks)):
            if before is not None:
                combine(n - 1, *before, c)
            if after is not None:
                score(n + 1, *after, c)
            soften(n, peaks[c], c)

    groups = HEADS // GROUP
    turns = [(group, None) for group in range(groups)]
    for start in legs_at(0):
        start()
    keep_first()
    score(0, *turns[0], 0)
    for n in range(groups):
        turn(n, turns[n - 1] if n > 0 else None, turns[n], turns[n + 1] if n + 1 < groups else None)
        arrive(0, n // 4, n % 4)
        for start in legs_at(n + 1):
            start()
    combine(groups - 1, *turns[-1], 0)

    def slots_of(k):
        return [STEP * k + 1 + c for c in range(STEP)]

    for c in range(STEP):
        score(0, 0, slots_of(0), c)

    def start_legs(count):
        for start in legs_at(count):
            start()

    def step(k, carry):
        ahead = [jnp.minimum(STEP * (k + 1) + 1 + c, 18) for c in range(STEP)]
        turns = [(group, slots_of(k)) for group in range(groups)] + [(0, ahead)]
        for n in range(groups):
            turn(n, turns[n - 1] if n > 0 else None, turns[n], turns[n + 1])
            if n == groups - 1:
                for c in range(STEP):
                    combine(n, *turns[n], c)

            @pl.when(k < 3)
            def _():
                arrive(k + 1, n // 4, n % 4)

            @pl.when(k > 0)
            def _():
                drain(k - 1, n % 2, n // 2)

            for at in range(3):
                if legs_at(8 * (at + 1) + n + 1):
                    @pl.when(k == at)
                    def _():
                        start_legs(8 * (at + 1) + n + 1)

            @pl.when(k == 3)
            def _():
                if n % 2 == 1:
                    arrive(4, 0, n // 2)
                    start_legs(33 + n // 2)
                drain(3, n % 2, n // 2)
                if n == groups - 2:
                    for half in range(2):
                        forward(half, 0, first[half], wait=True)
                    for by in range(1, 8):
                        z_copy(by).wait_send()
        return carry

    def short_step(m, carry):
        turns = [(group, [17 + 2 * m, 18 + 2 * m]) for group in range(groups)] + [(0, [19, 20])]
        for n in range(groups):
            turn(n, turns[n - 1] if n > 0 else None, turns[n], turns[n + 1])
            if n == groups - 1:
                for c in range(2):
                    combine(n, *turns[n], c)
            if n % 2 == 1:
                @pl.when(m == 0)
                def _():
                    arrive(4, 1, n // 2)
                    start_legs(37 + n // 2)
        return carry

    lax.fori_loop(0, 4, step, 0)
    lax.fori_loop(0, 2, short_step, 0)
    fourth_leg()

    for h in range(HEADS):
        group, lanes = h // GROUP, slice((h % GROUP) * TOK, (h % GROUP + 1) * TOK)
        attended = acc[group, 0:SIZE, lanes] * (1.0 / acc[group, SIZE:SIZE + 1, lanes])
        out_ref[:, h * SIZE:(h + 1) * SIZE] = attended.T.astype(BF16)

    for half in range(2):
        for jj in range(STEP):
            drain(4, half, jj)
    for by in range(1, 4):
        x_copy(by).wait_send()
    for n in range(3):
        y_copy(n).wait_send()
    own_copy().wait()
    across = (other_core + 2) % 4
    from_core = ((y, across), (1 - y, other_core), (1 - y, across), (y, other_core))
    for n in range(4):
        c_copy(n).wait_send()
        here = rows_of(*from_core[n])
        pltpu.make_async_copy(here, here, c_recv.at[n]).wait()


def on_device(queries, keys, values, segments, owners):
    whole = pl.BlockSpec(memory_space=pl.ANY)
    operands = (queries, keys, values, segments.reshape(1, TOK), owners.reshape(1, TOK))
    attended, cache = pl.pallas_call(
        kernel,
        out_shape=(
            jax.ShapeDtypeStruct((TOK, HEADS * SIZE), BF16),
            jax.ShapeDtypeStruct((4, 2, 64, 2048), BF16),
        ),
        in_specs=[whole] * 5,
        out_specs=(pl.BlockSpec(memory_space=pltpu.VMEM), whole),
        scratch_shapes=[
            pltpu.VMEM((TOK, HEADS * SIZE), BF16),
            pltpu.VMEM((HEADS // GROUP, SIZE, WIDE), BF16),
            pltpu.VMEM((TOK, 2 * SIZE), BF16),
            pltpu.VMEM((TOK, 2 * SIZE), BF16),
            pltpu.VMEM((2, KEY_ROW, TOK), BF16),
            pltpu.VMEM((1, TOK), jnp.int32),
            pltpu.VMEM((1, TOK), jnp.int32),
            pltpu.VMEM((2, REACH + 1, ALL_ROWS, TOK), BF16),
            pltpu.VMEM((TOK, TOK), F32),
            pltpu.VMEM((HEADS // GROUP, 1, WIDE), F32),
            pltpu.VMEM((HEADS // GROUP, KEY_ROW, WIDE), F32),
            pltpu.VMEM((STEP * TOK, WIDE), F32),
            pltpu.VMEM((STEP * TOK, WIDE), F32),
            pltpu.VMEM((STEP * TOK, WIDE), BF16),
            pltpu.VMEM((STEP * TOK, WIDE), BF16),
            pltpu.VMEM((STEP, 1, WIDE), F32),
            pltpu.VMEM((STEP, 1, WIDE), F32),
            pltpu.VMEM((1, WIDE), F32),
            pltpu.VMEM((1, WIDE), F32),
            pltpu.VMEM((4, 2, 8, 2 * SLOT, 2 * SIZE), BF16),
            pltpu.VMEM((8, 4, 2, 2 * SLOT, 2 * SIZE), BF16),
            pltpu.VMEM((4, 8, 2, 2 * SLOT, 2 * SIZE), BF16),
            pltpu.VMEM((2, 4, 64, 4 * SIZE), BF16),
            pltpu.SemaphoreType.DMA((5,)),
            pltpu.SemaphoreType.DMA((8, REACH + 1)),
            pltpu.SemaphoreType.DMA((2, REACH + 1)),
            pltpu.SemaphoreType.DMA((8,)),
            pltpu.SemaphoreType.DMA((8,)),
            pltpu.SemaphoreType.DMA((4,)),
            pltpu.SemaphoreType.DMA((4,)),
            pltpu.SemaphoreType.DMA((3,)),
            pltpu.SemaphoreType.DMA((3,)),
            pltpu.SemaphoreType.DMA((4,)),
            pltpu.SemaphoreType.DMA((4,)),
            pltpu.SemaphoreType.DMA(()),
        ],
        compiler_params=pltpu.CompilerParams(
            collective_id=0, has_side_effects=True, vmem_limit_bytes=40 * 1024 * 1024
        ),
        cost_estimate=pl.CostEstimate(flops=12_000_000_000, bytes_accessed=6_000_000, transcendentals=22_000_000),
        name="attend_and_send",
    )(*(pltpu.with_memory_space_constraint(a, pltpu.HBM) for a in operands))
    return attended, cache.reshape(64 * SLOT, 2048)


def solution(mesh):
    return jax.shard_map(
        on_device,
        mesh=mesh,
        in_specs=(
            P("inst", "head"),
            P("inst", "head"),
            P("inst", "head"),
            P("inst"),
            P("inst", None),
        ),
        out_specs=(P("inst", "head"), P("inst", None)),
        check_vma=False,
    )
```

```python
import functools

import jax
import jax.numpy as jnp
from jax import lax
from jax.experimental import pallas as pl
from jax.experimental.pallas import tpu as pltpu
from jax.sharding import PartitionSpec as P

MESH = pl.DeviceIdType.MESH
F32, BF16 = jnp.float32, jnp.bfloat16

HEADS, SIZE, RATIO = 16, 128, 8
TOK = 256
REACH = 20
SLOT = 8
STEP = 4
KEY_ROW, ALL_ROWS = SIZE + 16, 2 * SIZE + 16
HIDDEN = 1e30
GROUP = 2
WIDE = GROUP * TOK

Z_AFTER = {2: 0, 5: 0, 4: 0, 1: 1, 7: 11, 3: 11, 6: 12}
X_AFTER = {1: 25, 2: 26, 3: 29}
Y_AFTER = {0: 35, 2: 38, 1: 38}
TO_LOG2 = SIZE ** -0.5 * 1.4426950408889634

ARRIVALS = (
    ((16, 215, 308, 109, 214, 307, 101, 206, 102, 213, 17, 305, 18, 310, 212, 311, 204, 103, 20, 19),
     (16, 308, 109, 215, 301, 110, 214, 17, 307, 102, 213, 306, 205, 103, 18, 112, 19, 304, 211, 20)),
    ((16, 101, 308, 215, 117, 307, 214, 110, 213, 309, 102, 103, 305, 212, 18, 19, 306, 211, 204, 20),
     (101, 16, 17, 308, 215, 110, 309, 214, 302, 111, 206, 18, 307, 212, 305, 213, 103, 104, 19, 120)),
    ((16, 101, 308, 215, 17, 307, 214, 102, 109, 18, 306, 213, 111, 310, 212, 103, 305, 104, 19, 20),
     (101, 16, 17, 308, 215, 102, 18, 307, 214, 213, 111, 309, 306, 212, 103, 305, 19, 210, 104, 120)),
    ((16, 101, 308, 215, 17, 102, 307, 214, 18, 103, 309, 213, 110, 19, 205, 112, 311, 206, 104, 120),
     (101, 16, 17, 308, 215, 102, 309, 214, 18, 103, 306, 213, 19, 310, 212, 311, 104, 305, 207, 20)),
    ((16, 101, 308, 215, 17, 102, 307, 214, 18, 309, 103, 306, 204, 310, 19, 20, 311, 213, 205, 212),
     (101, 16, 215, 17, 308, 102, 309, 214, 18, 103, 213, 19, 104, 207, 110, 20, 306, 111, 312, 205)),
    ((101, 16, 17, 215, 308, 307, 102, 205, 309, 18, 103, 214, 306, 19, 104, 213, 110, 20, 212, 311),
     (16, 101, 215, 308, 102, 17, 214, 18, 103, 205, 309, 19, 104, 213, 307, 311, 20, 206, 310, 112)),
    ((101, 16, 308, 17, 206, 102, 18, 309, 215, 307, 103, 310, 214, 19, 104, 213, 311, 212, 20, 105),
     (16, 101, 215, 308, 17, 307, 206, 102, 103, 18, 214, 19, 104, 310, 209, 311, 20, 105, 312, 213)),
    ((207, 16, 101, 308, 102, 17, 309, 18, 215, 103, 214, 19, 213, 306, 104, 310, 212, 311, 20, 105),
     (16, 101, 207, 308, 17, 215, 102, 309, 18, 310, 103, 306, 104, 19, 214, 20, 105, 213, 311, 212)),
    ((308, 16, 215, 101, 207, 317, 102, 213, 103, 18, 309, 314, 19, 206, 310, 212, 104, 205, 111, 20),
     (16, 308, 109, 207, 317, 102, 215, 318, 214, 206, 103, 101, 19, 212, 310, 104, 311, 20, 313, 205)),
    ((16, 308, 101, 215, 109, 17, 214, 102, 207, 213, 318, 103, 104, 19, 206, 310, 20, 311, 212, 205),
     (308, 101, 16, 17, 309, 215, 110, 207, 318, 103, 213, 319, 206, 314, 104, 212, 102, 20, 311, 105)),
    ((16, 101, 308, 215, 17, 309, 214, 102, 207, 110, 18, 103, 213, 319, 206, 104, 212, 105, 320, 311),
     (308, 16, 101, 309, 215, 102, 17, 18, 310, 214, 111, 207, 213, 319, 104, 320, 212, 105, 206, 103)),
    ((16, 308, 101, 215, 102, 17, 309, 18, 207, 310, 214, 103, 111, 213, 19, 206, 104, 212, 320, 105),
     (101, 16, 308, 17, 309, 215, 214, 102, 310, 103, 18, 19, 311, 207, 112, 213, 320, 105, 206, 204)),
    ((16, 308, 101, 215, 17, 309, 214, 102, 207, 103, 18, 310, 19, 213, 311, 104, 206, 312, 20, 205),
     (101, 16, 308, 215, 17, 309, 102, 18, 310, 207, 103, 311, 214, 104, 19, 20, 206, 112, 205, 113)),
    ((101, 16, 308, 215, 17, 309, 207, 102, 214, 18, 310, 103, 313, 104, 19, 311, 206, 20, 205, 212),
     (16, 308, 101, 215, 102, 17, 309, 18, 310, 103, 214, 19, 207, 313, 206, 104, 311, 105, 20, 312)),
    ((16, 308, 101, 309, 215, 102, 17, 18, 314, 310, 207, 103, 206, 19, 213, 104, 311, 105, 20, 312),
     (308, 101, 16, 215, 17, 309, 206, 102, 207, 103, 18, 314, 19, 310, 104, 311, 213, 20, 312, 105)),
    ((308, 101, 16, 207, 17, 215, 309, 102, 310, 103, 214, 18, 19, 311, 220, 104, 312, 213, 105, 106),
     (16, 207, 308, 101, 309, 102, 17, 215, 18, 214, 310, 103, 104, 19, 311, 20, 312, 213, 105, 106)),
)


def offset_of(kind, link):
    y, z = divmod(kind, 8)
    return (16, 1 if z > 0 else -7, -1 if z < 7 else 7, 8 if y == 1 else -8)[link]


def target_of(kind, link):
    y, z = divmod(kind, 8)
    return (kind, y * 8 + (z + 1) % 8, y * 8 + (z + 7) % 8, (1 - y) * 8 + z)[link]


def forward_table():
    table = []
    for kind in range(16):
        halves = []
        for half in range(2):
            held = [0] + [a % 100 for a in ARRIVALS[kind][half]]
            rows = []
            for distance in held:
                row = []
                for link in range(4):
                    there = target_of(kind, link)
                    far = distance + offset_of(there, link)
                    order = ARRIVALS[there][half]
                    wanted = link * 100 + far
                    row.append(order.index(wanted) + 1 if 1 <= far <= REACH and wanted in order else 0)
                rows.append(row)
            halves.append(rows)
        table.append(halves)
    return table


TABLE = forward_table()


def kernel(q_hbm, k_hbm, v_hbm, seg_hbm, own_hbm, out_ref, cache_ref,
           q_own, q_turned, k_own, v_own, own_values, seg_ref, own_ref, kv, bias, top, acc, scores_a, scores_b, weights_a, weights_b,
           peaks_a, peaks_b, shrink_a, shrink_b,
           outgoing, mid, recv, block,
           in_sem, kv_send, kv_recv, z_send, z_recv, x_send, x_recv, y_send, y_recv, c_send, c_recv, own_sem):
    me, g = lax.axis_index("inst"), lax.axis_index("head")
    kind = me % 16
    x, y, z = me // 16, (me // 8) % 2, me % 8
    other_y = x * 16 + (1 - y) * 8 + z
    other_chip, other_core = (g + 2) % 4, g + 1 - 2 * (g % 2)
    near = (
        ((x + 1) % 4) * 16 + kind,
        me - z + (z + 1) % 8,
        me - z + (z + 7) % 8,
        other_y,
    )

    inputs = [
        pltpu.make_async_copy(src, dst, in_sem.at[n])
        for n, (src, dst) in enumerate(
            ((k_hbm, k_own), (v_hbm, v_own), (seg_hbm, seg_ref), (own_hbm, own_ref), (q_hbm, q_own)))
    ]
    for copy in inputs:
        copy.start()

    def along_z(by):
        return (me - z + (z + by) % 8, g)

    def along_x(by):
        return (((x + by) % 4) * 16 + kind, g)

    beside = ((me, other_chip), (other_y, g), (other_y, other_chip))
    sibling = (me, other_core)
    barrier = pltpu.get_barrier_semaphore()
    partners = [along_z(by) for by in range(1, 8)] + [along_x(by) for by in range(1, 4)] + list(beside) + [sibling]
    for partner in partners:
        pl.semaphore_signal(barrier, inc=1, device_id=partner, device_id_type=MESH)

    def pick(values):
        chosen = jnp.int32(values[0])
        if len(set(values)) == 1:
            return chosen
        for t in range(1, 16):
            chosen = jnp.where(kind == t, jnp.int32(values[t]), chosen)
        return chosen

    first = [[pick([TABLE[t][half][0][link] for t in range(16)]) for link in range(4)] for half in range(2)]
    def digits(half, jj, k):
        return [(codes[half][jj][link] >> (6 * k)) & 63 for link in range(4)]

    def forward(half, slot, theres, wait=False):
        for link in range(4):
            there = theres[link]

            @pl.when(there > 0)
            def _():
                copy = pltpu.make_async_remote_copy(
                    src_ref=kv.at[half, slot],
                    dst_ref=kv.at[half, there],
                    send_sem=kv_send.at[half * 4 + link, slot],
                    recv_sem=kv_recv.at[half, there],
                    device_id=(near[link], g),
                    device_id_type=MESH,
                )
                if wait:
                    copy.wait_send()
                else:
                    copy.start()

    def arrive(k, h, j):
        half, jj = j % 2, 2 * h + j // 2
        slot = STEP * k + jj + 1
        here = kv.at[half, slot]
        pltpu.make_async_copy(here, here, kv_recv.at[half, slot]).wait()
        forward(half, slot, digits(half, jj, k))

    def drain(k, half, jj):
        forward(half, STEP * k + jj + 1, digits(half, jj, k), wait=True)

    for copy in inputs[:3]:
        copy.wait()
    at0 = lax.broadcasted_iota(jnp.int32, (TOK, TOK), 0)
    at1 = lax.broadcasted_iota(jnp.int32, (TOK, TOK), 1)
    seg_row = seg_ref[...].astype(F32)
    seg_wide = jnp.broadcast_to(seg_row, (TOK, TOK))
    seg_tall = jnp.broadcast_to(jnp.sum(jnp.where(at0 == at1, seg_wide, 0.0), axis=1, keepdims=True), (TOK, TOK))
    first_seg, last_seg = jnp.min(seg_tall, axis=0, keepdims=True), jnp.max(seg_tall, axis=0, keepdims=True)
    reaches = (seg_row == last_seg).astype(F32)
    extra = lax.broadcasted_iota(jnp.int32, (16, TOK), 0)
    extra_rows = jnp.where(extra == 0, reaches, jnp.where(extra == 1, last_seg, 0.0)).astype(BF16)
    for half in range(2):
        feat = slice(half * SIZE, (half + 1) * SIZE)
        turned = v_own[:, feat].astype(F32).T
        kv[half, 0, 0:SIZE, :] = (turned * reaches).astype(BF16)
        kv[half, 0, SIZE:KEY_ROW, :] = extra_rows
        keys = k_own[:, feat].astype(F32)
        last_key = jnp.broadcast_to(keys[TOK - 1:TOK, :], (TOK, SIZE))
        keys = jnp.where(seg_tall[:, 0:SIZE] == last_seg[:, 0:SIZE], keys, last_key).astype(BF16)
        kv[half, 0, KEY_ROW:ALL_ROWS, 0:SIZE] = keys[0:SIZE]
        kv[half, 0, KEY_ROW:ALL_ROWS, SIZE:TOK] = keys[SIZE:TOK]
        if half == 0:
            pl.semaphore_wait(barrier, len(partners))
        forward(half, 0, first[half])

    codes = [
        [
            [pick([sum(TABLE[t][half][STEP * k + jj + 1][link] * 64 ** k for k in range(5)) for t in range(16)]) for link in range(4)]
            for jj in range(STEP)
        ]
        for half in range(2)
    ]

    for half in range(2):
        own_values[half, 0:SIZE, :] = v_own[:, half * SIZE:(half + 1) * SIZE].astype(F32).T.astype(BF16)
        own_values[half, SIZE:KEY_ROW, :] = jnp.where(extra == 0, 1.0, 0.0).astype(BF16)
    inputs[4].wait()
    for h in range(HEADS):
        turned = q_own[:, h * SIZE:(h + 1) * SIZE].astype(F32).T.astype(BF16)
        q_turned[h // GROUP, :, (h % GROUP) * TOK:(h % GROUP + 1) * TOK] = turned
    bias[...] = jnp.where((at0 <= at1) & (seg_tall == seg_wide), 0.0, -HIDDEN)

    inputs[3].wait()
    dest = own_ref[...]
    owner = lax.broadcasted_iota(jnp.int32, (64, TOK), 0)
    hot = (owner == dest).astype(F32)
    before = (lax.broadcasted_iota(jnp.int32, (TOK, TOK), 0) < lax.broadcasted_iota(jnp.int32, (TOK, TOK), 1)).astype(BF16)
    count = jnp.dot(hot.astype(BF16), before, preferred_element_type=F32)
    place = jnp.sum(hot * count, axis=0, keepdims=True).astype(jnp.int32)
    target = dest * (2 * SLOT) + place
    row = lax.broadcasted_iota(jnp.int32, (1024, TOK), 0)
    of_keys = (row == target).astype(BF16)
    of_values = (row == target + SLOT).astype(BF16)
    rows = jnp.dot(of_keys, k_own[...], preferred_element_type=F32)
    rows += jnp.dot(of_values, v_own[...], preferred_element_type=F32)
    outgoing[...] = rows.astype(BF16).reshape(4, 2, 8, 2 * SLOT, 2 * SIZE)

    def z_copy(by):
        return pltpu.make_async_remote_copy(
            src_ref=outgoing.at[:, :, (z + by) % 8], dst_ref=mid.at[z], send_sem=z_send.at[by], recv_sem=z_recv.at[z],
            device_id=along_z(by), device_id_type=MESH)

    def x_copy(by):
        return pltpu.make_async_remote_copy(
            src_ref=mid.at[:, (x + by) % 4], dst_ref=recv.at[x], send_sem=x_send.at[by], recv_sem=x_recv.at[x],
            device_id=along_x(by), device_id_type=MESH)

    def rows_of(source_y, group):
        return cache_ref.at[:, source_y, :, pl.ds(pl.multiple_of(group * 512, 512), 512)]

    def y_copy(n):
        return pltpu.make_async_remote_copy(
            src_ref=block.at[y if n == 0 else 1 - y], dst_ref=rows_of(y, g), send_sem=y_send.at[n], recv_sem=y_recv.at[n],
            device_id=beside[n], device_id_type=MESH)

    from_y = ((y, other_chip), (1 - y, g), (1 - y, other_chip))

    def c_copy(n):
        if n == 3:
            src, place = block.at[y], rows_of(y, g)
        else:
            src = place = rows_of(*from_y[n])
        return pltpu.make_async_remote_copy(
            src_ref=src, dst_ref=place, send_sem=c_send.at[n], recv_sem=c_recv.at[n],
            device_id=sibling, device_id_type=MESH)

    def own_copy():
        return pltpu.make_async_copy(block.at[y], rows_of(y, g), own_sem)

    def keep_first():
        for i in range(4):
            for j in range(2):
                mid[z, i, j] = outgoing[i, j, z]

    def second_leg():
        for by in range(1, 8):
            src = (z + 8 - by) % 8
            pltpu.make_async_copy(mid.at[src], mid.at[src], z_recv.at[src]).wait()
        for i in range(8):
            recv[x, i] = mid[i, x]

    def third_leg():
        for by in range(1, 4):
            src = (x + 4 - by) % 4
            pltpu.make_async_copy(recv.at[src], recv.at[src], x_recv.at[src]).wait()
        a = lax.broadcasted_iota(jnp.int32, (64, 128), 0)
        b = lax.broadcasted_iota(jnp.int32, (64, 128), 1)
        key_rows = (b == 2 * a - (a & 7)).astype(BF16)
        value_rows = (b == 2 * a - (a & 7) + 8).astype(BF16)
        for src in range(4):
            for j in range(2):
                arrived = recv[src, :, j].reshape(128, 2 * SIZE)
                block[j, src, :, 0:256] = jnp.dot(key_rows, arrived, preferred_element_type=F32).astype(BF16)
                block[j, src, :, 256:512] = jnp.dot(value_rows, arrived, preferred_element_type=F32).astype(BF16)
        c_copy(3).start()
        own_copy().start()

    legs = [(after, z_copy(by).start) for by, after in Z_AFTER.items()]
    legs += [(min(X_AFTER.values()), second_leg)] + [(after, x_copy(by).start) for by, after in X_AFTER.items()]
    legs += [(min(Y_AFTER.values()), third_leg)] + [(after, y_copy(n).start) for n, after in Y_AFTER.items()]

    def legs_at(count):
        return [start for after, start in legs if after == count]

    def fourth_leg():
        for n in range(3):
            here = rows_of(*from_y[n])
            pltpu.make_async_copy(here, here, y_recv.at[n]).wait()
            c_copy(n).start()

    scores_of, weights_of = (scores_a, scores_b), (weights_a, weights_b)
    peaks_of, shrink_of = (peaks_a, peaks_b), (shrink_a, shrink_b)
    first_wide = jnp.concatenate([(seg_row == first_seg).astype(F32)] * GROUP, axis=1)

    def half_of(group):
        return group // (RATIO // GROUP)

    def score(n, group, slots, c):
        half = half_of(group)
        if slots is None:
            keys = k_own[:, half * SIZE:(half + 1) * SIZE]
        else:
            keys = jnp.concatenate([kv[half, slots[c], KEY_ROW:ALL_ROWS, lanes:lanes + SIZE] for lanes in (0, SIZE)], axis=0)
        product = jnp.dot(keys, q_turned[group], preferred_element_type=F32)
        if slots is None:
            product += jnp.concatenate([bias[...]] * GROUP, axis=1)
        scores_of[n % 2][c * TOK:(c + 1) * TOK, :] = product
        peaks_of[n % 2][c] = jnp.max(product, axis=0, keepdims=True)

    def peak_rows(n, group, slots):
        if slots is None:
            top[group] = peaks_of[n % 2][0]
            return [top[group]]
        seen = []
        for slot in slots:
            block_seg = kv[half_of(group), slot, SIZE:KEY_ROW, :].astype(F32)[1:2, :]
            same = jnp.concatenate([(block_seg == first_seg).astype(F32)] * GROUP, axis=1)
            seen.append(same * first_wide > 0.5)
        old = top[group]
        peak = old
        for c in range(len(slots)):
            peak = jnp.maximum(peak, jnp.where(seen[c], peaks_of[n % 2][c], -HIDDEN))
        top[group] = peak
        shrink_of[n % 2][...] = jnp.exp2((old - peak) * TO_LOG2)
        return [jnp.where(seen[c], peak, HIDDEN) for c in range(len(slots))]

    def soften(n, peak, c):
        for at in range(c * TOK, (c + 1) * TOK, 16):
            rows = slice(at, at + 16)
            weights_of[n % 2][rows, :] = jnp.exp2((scores_of[n % 2][rows, :] - peak) * TO_LOG2).astype(BF16)

    def combine(n, group, slots, c):
        values = own_values[half_of(group)] if slots is None else kv[half_of(group), slots[c], 0:KEY_ROW, :]
        product = jnp.dot(values, weights_of[n % 2][c * TOK:(c + 1) * TOK, :], preferred_element_type=F32)
        if slots is None:
            acc[group] = product
        elif c == 0:
            acc[group] = acc[group] * shrink_of[n % 2][...] + product
        else:
            acc[group] += product

    def turn(n, before, now, after):
        peaks = peak_rows(n, *now)
        for c in range(len(peaks)):
            if before is not None:
                combine(n - 1, *before, c)
            if after is not None:
                score(n + 1, *after, c)
            soften(n, peaks[c], c)

    groups = HEADS // GROUP
    turns = [(group, None) for group in range(groups)]
    for start in legs_at(0):
        start()
    keep_first()
    score(0, *turns[0], 0)
    for n in range(groups):
        turn(n, turns[n - 1] if n > 0 else None, turns[n], turns[n + 1] if n + 1 < groups else None)
        arrive(0, n // 4, n % 4)
        for start in legs_at(n + 1):
            start()
    combine(groups - 1, *turns[-1], 0)

    def slots_of(k):
        return [STEP * k + 1 + c for c in range(STEP)]

    for c in range(STEP):
        score(0, 0, slots_of(0), c)

    def step(k, carry):
        turns = [(group, slots_of(k)) for group in range(groups)] + [(0, slots_of(jnp.minimum(k + 1, 4)))]
        for n in range(groups):
            turn(n, turns[n - 1] if n > 0 else None, turns[n], turns[n + 1])
            if n == groups - 1:
                for c in range(STEP):
                    combine(n, *turns[n], c)

            @pl.when(k < 4)
            def _():
                arrive(k + 1, n // 4, n % 4)

            @pl.when((k > 0) & (k < 4))
            def _():
                drain(k - 1, n % 2, n // 2)

            @pl.when(k == 3)
            def _():
                drain(3, n % 2, n // 2)
                if n == groups - 2:
                    for half in range(2):
                        forward(half, 0, first[half], wait=True)
                    for by in range(1, 8):
                        z_copy(by).wait_send()

            for at in range(4):
                starts = legs_at(8 * (at + 1) + n + 1)
                if starts:
                    @pl.when(k == at)
                    def _():
                        for start in starts:
                            start()
        return carry

    lax.fori_loop(0, 5, step, 0)
    fourth_leg()

    for h in range(HEADS):
        group, lanes = h // GROUP, slice((h % GROUP) * TOK, (h % GROUP + 1) * TOK)
        attended = acc[group, 0:SIZE, lanes] * (1.0 / acc[group, SIZE:SIZE + 1, lanes])
        out_ref[:, h * SIZE:(h + 1) * SIZE] = attended.T.astype(BF16)

    for half in range(2):
        for jj in range(STEP):
            drain(4, half, jj)
    for by in range(1, 4):
        x_copy(by).wait_send()
    for n in range(3):
        y_copy(n).wait_send()
    own_copy().wait()
    across = (other_core + 2) % 4
    from_core = ((y, across), (1 - y, other_core), (1 - y, across), (y, other_core))
    for n in range(4):
        c_copy(n).wait_send()
        here = rows_of(*from_core[n])
        pltpu.make_async_copy(here, here, c_recv.at[n]).wait()


def on_device(queries, keys, values, segments, owners):
    whole = pl.BlockSpec(memory_space=pl.ANY)
    operands = (queries, keys, values, segments.reshape(1, TOK), owners.reshape(1, TOK))
    attended, cache = pl.pallas_call(
        kernel,
        out_shape=(
            jax.ShapeDtypeStruct((TOK, HEADS * SIZE), BF16),
            jax.ShapeDtypeStruct((4, 2, 64, 2048), BF16),
        ),
        in_specs=[whole] * 5,
        out_specs=(pl.BlockSpec(memory_space=pltpu.VMEM), whole),
        scratch_shapes=[
            pltpu.VMEM((TOK, HEADS * SIZE), BF16),
            pltpu.VMEM((HEADS // GROUP, SIZE, WIDE), BF16),
            pltpu.VMEM((TOK, 2 * SIZE), BF16),
            pltpu.VMEM((TOK, 2 * SIZE), BF16),
            pltpu.VMEM((2, KEY_ROW, TOK), BF16),
            pltpu.VMEM((1, TOK), jnp.int32),
            pltpu.VMEM((1, TOK), jnp.int32),
            pltpu.VMEM((2, REACH + 1, ALL_ROWS, TOK), BF16),
            pltpu.VMEM((TOK, TOK), F32),
            pltpu.VMEM((HEADS // GROUP, 1, WIDE), F32),
            pltpu.VMEM((HEADS // GROUP, KEY_ROW, WIDE), F32),
            pltpu.VMEM((STEP * TOK, WIDE), F32),
            pltpu.VMEM((STEP * TOK, WIDE), F32),
            pltpu.VMEM((STEP * TOK, WIDE), BF16),
            pltpu.VMEM((STEP * TOK, WIDE), BF16),
            pltpu.VMEM((STEP, 1, WIDE), F32),
            pltpu.VMEM((STEP, 1, WIDE), F32),
            pltpu.VMEM((1, WIDE), F32),
            pltpu.VMEM((1, WIDE), F32),
            pltpu.VMEM((4, 2, 8, 2 * SLOT, 2 * SIZE), BF16),
            pltpu.VMEM((8, 4, 2, 2 * SLOT, 2 * SIZE), BF16),
            pltpu.VMEM((4, 8, 2, 2 * SLOT, 2 * SIZE), BF16),
            pltpu.VMEM((2, 4, 64, 4 * SIZE), BF16),
            pltpu.SemaphoreType.DMA((5,)),
            pltpu.SemaphoreType.DMA((8, REACH + 1)),
            pltpu.SemaphoreType.DMA((2, REACH + 1)),
            pltpu.SemaphoreType.DMA((8,)),
            pltpu.SemaphoreType.DMA((8,)),
            pltpu.SemaphoreType.DMA((4,)),
            pltpu.SemaphoreType.DMA((4,)),
            pltpu.SemaphoreType.DMA((3,)),
            pltpu.SemaphoreType.DMA((3,)),
            pltpu.SemaphoreType.DMA((4,)),
            pltpu.SemaphoreType.DMA((4,)),
            pltpu.SemaphoreType.DMA(()),
        ],
        compiler_params=pltpu.CompilerParams(
            collective_id=0, has_side_effects=True, vmem_limit_bytes=40 * 1024 * 1024
        ),
        cost_estimate=pl.CostEstimate(flops=12_000_000_000, bytes_accessed=6_000_000, transcendentals=22_000_000),
        name="attend_and_send",
    )(*(pltpu.with_memory_space_constraint(a, pltpu.HBM) for a in operands))
    return attended, cache.reshape(64 * SLOT, 2048)


def solution(mesh):
    return jax.shard_map(
        on_device,
        mesh=mesh,
        in_specs=(
            P("inst", "head"),
            P("inst", "head"),
            P("inst", "head"),
            P("inst"),
            P("inst", None),
        ),
        out_specs=(P("inst", "head"), P("inst", None)),
        check_vma=False,
    )
```
